32 devices in a mesh: wide: 8 (over z, x), narrow: 4 (over y, core).
Axes of the slice: x: 2, y: 2, z: 4, core: 2. Of those that a mesh axis runs over, the one named last changes fastest.
Arguments:
- coefficients: bfloat16 [512, 2, 512], P(('wide', 'narrow')), may hold values from -6 to 6
- radiation: bfloat16 [2, 512, 882], replicated, may hold values from -0.1875 to 0.1875
- interpolation: bfloat16 [882, 3328], replicated, may hold values from -0.21875 to 0.21875
- angles: float32 [8, 3328], replicated, may hold values from -3.140625 to 3.140625
- translations: float32 [316, 2, 3328], P(None, None, 'wide'), may hold values from -0.031746034 to 0.031746034
- sources: int32 [64, 189], P(('wide', 'narrow')), may hold values from 0 to 63
- operators: int32 [64, 189], P(('wide', 'narrow')), may hold values from 0 to 315
- counts: int32 [64], P(('wide', 'narrow')), may hold values from 63 to 189, as said below
Outputs:
- product: float32 [512, 2, 512], P(('wide', 'narrow'))
The draws below stay inside these ranges and needn't reach their ends.
Inputs may be any that keep to these rules, and one draw needn't show every extreme that they name: `counts`: entries of a list past its count are not used; some parent has exactly 189 entries and some exactly 63. `sources`: index values; a program may hold and send them packed several to one 32-bit word, as an allowed encoding. `operators`: index values; a program may hold and send them packed several to one 32-bit word, as an allowed encoding.
All inputs are finite; a program needn't handle non-finite values.
Results may differ from the reference program's by a relative error of at most 0.005.
Values sent between devices are 32-bit elements; how exact they have to be, the bound alone decides.
No kernel may reach another device: no remote copies, remote signals or barrier semaphores. Data moves between devices by JAX's collectives and lax.ppermute only.
A program may use at most 128 MiB of HBM per device.

```python
import jax
import jax.numpy as jnp
from jax import lax

NB = 512
Q0 = 882
Q1 = 3328
CH = 8
LIST = 189
OPS = 316
LEAVES = 512
PARENTS = 64


def draw_counts(key, part):
    values = jax.random.randint(key, (PARENTS,), LIST // 3, LIST + 1)
    values = values.at[0].set(LIST)
    values = values.at[1].set(LIST // 3)
    return values.astype(jnp.int32)


def set_ends(array, key, least, largest):
    spot = [jax.random.randint(jax.random.fold_in(key, axis), (), 0, length) for axis, length in enumerate(array.shape)]
    widest = array.shape.index(max(array.shape))
    beside = spot[:widest] + [(spot[widest] + 1) % array.shape[widest]] + spot[widest + 1:]
    return array.at[tuple(spot)].set(least).at[tuple(beside)].set(largest)


def block_levels(key, shape, pieces, low, high):
    def one(axis_at, shards_of):
        steps = jax.random.uniform(jax.random.fold_in(jax.random.fold_in(key, 6), axis_at), (shards_of,), jnp.float32, low / len(pieces), high / len(pieces))
        return jnp.repeat(jnp.exp(steps), shape[axis_at] // shards_of).reshape((-1,) + (1,) * (len(shape) - axis_at - 1))

    factor_of = one(*pieces[0])
    for cut in pieces[1:]:
        factor_of = factor_of * one(*cut)
    return factor_of


def noise(rng, shape, scale, most, cuts=(), kind=jnp.bfloat16):
    result = scale * jax.random.normal(rng, shape, jnp.float32)
    if cuts:
        result = result * block_levels(rng, shape, cuts, -0.22, 0.18)
    return jnp.clip(result, -most, most).astype(kind)


def setup_inputs(seed: int = 0) -> dict:
    key_list = jax.random.split(jax.random.key(seed), 9)
    coefficients = noise(key_list[0], (LEAVES, 2, NB), 1.0, 6.0, ((0, 32),))
    radiation = noise(key_list[1], (2, NB, Q0), (2 * NB) ** -0.5, 0.1875)
    interpolation = noise(key_list[2], (Q0, Q1), Q0 ** -0.5, 0.21875)
    angles = jnp.clip(jax.random.uniform(key_list[3], (CH, Q1), jnp.float32, -3.140625, 3.140625), -3.140625, 3.140625)
    translations = noise(key_list[4], (OPS, 2, Q1), (1.0 / LIST), 0.031746034, ((2, 8),), jnp.float32)
    sources = set_ends(jax.random.randint(key_list[5], (PARENTS, LIST), 0, PARENTS), jax.random.fold_in(key_list[5], 1), 0, PARENTS - 1).astype(jnp.int32)
    operators = set_ends(jax.random.randint(key_list[6], (PARENTS, LIST), 0, OPS), jax.random.fold_in(key_list[6], 1), 0, OPS - 1).astype(jnp.int32)
    counts = draw_counts(jax.random.fold_in(key_list[8], 71), 0)
    return dict(coefficients=coefficients, radiation=radiation, interpolation=interpolation, angles=angles, translations=translations, sources=sources, operators=operators, counts=counts)


def product_of(left, right):
    return jnp.dot(left, right, preferred_element_type=jnp.float32)


def reference(coefficients, radiation, interpolation, angles, translations, sources, operators, counts):
    coef_real = coefficients[:, 0]
    coef_imag = coefficients[:, 1]
    rad_real = radiation[0]
    rad_imag = radiation[1]
    leaf_real = product_of(coef_real, rad_real) - product_of(coef_imag, rad_imag)
    leaf_imag = product_of(coef_real, rad_imag) + product_of(coef_imag, rad_real)
    leaf = jnp.stack([leaf_real, leaf_imag], 1).astype(jnp.bfloat16)
    upward = product_of(leaf.reshape(LEAVES * 2, Q0), interpolation).reshape(PARENTS, CH, 2, Q1)
    cosines = jnp.cos(angles)[None]
    sines = jnp.sin(angles)[None]
    out_real = jnp.sum(cosines * upward[:, :, 0] - sines * upward[:, :, 1], 1)
    out_imag = jnp.sum(cosines * upward[:, :, 1] + sines * upward[:, :, 0], 1)
    outgoing = jnp.stack([out_real, out_imag], 1)

    def entry_step(carry, column):
        total_real, total_imag = carry
        weight = (column < counts).astype(jnp.float32)[:, None]
        picked = outgoing[sources[:, column]]
        operator_rows = translations[operators[:, column]]
        total_real = total_real + weight * (operator_rows[:, 0] * picked[:, 0] - operator_rows[:, 1] * picked[:, 1])
        total_imag = total_imag + weight * (operator_rows[:, 0] * picked[:, 1] + operator_rows[:, 1] * picked[:, 0])
        return (total_real, total_imag), None

    zeros = jnp.zeros((PARENTS, Q1), jnp.float32)
    (in_real, in_imag), unused = lax.scan(entry_step, (zeros, zeros), jnp.arange(LIST, dtype=jnp.int32))
    down_real = cosines * in_real[:, None] + sines * in_imag[:, None]
    down_imag = cosines * in_imag[:, None] - sines * in_real[:, None]
    downward = jnp.stack([down_real, down_imag], 2).astype(jnp.bfloat16)
    received = lax.dot_general(downward.reshape(LEAVES * 2, Q1), interpolation, (((1,), (1,)), ((), ())), preferred_element_type=jnp.float32)
    received = received.astype(jnp.bfloat16).reshape(LEAVES, 2, Q0)
    dims = (((1,), (1,)), ((), ()))
    recv_real = received[:, 0]
    recv_imag = received[:, 1]
    res_real = lax.dot_general(recv_real, rad_real, dims, preferred_element_type=jnp.float32) + lax.dot_general(recv_imag, rad_imag, dims, preferred_element_type=jnp.float32)
    res_imag = lax.dot_general(recv_imag, rad_real, dims, preferred_element_type=jnp.float32) - lax.dot_general(recv_real, rad_imag, dims, preferred_element_type=jnp.float32)
    return jnp.stack([res_real, res_imag], 1)
```

```python
import jax
import jax.numpy as jnp
from jax import lax
from jax.experimental import pallas as pl
from jax.experimental.pallas import tpu as pltpu
from jax.sharding import PartitionSpec as P

F32 = jnp.float32
BF16 = jnp.bfloat16
MIB = 2**20
NT = (((1,), (1,)), ((), ()))


class Plan:
    def __init__(self, parents, dirs, length, ops):
        self.parents = parents
        self.dirs = dirs
        self.length = length
        self.ops = ops
        self.tiles = -(-dirs // 128)
        self.width = 128 * self.tiles
        spare = self.width - dirs
        used = dirs - 128 * (self.tiles - 1)
        self.bits = (ops - 1).bit_length()
        if 2 * spare >= length:
            self.extra = 0
            self.pieces = [
                (self.tiles - 1, used, spare, 0),
                (2 * self.tiles - 1, used, length - spare, spare),
            ]
        else:
            self.extra = -(-length // 128)
            self.pieces = [
                (2 * self.tiles + e, 0, min(128, length - 128 * e), 128 * e)
                for e in range(self.extra)
            ]
        self.rows = 2 * self.tiles + self.extra
        self.code_width = -(-length // 128) * 128


def sin_cos(angle):
    turns = jnp.floor(angle * 0.6366197723675814 + 0.5)
    quarter = turns.astype(jnp.int32)
    rest = angle - turns * 1.5703125
    rest = rest - turns * 4.837512969970703e-4
    rest = rest - turns * 7.54978995489188e-8
    square = rest * rest
    sine = ((-1.9515295891e-4 * square + 8.3321608736e-3) * square - 1.6666654611e-1) * square * rest + rest
    cosine = ((2.443315711809948e-5 * square - 1.388731625493765e-3) * square + 4.166664568298827e-2) * (
        square * square
    ) - 0.5 * square + 1.0
    swap = (quarter & 1) == 1
    sin_value = jnp.where(swap, cosine, sine)
    cos_value = jnp.where(swap, sine, cosine)
    sin_value = jnp.where((quarter & 2) == 2, -sin_value, sin_value)
    cos_value = jnp.where(((quarter + 1) & 2) == 2, -cos_value, cos_value)
    return sin_value, cos_value


def arrange(boxes, swapped):
    row = lax.broadcasted_iota(jnp.int32, (128, 2 * boxes), 0)
    column = lax.broadcasted_iota(jnp.int32, (128, 2 * boxes), 1)
    real_at = 2 * row
    imag_at = 2 * (row - boxes) + 1
    if swapped:
        first = jnp.where((row < boxes) & (column == real_at + 1), -1.0, 0.0)
        second = jnp.where((row >= boxes) & (row < 2 * boxes) & (column == imag_at - 1), 1.0, 0.0)
    else:
        first = jnp.where((row < boxes) & (column == real_at), 1.0, 0.0)
        second = jnp.where((row >= boxes) & (row < 2 * boxes) & (column == imag_at), 1.0, 0.0)
    return (first + second).astype(BF16)


def upward_kernel(plan, n_wide, n_narrow, chunk):
    def kernel(
        counts, coef, rad_hbm, interp_hbm, angles, sources, operators,
        send, cos_out, sin_out,
        rad, interp, even, odd, codes, real_buf, imag_buf, sems,
    ):
        parent_dirs = angles.shape[1]
        leaf_dirs = rad.shape[0]
        boxes = coef.shape[0]
        parents_dev = boxes // 8
        n_chunks = parent_dirs // chunk
        rad_copy = pltpu.make_async_copy(rad_hbm, rad, sems.at[n_chunks])
        rad_copy.start()
        copies = []
        for c in range(n_chunks):
            cut = (slice(None), pl.ds(c * chunk, chunk))
            copies.append(pltpu.make_async_copy(interp_hbm.at[cut], interp.at[cut], sems.at[c]))
            copies[-1].start()

        sines, cosines = sin_cos(angles[...])
        sin_out[...] = sines
        cos_out[...] = cosines

        code = sources[...] * (1 << plan.bits) + operators[...]
        at = lax.broadcasted_iota(jnp.int32, code.shape, 1)
        parent = lax.broadcasted_iota(jnp.int32, code.shape, 0)
        limit = jnp.zeros(code.shape, jnp.int32)
        for p in range(parents_dev):
            limit = jnp.where(parent == p, counts[p], limit)
        codes[...] = jnp.full(codes.shape, -1.0, F32)
        codes[:, 0 : plan.length] = jnp.where(at < limit, code, -1).astype(F32)

        rows = coef[...].reshape(2 * boxes, coef.shape[2])
        plain = jnp.dot(arrange(boxes, False), rows, preferred_element_type=F32).astype(BF16)
        turned = jnp.dot(arrange(boxes, True), rows, preferred_element_type=F32).astype(BF16)
        weights = jnp.concatenate([plain, turned], 0)

        rad_copy.wait()
        matrix = rad[...].reshape(2 * leaf_dirs, rad.shape[2])
        both = lax.dot_general(matrix, weights, NT, preferred_element_type=F32)
        even[...] = both[:, 0:128]
        odd[...] = both[:, 128:256]
        leaf_t = even[pl.ds(0, leaf_dirs, stride=2), :] + odd[pl.ds(1, leaf_dirs, stride=2), :]
        leaf = jnp.transpose(leaf_t)[0 : 2 * boxes].astype(BF16)

        for c in range(n_chunks):
            copies[c].wait()
            cut = slice(c * chunk, (c + 1) * chunk)
            up = jnp.dot(leaf, interp[:, cut], preferred_element_type=F32)
            cs = cos_out[:, cut]
            sn = sin_out[:, cut]
            for p in range(parents_dev):
                up_real = up[8 * p : 8 * p + 8]
                up_imag = up[boxes + 8 * p : boxes + 8 * p + 8]
                real_buf[p : p + 1, cut] = jnp.sum(cs * up_real - sn * up_imag, 0, keepdims=True)
                imag_buf[p : p + 1, cut] = jnp.sum(cs * up_imag + sn * up_real, 0, keepdims=True)

        lane = lax.broadcasted_iota(jnp.int32, (parents_dev, 128), 1)
        tails = {}
        for tile, start, count, first in plan.pieces:
            turn = (start - first) % plan.code_width
            moved = codes[...] if turn == 0 else pltpu.roll(codes[...], turn, 1)
            tails[tile] = (moved[:, 0:128], (lane >= start) & (lane < start + count))
        for w in range(n_wide):
            base = plan.dirs * w // 128 * 128
            shift = plan.dirs * w % 128
            span = -(-(shift + plan.dirs) // 128) * 128
            span = min(max(span, plan.width), parent_dirs - base)
            for part, buf in ((0, real_buf), (1, imag_buf)):
                value = buf[:, base : base + span]
                if shift:
                    value = pltpu.roll(value, span - shift, 1)
                for k in range(plan.tiles):
                    tile = part * plan.tiles + k
                    piece = value[:, 128 * k : 128 * k + 128]
                    if k == plan.tiles - 1:
                        piece = jnp.where(lane < plan.dirs - 128 * k, piece, -1.0)
                    if tile in tails:
                        piece = jnp.where(tails[tile][1], tails[tile][0], piece)
                    for n in range(n_narrow):
                        first = (w * n_narrow + n) * parents_dev * plan.rows + tile
                        send[pl.ds(first, parents_dev, stride=plan.rows), :] = piece
            for e in range(plan.extra):
                tile = 2 * plan.tiles + e
                piece = jnp.where(tails[tile][1], tails[tile][0], -1.0)
                for n in range(n_narrow):
                    first = (w * n_narrow + n) * parents_dev * plan.rows + tile
                    send[pl.ds(first, parents_dev, stride=plan.rows), :] = piece

    return kernel


def translate_kernel(plan, n_wide, n_narrow, parents_dev):
    targets = n_wide * parents_dev
    group = max(1, min(targets, 1024 // plan.parents))
    step = min(256, plan.width)

    def kernel(table_in, received, out, table, tally, a_real, a_imag):
        mine = lax.axis_index("narrow")
        table[...] = jnp.zeros(table.shape, BF16)
        table[:, 0 : plan.dirs, 0 : plan.ops] = table_in[...].astype(BF16)
        lane = lax.broadcasted_iota(jnp.int32, (1, 128), 1)
        source_at = lax.broadcasted_iota(jnp.int32, (plan.parents, 128), 0)
        op_at = lax.broadcasted_iota(jnp.int32, (table.shape[2], 128), 0)

        def do_group(first_target):
            for i in range(group):
                target = first_target + i
                w = target // parents_dev
                p = target % parents_dev
                row = ((w * n_narrow + mine) * parents_dev + p) * plan.rows
                hits, picks = [], []
                for tile, start, count, _ in plan.pieces:
                    code = received[pl.ds(row + tile, 1), :]
                    code = jnp.where((lane >= start) & (lane < start + count), code, -1.0).astype(jnp.int32)
                    hits.append(jnp.where(source_at == (code >> plan.bits), 1.0, 0.0).astype(BF16))
                    picks.append(jnp.where(op_at == (code & ((1 << plan.bits) - 1)), 1.0, 0.0).astype(BF16))
                count_of = lax.dot_general(
                    jnp.concatenate(hits, 1), jnp.concatenate(picks, 1), NT, preferred_element_type=F32
                )
                tally[i * plan.parents : (i + 1) * plan.parents, :] = count_of.astype(BF16)
            for j in range(plan.width // step):
                cut = slice(j * step, (j + 1) * step)
                a_real[...] = lax.dot_general(tally[...], table[0, cut, :], NT, preferred_element_type=F32)
                a_imag[...] = lax.dot_general(tally[...], table[1, cut, :], NT, preferred_element_type=F32)
                for q in range(step // 128):
                    k = j * (step // 128) + q
                    lanes = slice(128 * q, 128 * q + 128)
                    out_real = received[pl.ds(k, plan.parents, stride=plan.rows), :]
                    out_imag = received[pl.ds(plan.tiles + k, plan.parents, stride=plan.rows), :]
                    for i in range(group):
                        own = slice(i * plan.parents, (i + 1) * plan.parents)
                        op_real = a_real[own, lanes]
                        op_imag = a_imag[own, lanes]
                        real = jnp.sum(op_real * out_real - op_imag * out_imag, 0, keepdims=True)
                        imag = jnp.sum(op_real * out_imag + op_imag * out_real, 0, keepdims=True)
                        at = (first_target + i) * 2 * plan.tiles + k
                        out[pl.ds(at, 1), :] = real
                        out[pl.ds(at + plan.tiles, 1), :] = imag

        if targets == group:
            do_group(0)
        else:
            pl.loop(0, targets // group)(lambda g: do_group(g * group))

    return kernel, group, step


def downward_kernel(plan, n_wide):
    def kernel(received, cosines, sines, interp, rad, product, inner, twin):
        parent_dirs = cosines.shape[1]
        leaf_dirs = rad.shape[0]
        parents_dev = product.shape[0] // 8
        boxes = product.shape[0]
        parts = 2 * parents_dev
        lane = lax.broadcasted_iota(jnp.int32, (parts, plan.width), 1)
        inner[...] = jnp.zeros(inner.shape, F32)
        for w in range(n_wide):
            base = plan.dirs * w // 128 * 128
            shift = plan.dirs * w % 128
            span = -(-(shift + plan.dirs) // 128) * 128
            tiles = [
                received[pl.ds(w * parts * plan.tiles + k, parts, stride=plan.tiles), :]
                for k in range(plan.tiles)
            ]
            value = tiles[0] if plan.tiles == 1 else jnp.concatenate(tiles, 1)
            value = jnp.where(lane < plan.dirs, value, 0.0)
            if span > plan.width:
                value = jnp.concatenate([value, jnp.zeros((parts, span - plan.width), F32)], 1)
            if shift:
                value = pltpu.roll(value, shift, 1)
            span = min(value.shape[1], inner.shape[1] - base)
            inner[:, base : base + span] += value[:, 0:span]
        cs = cosines[...]
        sn = sines[...]
        reals, imags = [], []
        for p in range(parents_dev):
            in_real = inner[2 * p : 2 * p + 1, 0:parent_dirs]
            in_imag = inner[2 * p + 1 : 2 * p + 2, 0:parent_dirs]
            reals.append(cs * in_real + sn * in_imag)
            imags.append(cs * in_imag - sn * in_real)
        blank = jnp.zeros((128 - 2 * boxes, parent_dirs), F32)
        down = jnp.concatenate(
            reals + imags + [blank] + imags + [-r for r in reals] + [blank], 0
        ).astype(BF16)
        got = lax.dot_general(interp[...], down, NT, preferred_element_type=F32)
        twin[pl.ds(0, leaf_dirs, stride=2), :] = got[:, 0:128]
        twin[pl.ds(1, leaf_dirs, stride=2), :] = got[:, 128:256]
        flat = jnp.transpose(twin[...])[0 : 2 * boxes].astype(BF16)
        matrix = rad[...].reshape(2 * leaf_dirs, rad.shape[2])
        result = jnp.dot(flat, matrix, preferred_element_type=F32)
        product[:, 0, :] = result[0:boxes]
        product[:, 1, :] = result[boxes : 2 * boxes]

    return kernel


def on_device(
    coefficients, radiation, interpolation, angles, translations, sources, operators, counts
):
    boxes = coefficients.shape[0]
    parents_dev = boxes // 8
    leaf_dirs, parent_dirs = interpolation.shape
    bases = coefficients.shape[2]
    n_wide = lax.axis_size("wide")
    n_narrow = lax.axis_size("narrow")
    n_all = n_wide * n_narrow
    dirs = translations.shape[2]
    n_ops = translations.shape[0]
    plan = Plan(parents_dev * n_all, dirs, sources.shape[1], n_ops)
    rad = jnp.transpose(radiation, (2, 0, 1))
    table = jnp.transpose(translations, (1, 2, 0))
    chunk = 256
    vmem = pl.BlockSpec(memory_space=pltpu.VMEM)
    smem = pl.BlockSpec(memory_space=pltpu.SMEM)
    anywhere = pl.BlockSpec(memory_space=pl.ANY)

    send, cosines, sines = pl.pallas_call(
        upward_kernel(plan, n_wide, n_narrow, chunk),
        out_shape=(
            jax.ShapeDtypeStruct((n_all * parents_dev * plan.rows, 128), F32),
            jax.ShapeDtypeStruct(angles.shape, F32),
            jax.ShapeDtypeStruct(angles.shape, F32),
        ),
        in_specs=[smem, vmem, anywhere, anywhere, vmem, vmem, vmem],
        out_specs=(vmem, vmem, vmem),
        scratch_shapes=[
            pltpu.VMEM((leaf_dirs, 2, bases), BF16),
            pltpu.VMEM((leaf_dirs, parent_dirs), BF16),
            pltpu.VMEM((2 * leaf_dirs, 128), F32),
            pltpu.VMEM((2 * leaf_dirs, 128), F32),
            pltpu.VMEM((parents_dev, plan.code_width), F32),
            pltpu.VMEM((parents_dev, parent_dirs), F32),
            pltpu.VMEM((parents_dev, parent_dirs), F32),
            pltpu.SemaphoreType.DMA((parent_dirs // chunk + 1,)),
        ],
        compiler_params=pltpu.CompilerParams(vmem_limit_bytes=32 * MIB),
        name="upward",
    )(counts, coefficients, rad, interpolation, angles, sources, operators)

    send = send.reshape(n_all, parents_dev * plan.rows, 128)
    received = lax.all_to_all(send, ("wide", "narrow"), split_axis=0, concat_axis=0, tiled=True)
    received = received.reshape(-1, 128)

    body, group, step = translate_kernel(plan, n_wide, n_narrow, parents_dev)
    op_lanes = -(-n_ops // 128) * 128
    incoming = pl.pallas_call(
        body,
        out_shape=jax.ShapeDtypeStruct((n_wide * parents_dev * 2 * plan.tiles, 128), F32),
        in_specs=[vmem, vmem],
        out_specs=vmem,
        scratch_shapes=[
            pltpu.VMEM((2, plan.width, op_lanes), BF16),
            pltpu.VMEM((group * plan.parents, op_lanes), BF16),
            pltpu.VMEM((group * plan.parents, step), F32),
            pltpu.VMEM((group * plan.parents, step), F32),
        ],
        compiler_params=pltpu.CompilerParams(vmem_limit_bytes=24 * MIB),
        name="translate",
    )(table, received)

    incoming = incoming.reshape(n_wide, parents_dev * 2 * plan.tiles, 128)
    back = lax.all_to_all(incoming, "wide", split_axis=0, concat_axis=0, tiled=True)
    back = back.reshape(-1, 128)

    return pl.pallas_call(
        downward_kernel(plan, n_wide),
        out_shape=jax.ShapeDtypeStruct((boxes, 2, bases), F32),
        in_specs=[vmem] * 5,
        out_specs=vmem,
        scratch_shapes=[
            pltpu.VMEM((2 * parents_dev, parent_dirs + 128), F32),
            pltpu.VMEM((2 * leaf_dirs, 128), F32),
        ],
        compiler_params=pltpu.CompilerParams(vmem_limit_bytes=32 * MIB),
        name="downward",
    )(back, cosines, sines, interpolation, rad)


def solution(mesh):
    in_specs = (
        P(("wide", "narrow"), None, None),
        P(),
        P(),
        P(),
        P(None, None, "wide"),
        P(("wide", "narrow"), None),
        P(("wide", "narrow"), None),
        P(("wide", "narrow")),
    )
    out_specs = P(("wide", "narrow"), None, None)
    return jax.shard_map(
        on_device, mesh=mesh, in_specs=in_specs, out_specs=out_specs, check_vma=False
    )
```

```python
import jax
import jax.numpy as jnp
from jax import lax
from jax.experimental import pallas as pl
from jax.experimental.pallas import tpu as pltpu
from jax.sharding import PartitionSpec as P

F32 = jnp.float32
BF16 = jnp.bfloat16
MIB = 2**20
NT = (((1,), (1,)), ((), ()))


class Plan:
    def __init__(self, parents, dirs, length, ops):
        self.parents = parents
        self.dirs = dirs
        self.length = length
        self.ops = ops
        self.tiles = -(-dirs // 128)
        self.width = 128 * self.tiles
        spare = self.width - dirs
        used = dirs - 128 * (self.tiles - 1)
        self.bits = (ops - 1).bit_length()
        if 2 * spare >= length:
            self.extra = 0
            self.pieces = [
                (self.tiles - 1, used, spare, 0),
                (2 * self.tiles - 1, used, length - spare, spare),
            ]
        else:
            self.extra = -(-length // 128)
            self.pieces = [
                (2 * self.tiles + e, 0, min(128, length - 128 * e), 128 * e)
                for e in range(self.extra)
            ]
        self.rows = 2 * self.tiles + self.extra
        self.code_width = -(-length // 128) * 128


def sin_cos(angle):
    turns = jnp.floor(angle * 0.6366197723675814 + 0.5)
    quarter = turns.astype(jnp.int32)
    rest = angle - turns * 1.5703125
    rest = rest - turns * 4.837512969970703e-4
    rest = rest - turns * 7.54978995489188e-8
    square = rest * rest
    sine = ((-1.9515295891e-4 * square + 8.3321608736e-3) * square - 1.6666654611e-1) * square * rest + rest
    cosine = ((2.443315711809948e-5 * square - 1.388731625493765e-3) * square + 4.166664568298827e-2) * (
        square * square
    ) - 0.5 * square + 1.0
    swap = (quarter & 1) == 1
    sin_value = jnp.where(swap, cosine, sine)
    cos_value = jnp.where(swap, sine, cosine)
    sin_value = jnp.where((quarter & 2) == 2, -sin_value, sin_value)
    cos_value = jnp.where(((quarter + 1) & 2) == 2, -cos_value, cos_value)
    return sin_value, cos_value


def arrange(boxes, swapped):
    row = lax.broadcasted_iota(jnp.int32, (128, 2 * boxes), 0)
    column = lax.broadcasted_iota(jnp.int32, (128, 2 * boxes), 1)
    real_at = 2 * row
    imag_at = 2 * (row - boxes) + 1
    if swapped:
        first = jnp.where((row < boxes) & (column == real_at + 1), -1.0, 0.0)
        second = jnp.where((row >= boxes) & (row < 2 * boxes) & (column == imag_at - 1), 1.0, 0.0)
    else:
        first = jnp.where((row < boxes) & (column == real_at), 1.0, 0.0)
        second = jnp.where((row >= boxes) & (row < 2 * boxes) & (column == imag_at), 1.0, 0.0)
    return (first + second).astype(BF16)


def upward_kernel(plan, n_wide, n_narrow, cuts):
    def kernel(
        counts_hbm, coef_hbm, rad_hbm, interp_hbm, angles_hbm, sources_hbm, operators_hbm,
        send, cos_out, sin_out,
        counts, coef, rad, interp, angles, sources, operators,
        even, odd, codes, real_buf, imag_buf, sems,
    ):
        parent_dirs = angles.shape[1]
        leaf_dirs = rad.shape[0]
        boxes = coef.shape[0]
        parents_dev = boxes // 8
        n_chunks = len(cuts) - 1
        first = []
        for source, target in (
            (angles_hbm, angles),
            (coef_hbm, coef),
            (rad_hbm, rad),
            (sources_hbm, sources),
            (operators_hbm, operators),
            (counts_hbm, counts),
        ):
            first.append(pltpu.make_async_copy(source, target, sems.at[n_chunks + len(first)]))
            first[-1].start()
        copies = []
        for c in range(n_chunks):
            cut = (slice(None), pl.ds(cuts[c], cuts[c + 1] - cuts[c]))
            copies.append(pltpu.make_async_copy(interp_hbm.at[cut], interp.at[cut], sems.at[c]))
            copies[-1].start()

        first[0].wait()
        sines, cosines = sin_cos(angles[...])
        sin_out[...] = sines
        cos_out[...] = cosines

        for copy in first[3:]:
            copy.wait()
        code = sources[...] * (1 << plan.bits) + operators[...]
        at = lax.broadcasted_iota(jnp.int32, code.shape, 1)
        parent = lax.broadcasted_iota(jnp.int32, code.shape, 0)
        limit = jnp.zeros(code.shape, jnp.int32)
        for p in range(parents_dev):
            limit = jnp.where(parent == p, counts[p], limit)
        codes[...] = jnp.full(codes.shape, -1.0, F32)
        codes[:, 0 : plan.length] = jnp.where(at < limit, code, -1).astype(F32)

        first[1].wait()
        rows = coef[...].reshape(2 * boxes, coef.shape[2])
        plain = jnp.dot(arrange(boxes, False), rows, preferred_element_type=F32).astype(BF16)
        turned = jnp.dot(arrange(boxes, True), rows, preferred_element_type=F32).astype(BF16)
        weights = jnp.concatenate([plain, turned], 0)

        first[2].wait()
        matrix = rad[...].reshape(2 * leaf_dirs, rad.shape[2])
        both = lax.dot_general(matrix, weights, NT, preferred_element_type=F32)
        even[...] = both[:, 0:128]
        odd[...] = both[:, 128:256]
        leaf_t = even[pl.ds(0, leaf_dirs, stride=2), :] + odd[pl.ds(1, leaf_dirs, stride=2), :]
        leaf = jnp.transpose(leaf_t)[0 : 2 * boxes].astype(BF16)

        lane = lax.broadcasted_iota(jnp.int32, (parents_dev, 128), 1)
        tails = {}
        for tile, start, count, first_entry in plan.pieces:
            turn = (start - first_entry) % plan.code_width
            moved = codes[...] if turn == 0 else pltpu.roll(codes[...], turn, 1)
            tails[tile] = (moved[:, 0:128], (lane >= start) & (lane < start + count))

        def put(w, tile, piece):
            for n in range(n_narrow):
                first_row = (w * n_narrow + n) * parents_dev * plan.rows + tile
                send[pl.ds(first_row, parents_dev, stride=plan.rows), :] = piece

        def pack(w):
            base = plan.dirs * w // 128 * 128
            shift = plan.dirs * w % 128
            span = -(-(shift + plan.dirs) // 128) * 128
            span = min(max(span, plan.width), parent_dirs - base)
            for part, buf in ((0, real_buf), (1, imag_buf)):
                value = buf[:, base : base + span]
                if shift:
                    value = pltpu.roll(value, span - shift, 1)
                for k in range(plan.tiles):
                    tile = part * plan.tiles + k
                    piece = value[:, 128 * k : 128 * k + 128]
                    if k == plan.tiles - 1:
                        piece = jnp.where(lane < plan.dirs - 128 * k, piece, -1.0)
                    if tile in tails:
                        piece = jnp.where(tails[tile][1], tails[tile][0], piece)
                    put(w, tile, piece)
            for e in range(plan.extra):
                tile = 2 * plan.tiles + e
                put(w, tile, jnp.where(tails[tile][1], tails[tile][0], -1.0))

        packed = 0
        for c in range(n_chunks):
            copies[c].wait()
            cut = slice(cuts[c], cuts[c + 1])
            up = jnp.dot(leaf, interp[:, cut], preferred_element_type=F32)
            cs = cos_out[:, cut]
            sn = sin_out[:, cut]
            for p in range(parents_dev):
                up_real = up[8 * p : 8 * p + 8]
                up_imag = up[boxes + 8 * p : boxes + 8 * p + 8]
                real_buf[p : p + 1, cut] = jnp.sum(cs * up_real - sn * up_imag, 0, keepdims=True)
                imag_buf[p : p + 1, cut] = jnp.sum(cs * up_imag + sn * up_real, 0, keepdims=True)
            while packed < n_wide and -(-plan.dirs * (packed + 1) // 128) * 128 <= cuts[c + 1]:
                pack(packed)
                packed += 1

    return kernel


def translate_kernel(plan, n_wide, n_narrow, parents_dev):
    targets = n_wide * parents_dev
    group = max(1, min(targets, 1024 // plan.parents))
    step = min(256, plan.width)

    def kernel(table_in, received, out, table, tally, a_real, a_imag):
        mine = lax.axis_index("narrow")
        table[...] = jnp.zeros(table.shape, BF16)
        table[:, 0 : plan.dirs, 0 : plan.ops] = table_in[...].astype(BF16)
        lane = lax.broadcasted_iota(jnp.int32, (1, 128), 1)
        source_at = lax.broadcasted_iota(jnp.int32, (plan.parents, 128), 0)
        op_at = lax.broadcasted_iota(jnp.int32, (table.shape[2], 128), 0)

        def do_group(first_target):
            for i in range(group):
                target = first_target + i
                w = target // parents_dev
                p = target % parents_dev
                row = ((w * n_narrow + mine) * parents_dev + p) * plan.rows
                hits, picks = [], []
                for tile, start, count, _ in plan.pieces:
                    code = received[pl.ds(row + tile, 1), :]
                    code = jnp.where((lane >= start) & (lane < start + count), code, -1.0).astype(jnp.int32)
                    hits.append(jnp.where(source_at == (code >> plan.bits), 1.0, 0.0).astype(BF16))
                    picks.append(jnp.where(op_at == (code & ((1 << plan.bits) - 1)), 1.0, 0.0).astype(BF16))
                count_of = lax.dot_general(
                    jnp.concatenate(hits, 1), jnp.concatenate(picks, 1), NT, preferred_element_type=F32
                )
                tally[i * plan.parents : (i + 1) * plan.parents, :] = count_of.astype(BF16)
            for j in range(plan.width // step):
                cut = slice(j * step, (j + 1) * step)
                a_real[...] = lax.dot_general(tally[...], table[0, cut, :], NT, preferred_element_type=F32)
                a_imag[...] = lax.dot_general(tally[...], table[1, cut, :], NT, preferred_element_type=F32)
                for q in range(step // 128):
                    k = j * (step // 128) + q
                    lanes = slice(128 * q, 128 * q + 128)
                    out_real = received[pl.ds(k, plan.parents, stride=plan.rows), :]
                    out_imag = received[pl.ds(plan.tiles + k, plan.parents, stride=plan.rows), :]
                    for i in range(group):
                        own = slice(i * plan.parents, (i + 1) * plan.parents)
                        op_real = a_real[own, lanes]
                        op_imag = a_imag[own, lanes]
                        real = jnp.sum(op_real * out_real - op_imag * out_imag, 0, keepdims=True)
                        imag = jnp.sum(op_real * out_imag + op_imag * out_real, 0, keepdims=True)
                        at = (first_target + i) * 2 * plan.tiles + k
                        out[pl.ds(at, 1), :] = real
                        out[pl.ds(at + plan.tiles, 1), :] = imag

        if targets == group:
            do_group(0)
        else:
            pl.loop(0, targets // group)(lambda g: do_group(g * group))

    return kernel, group, step


def downward_kernel(plan, n_wide):
    def kernel(received, cosines, sines, interp, rad, product, inner, twin):
        parent_dirs = cosines.shape[1]
        leaf_dirs = rad.shape[0]
        parents_dev = product.shape[0] // 8
        boxes = product.shape[0]
        parts = 2 * parents_dev
        lane = lax.broadcasted_iota(jnp.int32, (parts, plan.width), 1)
        inner[...] = jnp.zeros(inner.shape, F32)
        for w in range(n_wide):
            base = plan.dirs * w // 128 * 128
            shift = plan.dirs * w % 128
            span = -(-(shift + plan.dirs) // 128) * 128
            tiles = [
                received[pl.ds(w * parts * plan.tiles + k, parts, stride=plan.tiles), :]
                for k in range(plan.tiles)
            ]
            value = tiles[0] if plan.tiles == 1 else jnp.concatenate(tiles, 1)
            value = jnp.where(lane < plan.dirs, value, 0.0)
            if span > plan.width:
                value = jnp.concatenate([value, jnp.zeros((parts, span - plan.width), F32)], 1)
            if shift:
                value = pltpu.roll(value, shift, 1)
            span = min(value.shape[1], inner.shape[1] - base)
            inner[:, base : base + span] += value[:, 0:span]
        cs = cosines[...]
        sn = sines[...]
        reals, imags = [], []
        for p in range(parents_dev):
            in_real = inner[2 * p : 2 * p + 1, 0:parent_dirs]
            in_imag = inner[2 * p + 1 : 2 * p + 2, 0:parent_dirs]
            reals.append(cs * in_real + sn * in_imag)
            imags.append(cs * in_imag - sn * in_real)
        blank = jnp.zeros((128 - 2 * boxes, parent_dirs), F32)
        down = jnp.concatenate(
            reals + imags + [blank] + imags + [-r for r in reals] + [blank], 0
        ).astype(BF16)
        got = lax.dot_general(interp[...], down, NT, preferred_element_type=F32)
        twin[pl.ds(0, leaf_dirs, stride=2), :] = got[:, 0:128]
        twin[pl.ds(1, leaf_dirs, stride=2), :] = got[:, 128:256]
        flat = jnp.transpose(twin[...])[0 : 2 * boxes].astype(BF16)
        matrix = rad[...].reshape(2 * leaf_dirs, rad.shape[2])
        result = jnp.dot(flat, matrix, preferred_element_type=F32)
        product[:, 0, :] = result[0:boxes]
        product[:, 1, :] = result[boxes : 2 * boxes]

    return kernel


def on_device(
    coefficients, radiation, interpolation, angles, translations, sources, operators, counts
):
    boxes = coefficients.shape[0]
    parents_dev = boxes // 8
    leaf_dirs, parent_dirs = interpolation.shape
    bases = coefficients.shape[2]
    n_wide = lax.axis_size("wide")
    n_narrow = lax.axis_size("narrow")
    n_all = n_wide * n_narrow
    dirs = translations.shape[2]
    n_ops = translations.shape[0]
    plan = Plan(parents_dev * n_all, dirs, sources.shape[1], n_ops)
    rad = jnp.transpose(radiation, (2, 0, 1))
    table = jnp.transpose(translations, (1, 2, 0))
    cuts = [0, 1664]
    cuts = [c for c in cuts if c < parent_dirs] + [parent_dirs]
    vmem = pl.BlockSpec(memory_space=pltpu.VMEM)
    anywhere = pl.BlockSpec(memory_space=pl.ANY)

    send, cosines, sines = pl.pallas_call(
        upward_kernel(plan, n_wide, n_narrow, cuts),
        out_shape=(
            jax.ShapeDtypeStruct((n_all * parents_dev * plan.rows, 128), F32),
            jax.ShapeDtypeStruct(angles.shape, F32),
            jax.ShapeDtypeStruct(angles.shape, F32),
        ),
        in_specs=[anywhere] * 7,
        out_specs=(vmem, vmem, vmem),
        scratch_shapes=[
            pltpu.SMEM((parents_dev,), jnp.int32),
            pltpu.VMEM((boxes, 2, bases), BF16),
            pltpu.VMEM((leaf_dirs, 2, bases), BF16),
            pltpu.VMEM((leaf_dirs, parent_dirs), BF16),
            pltpu.VMEM(angles.shape, F32),
            pltpu.VMEM(sources.shape, jnp.int32),
            pltpu.VMEM(operators.shape, jnp.int32),
            pltpu.VMEM((2 * leaf_dirs, 128), F32),
            pltpu.VMEM((2 * leaf_dirs, 128), F32),
            pltpu.VMEM((parents_dev, plan.code_width), F32),
            pltpu.VMEM((parents_dev, parent_dirs), F32),
            pltpu.VMEM((parents_dev, parent_dirs), F32),
            pltpu.SemaphoreType.DMA((len(cuts) + 5,)),
        ],
        compiler_params=pltpu.CompilerParams(vmem_limit_bytes=56 * MIB),
        name="upward",
    )(counts, coefficients, rad, interpolation, angles, sources, operators)

    send = send.reshape(n_all, parents_dev * plan.rows, 128)
    received = lax.all_to_all(send, ("wide", "narrow"), split_axis=0, concat_axis=0, tiled=True)
    received = received.reshape(-1, 128)

    body, group, step = translate_kernel(plan, n_wide, n_narrow, parents_dev)
    op_lanes = -(-n_ops // 128) * 128
    incoming = pl.pallas_call(
        body,
        out_shape=jax.ShapeDtypeStruct((n_wide * parents_dev * 2 * plan.tiles, 128), F32),
        in_specs=[vmem, vmem],
        out_specs=vmem,
        scratch_shapes=[
            pltpu.VMEM((2, plan.width, op_lanes), BF16),
            pltpu.VMEM((group * plan.parents, op_lanes), BF16),
            pltpu.VMEM((group * plan.parents, step), F32),
            pltpu.VMEM((group * plan.parents, step), F32),
        ],
        compiler_params=pltpu.CompilerParams(vmem_limit_bytes=24 * MIB),
        name="translate",
    )(table, received)

    incoming = incoming.reshape(n_wide, parents_dev * 2 * plan.tiles, 128)
    back = lax.all_to_all(incoming, "wide", split_axis=0, concat_axis=0, tiled=True)
    back = back.reshape(-1, 128)

    return pl.pallas_call(
        downward_kernel(plan, n_wide),
        out_shape=jax.ShapeDtypeStruct((boxes, 2, bases), F32),
        in_specs=[vmem] * 5,
        out_specs=vmem,
        scratch_shapes=[
            pltpu.VMEM((2 * parents_dev, parent_dirs + 128), F32),
            pltpu.VMEM((2 * leaf_dirs, 128), F32),
        ],
        compiler_params=pltpu.CompilerParams(vmem_limit_bytes=32 * MIB),
        name="downward",
    )(back, cosines, sines, interpolation, rad)


def solution(mesh):
    in_specs = (
        P(("wide", "narrow"), None, None),
        P(),
        P(),
        P(),
        P(None, None, "wide"),
        P(("wide", "narrow"), None),
        P(("wide", "narrow"), None),
        P(("wide", "narrow")),
    )
    out_specs = P(("wide", "narrow"), None, None)
    return jax.shard_map(
        on_device, mesh=mesh, in_specs=in_specs, out_specs=out_specs, check_vma=False
    )
```

```python
import jax
import jax.numpy as jnp
from jax import lax
from jax.experimental import pallas as pl
from jax.experimental.pallas import tpu as pltpu
from jax.sharding import PartitionSpec as P

F32 = jnp.float32
BF16 = jnp.bfloat16
MIB = 2**20
NT = (((1,), (1,)), ((), ()))


class Plan:
    def __init__(self, parents, dirs, length, ops):
        self.parents = parents
        self.dirs = dirs
        self.length = length
        self.ops = ops
        self.tiles = -(-dirs // 128)
        self.width = 128 * self.tiles
        spare = self.width - dirs
        used = dirs - 128 * (self.tiles - 1)
        self.bits = (ops - 1).bit_length()
        if 2 * spare >= length:
            self.extra = 0
            self.pieces = [
                (self.tiles - 1, used, spare, 0),
                (2 * self.tiles - 1, used, length - spare, spare),
            ]
        else:
            self.extra = -(-length // 128)
            self.pieces = [
                (2 * self.tiles + e, 0, min(128, length - 128 * e), 128 * e)
                for e in range(self.extra)
            ]
        self.rows = 2 * self.tiles + self.extra
        self.code_width = -(-length // 128) * 128


def sin_cos(angle):
    turns = jnp.floor(angle * 0.6366197723675814 + 0.5)
    quarter = turns.astype(jnp.int32)
    rest = angle - turns * 1.5703125
    rest = rest - turns * 4.837512969970703e-4
    rest = rest - turns * 7.54978995489188e-8
    square = rest * rest
    sine = ((-1.9515295891e-4 * square + 8.3321608736e-3) * square - 1.6666654611e-1) * square * rest + rest
    cosine = ((2.443315711809948e-5 * square - 1.388731625493765e-3) * square + 4.166664568298827e-2) * (
        square * square
    ) - 0.5 * square + 1.0
    swap = (quarter & 1) == 1
    sin_value = jnp.where(swap, cosine, sine)
    cos_value = jnp.where(swap, sine, cosine)
    sin_value = jnp.where((quarter & 2) == 2, -sin_value, sin_value)
    cos_value = jnp.where(((quarter + 1) & 2) == 2, -cos_value, cos_value)
    return sin_value, cos_value


def arrange(boxes, swapped):
    row = lax.broadcasted_iota(jnp.int32, (128, 2 * boxes), 0)
    column = lax.broadcasted_iota(jnp.int32, (128, 2 * boxes), 1)
    real_at = 2 * row
    imag_at = 2 * (row - boxes) + 1
    if swapped:
        first = jnp.where((row < boxes) & (column == real_at + 1), -1.0, 0.0)
        second = jnp.where((row >= boxes) & (row < 2 * boxes) & (column == imag_at - 1), 1.0, 0.0)
    else:
        first = jnp.where((row < boxes) & (column == real_at), 1.0, 0.0)
        second = jnp.where((row >= boxes) & (row < 2 * boxes) & (column == imag_at), 1.0, 0.0)
    return (first + second).astype(BF16)


def upward_kernel(plan, n_wide, n_narrow, cuts):
    def kernel(
        counts_hbm, coef_hbm, rad_hbm, interp_hbm, angles_hbm, sources_hbm, operators_hbm,
        send, cos_out, sin_out,
        counts, coef, rad, interp, angles, sources, operators,
        even, odd, codes, real_buf, imag_buf, sems,
    ):
        parent_dirs = angles.shape[1]
        leaf_dirs = rad.shape[0]
        boxes = coef.shape[0]
        parents_dev = boxes // 8
        n_chunks = len(cuts) - 1
        half = -(-leaf_dirs // 16) * 16
        first = []
        for source, target in (
            (angles_hbm, angles),
            (coef_hbm, coef),
            (rad_hbm, rad),
            (sources_hbm, sources),
            (operators_hbm, operators),
            (counts_hbm, counts),
        ):
            first.append(pltpu.make_async_copy(source, target, sems.at[n_chunks + len(first)]))
            first[-1].start()
        copies = []
        for c in range(n_chunks):
            cut = (slice(None), pl.ds(cuts[c], cuts[c + 1] - cuts[c]))
            copies.append(pltpu.make_async_copy(interp_hbm.at[cut], interp.at[cut], sems.at[c]))
            copies[-1].start()

        first[0].wait()
        sines, cosines = sin_cos(angles[...])
        sin_out[...] = sines
        cos_out[...] = cosines

        for copy in first[3:]:
            copy.wait()
        code = sources[...] * (1 << plan.bits) + operators[...]
        at = lax.broadcasted_iota(jnp.int32, code.shape, 1)
        parent = lax.broadcasted_iota(jnp.int32, code.shape, 0)
        limit = jnp.zeros(code.shape, jnp.int32)
        for p in range(parents_dev):
            limit = jnp.where(parent == p, counts[p], limit)
        codes[...] = jnp.full(codes.shape, -1.0, F32)
        codes[:, 0 : plan.length] = jnp.where(at < limit, code, -1).astype(F32)

        first[1].wait()
        rows = coef[...].reshape(2 * boxes, coef.shape[2])
        plain = jnp.dot(arrange(boxes, False), rows, preferred_element_type=F32).astype(BF16)
        turned = jnp.dot(arrange(boxes, True), rows, preferred_element_type=F32).astype(BF16)
        weights = jnp.concatenate([plain, turned], 0)

        first[2].wait()
        matrix = rad[...].reshape(2 * leaf_dirs, rad.shape[2])
        weights_t = jnp.transpose(weights)
        for a in range(0, 2 * leaf_dirs, half):
            z = min(a + half, 2 * leaf_dirs)
            both = jnp.dot(matrix[a:z], weights_t, preferred_element_type=F32)
            even[a:z, :] = both[:, 0:128]
            odd[a:z, :] = both[:, 128:256]
        leaf_t = even[pl.ds(0, leaf_dirs, stride=2), :] + odd[pl.ds(1, leaf_dirs, stride=2), :]
        leaf = jnp.transpose(leaf_t)[0 : 2 * boxes].astype(BF16)

        lane = lax.broadcasted_iota(jnp.int32, (parents_dev, 128), 1)
        tails = {}
        for tile, start, count, first_entry in plan.pieces:
            turn = (start - first_entry) % plan.code_width
            moved = codes[...] if turn == 0 else pltpu.roll(codes[...], turn, 1)
            tails[tile] = (moved[:, 0:128], (lane >= start) & (lane < start + count))

        def put(w, tile, piece):
            for n in range(n_narrow):
                first_row = (w * n_narrow + n) * parents_dev * plan.rows + tile
                send[pl.ds(first_row, parents_dev, stride=plan.rows), :] = piece

        def pack(w):
            base = plan.dirs * w // 128 * 128
            shift = plan.dirs * w % 128
            span = -(-(shift + plan.dirs) // 128) * 128
            span = min(max(span, plan.width), parent_dirs - base)
            for part, buf in ((0, real_buf), (1, imag_buf)):
                value = buf[:, base : base + span]
                if shift:
                    value = pltpu.roll(value, span - shift, 1)
                for k in range(plan.tiles):
                    tile = part * plan.tiles + k
                    piece = value[:, 128 * k : 128 * k + 128]
                    if k == plan.tiles - 1:
                        piece = jnp.where(lane < plan.dirs - 128 * k, piece, -1.0)
                    if tile in tails:
                        piece = jnp.where(tails[tile][1], tails[tile][0], piece)
                    put(w, tile, piece)
            for e in range(plan.extra):
                tile = 2 * plan.tiles + e
                put(w, tile, jnp.where(tails[tile][1], tails[tile][0], -1.0))

        packed = 0
        for c in range(n_chunks):
            copies[c].wait()
            cut = slice(cuts[c], cuts[c + 1])
            up = jnp.dot(leaf, interp[:, cut], preferred_element_type=F32)
            cs = cos_out[:, cut]
            sn = sin_out[:, cut]
            for p in range(parents_dev):
                up_real = up[8 * p : 8 * p + 8]
                up_imag = up[boxes + 8 * p : boxes + 8 * p + 8]
                real_buf[p : p + 1, cut] = jnp.sum(cs * up_real - sn * up_imag, 0, keepdims=True)
                imag_buf[p : p + 1, cut] = jnp.sum(cs * up_imag + sn * up_real, 0, keepdims=True)
            while packed < n_wide and -(-plan.dirs * (packed + 1) // 128) * 128 <= cuts[c + 1]:
                pack(packed)
                packed += 1

    return kernel


def translate_kernel(plan, n_wide, n_narrow, parents_dev):
    targets = n_wide * parents_dev
    group = max(1, min(targets, 1024 // plan.parents))
    step = min(256, plan.width)

    def kernel(table_in, received, out, table, tally, a_real, a_imag):
        mine = lax.axis_index("narrow")
        table[...] = jnp.zeros(table.shape, BF16)
        table[:, 0 : plan.dirs, 0 : plan.ops] = table_in[...].astype(BF16)
        lane = lax.broadcasted_iota(jnp.int32, (1, 128), 1)
        highs = table.shape[2] // 128
        kind = BF16 if highs * plan.parents <= 256 else F32
        key_at = lax.broadcasted_iota(jnp.int32, (highs * plan.parents, 128), 0).astype(kind)
        low_at = lax.broadcasted_iota(jnp.int32, (128, 128), 0).astype(BF16)

        def do_group(first_target):
            for i in range(group):
                target = first_target + i
                w = target // parents_dev
                p = target % parents_dev
                row = ((w * n_narrow + mine) * parents_dev + p) * plan.rows
                keys, lows = [], []
                for tile, start, count, _ in plan.pieces:
                    code = received[pl.ds(row + tile, 1), :]
                    code = jnp.where((lane >= start) & (lane < start + count), code, -1.0).astype(jnp.int32)
                    op = code & ((1 << plan.bits) - 1)
                    key = jnp.where(code < 0, -1, (op >> 7) * plan.parents + (code >> plan.bits))
                    keys.append(jnp.where(key_at == key.astype(kind), jnp.ones((), kind), jnp.zeros((), kind)).astype(BF16))
                    lows.append(jnp.where(low_at == (op & 127).astype(BF16), jnp.ones((), BF16), jnp.zeros((), BF16)))
                count_of = lax.dot_general(
                    jnp.concatenate(keys, 1), jnp.concatenate(lows, 1), NT, preferred_element_type=F32
                ).astype(BF16)
                own = slice(i * plan.parents, (i + 1) * plan.parents)
                for h in range(highs):
                    tally[own, 128 * h : 128 * h + 128] = count_of[h * plan.parents : (h + 1) * plan.parents]
            for j in range(plan.width // step):
                cut = slice(j * step, (j + 1) * step)
                for a in range(0, tally.shape[0], 512):
                    z = min(a + 512, tally.shape[0])
                    a_real[a:z, :] = lax.dot_general(tally[a:z, :], table[0, cut, :], NT, preferred_element_type=F32)
                    a_imag[a:z, :] = lax.dot_general(tally[a:z, :], table[1, cut, :], NT, preferred_element_type=F32)
                for q in range(step // 128):
                    k = j * (step // 128) + q
                    lanes = slice(128 * q, 128 * q + 128)
                    out_real = received[pl.ds(k, plan.parents, stride=plan.rows), :]
                    out_imag = received[pl.ds(plan.tiles + k, plan.parents, stride=plan.rows), :]
                    for i in range(group):
                        own = slice(i * plan.parents, (i + 1) * plan.parents)
                        op_real = a_real[own, lanes]
                        op_imag = a_imag[own, lanes]
                        real = jnp.sum(op_real * out_real - op_imag * out_imag, 0, keepdims=True)
                        imag = jnp.sum(op_real * out_imag + op_imag * out_real, 0, keepdims=True)
                        at = (first_target + i) * 2 * plan.tiles + k
                        out[pl.ds(at, 1), :] = real
                        out[pl.ds(at + plan.tiles, 1), :] = imag

        if targets == group:
            do_group(0)
        else:
            pl.loop(0, targets // group)(lambda g: do_group(g * group))

    return kernel, group, step


def downward_kernel(plan, n_wide):
    def kernel(received, cosines, sines, interp, rad, product, inner, twin):
        parent_dirs = cosines.shape[1]
        leaf_dirs = rad.shape[0]
        parents_dev = product.shape[0] // 8
        boxes = product.shape[0]
        parts = 2 * parents_dev
        lane = lax.broadcasted_iota(jnp.int32, (parts, plan.width), 1)
        inner[...] = jnp.zeros(inner.shape, F32)
        for w in range(n_wide):
            base = plan.dirs * w // 128 * 128
            shift = plan.dirs * w % 128
            span = -(-(shift + plan.dirs) // 128) * 128
            tiles = [
                received[pl.ds(w * parts * plan.tiles + k, parts, stride=plan.tiles), :]
                for k in range(plan.tiles)
            ]
            value = tiles[0] if plan.tiles == 1 else jnp.concatenate(tiles, 1)
            value = jnp.where(lane < plan.dirs, value, 0.0)
            if span > plan.width:
                value = jnp.concatenate([value, jnp.zeros((parts, span - plan.width), F32)], 1)
            if shift:
                value = pltpu.roll(value, shift, 1)
            span = min(value.shape[1], inner.shape[1] - base)
            inner[:, base : base + span] += value[:, 0:span]
        cs = cosines[...]
        sn = sines[...]
        reals, imags = [], []
        for p in range(parents_dev):
            in_real = inner[2 * p : 2 * p + 1, 0:parent_dirs]
            in_imag = inner[2 * p + 1 : 2 * p + 2, 0:parent_dirs]
            reals.append(cs * in_real + sn * in_imag)
            imags.append(cs * in_imag - sn * in_real)
        blank = jnp.zeros((128 - 2 * boxes, parent_dirs), F32)
        down = jnp.concatenate(
            reals + imags + [blank] + imags + [-r for r in reals] + [blank], 0
        ).astype(BF16)
        down_t = jnp.transpose(down)
        quarter = -(-leaf_dirs // 64) * 16
        got = jnp.concatenate(
            [
                jnp.dot(interp[a : min(a + quarter, leaf_dirs), :], down_t, preferred_element_type=F32)
                for a in range(0, leaf_dirs, quarter)
            ],
            0,
        )
        twin[pl.ds(0, leaf_dirs, stride=2), :] = got[:, 0:128]
        twin[pl.ds(1, leaf_dirs, stride=2), :] = got[:, 128:256]
        flat = jnp.transpose(twin[...])[0 : 2 * boxes].astype(BF16)
        matrix = rad[...].reshape(2 * leaf_dirs, rad.shape[2])
        result = jnp.dot(flat, matrix, preferred_element_type=F32)
        product[:, 0, :] = result[0:boxes]
        product[:, 1, :] = result[boxes : 2 * boxes]

    return kernel


def on_device(
    coefficients, radiation, interpolation, angles, translations, sources, operators, counts
):
    boxes = coefficients.shape[0]
    parents_dev = boxes // 8
    leaf_dirs, parent_dirs = interpolation.shape
    bases = coefficients.shape[2]
    n_wide = lax.axis_size("wide")
    n_narrow = lax.axis_size("narrow")
    n_all = n_wide * n_narrow
    dirs = translations.shape[2]
    n_ops = translations.shape[0]
    plan = Plan(parents_dev * n_all, dirs, sources.shape[1], n_ops)
    rad = jnp.transpose(radiation, (2, 0, 1))
    table = jnp.transpose(translations, (1, 2, 0))
    cuts = [0, 1664]
    cuts = [c for c in cuts if c < parent_dirs] + [parent_dirs]
    vmem = pl.BlockSpec(memory_space=pltpu.VMEM)
    anywhere = pl.BlockSpec(memory_space=pl.ANY)

    send, cosines, sines = pl.pallas_call(
        upward_kernel(plan, n_wide, n_narrow, cuts),
        out_shape=(
            jax.ShapeDtypeStruct((n_all * parents_dev * plan.rows, 128), F32),
            jax.ShapeDtypeStruct(angles.shape, F32),
            jax.ShapeDtypeStruct(angles.shape, F32),
        ),
        in_specs=[anywhere] * 7,
        out_specs=(vmem, vmem, vmem),
        scratch_shapes=[
            pltpu.SMEM((parents_dev,), jnp.int32),
            pltpu.VMEM((boxes, 2, bases), BF16),
            pltpu.VMEM((leaf_dirs, 2, bases), BF16),
            pltpu.VMEM((leaf_dirs, parent_dirs), BF16),
            pltpu.VMEM(angles.shape, F32),
            pltpu.VMEM(sources.shape, jnp.int32),
            pltpu.VMEM(operators.shape, jnp.int32),
            pltpu.VMEM((2 * leaf_dirs, 128), F32),
            pltpu.VMEM((2 * leaf_dirs, 128), F32),
            pltpu.VMEM((parents_dev, plan.code_width), F32),
            pltpu.VMEM((parents_dev, parent_dirs), F32),
            pltpu.VMEM((parents_dev, parent_dirs), F32),
            pltpu.SemaphoreType.DMA((len(cuts) + 5,)),
        ],
        compiler_params=pltpu.CompilerParams(vmem_limit_bytes=56 * MIB),
        name="upward",
    )(counts, coefficients, rad, interpolation, angles, sources, operators)

    send = send.reshape(n_all, parents_dev * plan.rows, 128)
    received = lax.all_to_all(send, ("wide", "narrow"), split_axis=0, concat_axis=0, tiled=True)
    received = received.reshape(-1, 128)

    body, group, step = translate_kernel(plan, n_wide, n_narrow, parents_dev)
    op_lanes = -(-n_ops // 128) * 128
    incoming = pl.pallas_call(
        body,
        out_shape=jax.ShapeDtypeStruct((n_wide * parents_dev * 2 * plan.tiles, 128), F32),
        in_specs=[vmem, vmem],
        out_specs=vmem,
        scratch_shapes=[
            pltpu.VMEM((2, plan.width, op_lanes), BF16),
            pltpu.VMEM((group * plan.parents, op_lanes), BF16),
            pltpu.VMEM((group * plan.parents, step), F32),
            pltpu.VMEM((group * plan.parents, step), F32),
        ],
        compiler_params=pltpu.CompilerParams(vmem_limit_bytes=24 * MIB),
        name="translate",
    )(table, received)

    incoming = incoming.reshape(n_wide, parents_dev * 2 * plan.tiles, 128)
    back = lax.all_to_all(incoming, "wide", split_axis=0, concat_axis=0, tiled=True)
    back = back.reshape(-1, 128)

    return pl.pallas_call(
        downward_kernel(plan, n_wide),
        out_shape=jax.ShapeDtypeStruct((boxes, 2, bases), F32),
        in_specs=[vmem] * 5,
        out_specs=vmem,
        scratch_shapes=[
            pltpu.VMEM((2 * parents_dev, parent_dirs + 128), F32),
            pltpu.VMEM((2 * leaf_dirs, 128), F32),
        ],
        compiler_params=pltpu.CompilerParams(vmem_limit_bytes=32 * MIB),
        name="downward",
    )(back, cosines, sines, interpolation, rad)


def solution(mesh):
    in_specs = (
        P(("wide", "narrow"), None, None),
        P(),
        P(),
        P(),
        P(None, None, "wide"),
        P(("wide", "narrow"), None),
        P(("wide", "narrow"), None),
        P(("wide", "narrow")),
    )
    out_specs = P(("wide", "narrow"), None, None)
    return jax.shard_map(
        on_device, mesh=mesh, in_specs=in_specs, out_specs=out_specs, check_vma=False
    )
```

```python
import jax
import jax.numpy as jnp
from jax import lax
from jax.experimental import pallas as pl
from jax.experimental.pallas import tpu as pltpu
from jax.sharding import PartitionSpec as P

F32 = jnp.float32
BF16 = jnp.bfloat16
MIB = 2**20
NT = (((1,), (1,)), ((), ()))


class Plan:
    def __init__(self, own, n_wide, n_narrow, dirs, length, ops):
        self.own = own
        self.n_wide = n_wide
        self.n_narrow = n_narrow
        self.devices = n_wide * n_narrow
        self.parents = own * self.devices
        first = n_wide * 5 // 8
        self.order = list(range(first, -1, -1)) + list(range(first + 1, n_wide))
        self.cores = 2 if n_narrow % 2 == 0 else 1
        self.pairs = n_narrow // self.cores
        self.peers = n_wide * self.pairs
        self.dirs = dirs
        self.length = length
        self.ops = ops
        self.full = dirs // 128
        self.rest = dirs % 128
        self.tiles = -(-dirs // 128)
        self.width = 128 * self.tiles
        self.bits = ops.bit_length()
        entry_bits = self.bits + (self.parents - 1).bit_length()
        self.none = (1 << entry_bits) - 1
        self.rest_row = own * 2 * self.full
        self.shared = 2 * own * self.rest <= 128
        rest_rows = 0 if not self.rest else 1 if self.shared else 2 * own
        self.list_row = self.rest_row + rest_rows
        self.dense = entry_bits <= 15 and length <= 192
        self.entry_tiles = 2 if self.dense else -(-length // 128)
        self.list_rows = 1 if self.dense else self.entry_tiles
        self.rows = self.list_row + own * self.list_rows

    def rest_at(self, p, part):
        if self.shared:
            return self.rest_row, (2 * p + part) * self.rest
        return self.rest_row + 2 * p + part, 0

    def groups(self):
        return [
            [w * self.n_narrow + pair * self.cores + core for w in self.order for pair in range(self.pairs)]
            for core in range(self.cores)
        ]

    def place(self, source):
        narrow_shift = self.own.bit_length() - 1
        device = source >> narrow_shift
        place = jnp.zeros(source.shape, jnp.int32)
        for i, w in enumerate(self.order):
            for pair in range(self.pairs):
                for core in range(self.cores):
                    flat = w * self.n_narrow + pair * self.cores + core
                    block = core * self.peers + i * self.pairs + pair
                    place = jnp.where(device == flat, block, place)
        return (source & (self.own - 1)) * self.devices + place

    def encode(self, entries, lane):
        if not self.dense:
            return entries
        first, third = entries
        low = jnp.where(lane < 64, third & 255, pltpu.roll(third, 64, 1) >> 8)
        return [first * 256 + low]

    def decode(self, words, lane):
        if not self.dense:
            return words
        low = words[0] & 255
        third = low + (pltpu.roll(low, 64, 1) << 8)
        return [words[0] >> 8, jnp.where(lane < 64, third, self.none)]


def sin_cos(angle):
    turns = jnp.floor(angle * 0.6366197723675814 + 0.5)
    quarter = turns.astype(jnp.int32)
    rest = angle - turns * 1.5703125
    rest = rest - turns * 4.837512969970703e-4
    rest = rest - turns * 7.54978995489188e-8
    square = rest * rest
    sine = ((-1.9515295891e-4 * square + 8.3321608736e-3) * square - 1.6666654611e-1) * square * rest + rest
    cosine = ((2.443315711809948e-5 * square - 1.388731625493765e-3) * square + 4.166664568298827e-2) * (
        square * square
    ) - 0.5 * square + 1.0
    swap = (quarter & 1) == 1
    sin_value = jnp.where(swap, cosine, sine)
    cos_value = jnp.where(swap, sine, cosine)
    sin_value = jnp.where((quarter & 2) == 2, -sin_value, sin_value)
    cos_value = jnp.where(((quarter + 1) & 2) == 2, -cos_value, cos_value)
    return sin_value, cos_value


def arrange(boxes, swapped):
    row = lax.broadcasted_iota(jnp.int32, (128, 2 * boxes), 0)
    column = lax.broadcasted_iota(jnp.int32, (128, 2 * boxes), 1)
    real_at = 2 * row
    imag_at = 2 * (row - boxes) + 1
    if swapped:
        first = jnp.where((row < boxes) & (column == real_at + 1), -1.0, 0.0)
        second = jnp.where((row >= boxes) & (row < 2 * boxes) & (column == imag_at - 1), 1.0, 0.0)
    else:
        first = jnp.where((row < boxes) & (column == real_at), 1.0, 0.0)
        second = jnp.where((row >= boxes) & (row < 2 * boxes) & (column == imag_at), 1.0, 0.0)
    return (first + second).astype(BF16)


def upward_kernel(plan, cuts):
    def kernel(
        counts_hbm, coef_hbm, rad_hbm, interp_hbm, angles_hbm, sources_hbm, operators_hbm,
        send, cos_out, sin_out,
        counts, coef, rad, interp, angles, sources, operators,
        even, odd, codes, real_buf, imag_buf, sems,
    ):
        parent_dirs = angles.shape[1]
        leaf_dirs = rad.shape[0]
        boxes = coef.shape[0]
        parents_dev = boxes // 8
        n_chunks = len(cuts) - 1
        half = -(-leaf_dirs // 16) * 16
        first = []
        for source, target in (
            (angles_hbm, angles),
            (coef_hbm, coef),
            (rad_hbm, rad),
            (sources_hbm, sources),
            (operators_hbm, operators),
            (counts_hbm, counts),
        ):
            first.append(pltpu.make_async_copy(source, target, sems.at[n_chunks + len(first)]))
            first[-1].start()
        copies = []
        for c in range(n_chunks):
            cut = (slice(None), pl.ds(cuts[c], cuts[c + 1] - cuts[c]))
            copies.append(pltpu.make_async_copy(interp_hbm.at[cut], interp.at[cut], sems.at[c]))
            copies[-1].start()

        first[0].wait()
        sines, cosines = sin_cos(angles[...])
        sin_out[...] = sines
        cos_out[...] = cosines

        for copy in first[3:]:
            copy.wait()
        code = plan.place(sources[...]) * (1 << plan.bits) + operators[...]
        at = lax.broadcasted_iota(jnp.int32, code.shape, 1)
        parent = lax.broadcasted_iota(jnp.int32, code.shape, 0)
        limit = jnp.zeros(code.shape, jnp.int32)
        for p in range(parents_dev):
            limit = jnp.where(parent == p, counts[p], limit)
        codes[...] = jnp.full(codes.shape, plan.none, jnp.int32)
        codes[:, 0 : plan.length] = jnp.where(at < limit, code, plan.none)

        first[1].wait()
        rows = coef[...].reshape(2 * boxes, coef.shape[2])
        plain = jnp.dot(arrange(boxes, False), rows, preferred_element_type=F32).astype(BF16)
        turned = jnp.dot(arrange(boxes, True), rows, preferred_element_type=F32).astype(BF16)
        weights = jnp.concatenate([plain, turned], 0)

        first[2].wait()
        matrix = rad[...].reshape(2 * leaf_dirs, rad.shape[2])
        weights_t = jnp.transpose(weights)
        for a in range(0, 2 * leaf_dirs, half):
            z = min(a + half, 2 * leaf_dirs)
            both = jnp.dot(matrix[a:z], weights_t, preferred_element_type=F32)
            even[a:z, :] = both[:, 0:128]
            odd[a:z, :] = both[:, 128:256]
        leaf_t = even[pl.ds(0, leaf_dirs, stride=2), :] + odd[pl.ds(1, leaf_dirs, stride=2), :]
        leaf = jnp.transpose(leaf_t)[0 : 2 * boxes].astype(BF16)

        lane = lax.broadcasted_iota(jnp.int32, (parents_dev, 128), 1)
        words = plan.encode([codes[:, 128 * e : 128 * e + 128] for e in range(plan.entry_tiles)], lane)

        def put(w, row, stride, piece):
            for pair in range(plan.pairs):
                at_row = (plan.order.index(w) * plan.pairs + pair) * plan.rows + row
                send[pl.ds(at_row, piece.shape[0], stride=stride), :] = piece

        def pack(w):
            base = plan.dirs * w // 128 * 128
            shift = plan.dirs * w % 128
            span = -(-(shift + plan.dirs) // 128) * 128
            span = min(max(span, plan.width), parent_dirs - base)
            rests = []
            for part, buf in ((0, real_buf), (1, imag_buf)):
                value = buf[:, base : base + span]
                if shift:
                    value = pltpu.roll(value, span - shift, 1)
                for k in range(plan.full):
                    put(w, part * plan.full + k, 2 * plan.full, value[:, 128 * k : 128 * k + 128])
                if plan.rest:
                    piece = value[:, 128 * plan.full : plan.width]
                    rests.append(jnp.where(lane < plan.rest, piece, 0.0))
            if plan.rest and plan.shared:
                total = jnp.zeros((1, 128), F32)
                for p in range(parents_dev):
                    for part in range(2):
                        turn = plan.rest_at(p, part)[1]
                        piece = rests[part] if turn == 0 else pltpu.roll(rests[part], turn, 1)
                        total = total + piece[p : p + 1]
                put(w, plan.rest_row, 1, total)
            elif plan.rest:
                for part in range(2):
                    put(w, plan.rest_row + part, 2, rests[part])
            for e, word in enumerate(words):
                put(w, plan.list_row + e, plan.list_rows, word.astype(F32))

        packed = 0
        n_wide = plan.n_wide
        for c in range(n_chunks):
            copies[c].wait()
            cut = slice(cuts[c], cuts[c + 1])
            up = jnp.dot(leaf, interp[:, cut], preferred_element_type=F32)
            cs = cos_out[:, cut]
            sn = sin_out[:, cut]
            for p in range(parents_dev):
                up_real = up[8 * p : 8 * p + 8]
                up_imag = up[boxes + 8 * p : boxes + 8 * p + 8]
                real_buf[p : p + 1, cut] = jnp.sum(cs * up_real - sn * up_imag, 0, keepdims=True)
                imag_buf[p : p + 1, cut] = jnp.sum(cs * up_imag + sn * up_real, 0, keepdims=True)
            while packed < n_wide and -(-plan.dirs * (packed + 1) // 128) * 128 <= cuts[c + 1]:
                pack(packed)
                packed += 1

    return kernel


def translate_kernel(plan):
    own = plan.own
    targets = plan.n_wide * own
    group = max(1, min(targets, 1024 // plan.parents))
    step = min(256, plan.width)

    def kernel(table_in, received, out, table, tally, a_real, a_imag, keys, lows):
        mine = lax.axis_index("narrow")
        own_block = lax.rem(mine, plan.cores) * plan.peers + lax.div(mine, plan.cores)
        table[...] = jnp.zeros(table.shape, BF16)
        table[:, 0 : plan.dirs, 0 : plan.ops] = table_in[...].astype(BF16)
        highs = table.shape[2] // 128
        kind = BF16 if highs * plan.parents <= 256 else F32
        key_at = lax.broadcasted_iota(jnp.int32, (highs * plan.parents, 128), 0).astype(kind)
        low_at = lax.broadcasted_iota(jnp.int32, (128, 128), 0).astype(BF16)
        lane = lax.broadcasted_iota(jnp.int32, (targets, 128), 1)

        words = []
        for e in range(plan.list_rows):
            rows = [
                received[
                    pl.ds((own_block + i * plan.pairs) * plan.rows + plan.list_row + p * plan.list_rows + e, 1), :
                ]
                for i in range(plan.n_wide)
                for p in range(own)
            ]
            words.append(jnp.concatenate(rows, 0).astype(jnp.int32))
        for e, entry in enumerate(plan.decode(words, lane)):
            op = entry & ((1 << plan.bits) - 1)
            high = op >> 7
            keys[e] = jnp.where(high < highs, high * plan.parents + (entry >> plan.bits), -1)
            lows[e] = op & 127

        def pattern(part, k):
            pieces = []
            for p in range(own):
                if k < plan.full:
                    row, turn = (2 * p + part) * plan.full + k, 0
                else:
                    row, turn = plan.rest_at(p, part)
                piece = received[pl.ds(row, plan.devices, stride=plan.rows), :]
                pieces.append(pltpu.roll(piece, 128 - turn, 1) if turn else piece)
            return jnp.concatenate(pieces, 0)

        def do_group(first_target):
            for i in range(group):
                key_hits, low_hits = [], []
                for e in range(plan.entry_tiles):
                    key = keys[e, pl.ds(first_target + i, 1), :].astype(kind)
                    low = lows[e, pl.ds(first_target + i, 1), :].astype(BF16)
                    key_hits.append(jnp.where(key_at == key, jnp.ones((), kind), jnp.zeros((), kind)).astype(BF16))
                    low_hits.append(jnp.where(low_at == low, jnp.ones((), BF16), jnp.zeros((), BF16)))
                count_of = lax.dot_general(
                    jnp.concatenate(key_hits, 1), jnp.concatenate(low_hits, 1), NT, preferred_element_type=F32
                ).astype(BF16)
                rows = slice(i * plan.parents, (i + 1) * plan.parents)
                for h in range(highs):
                    tally[rows, 128 * h : 128 * h + 128] = count_of[h * plan.parents : (h + 1) * plan.parents]
            for j in range(plan.width // step):
                cut = slice(j * step, (j + 1) * step)
                for a in range(0, tally.shape[0], 512):
                    z = min(a + 512, tally.shape[0])
                    a_real[a:z, :] = lax.dot_general(tally[a:z, :], table[0, cut, :], NT, preferred_element_type=F32)
                    a_imag[a:z, :] = lax.dot_general(tally[a:z, :], table[1, cut, :], NT, preferred_element_type=F32)
                for q in range(step // 128):
                    k = j * (step // 128) + q
                    lanes = slice(128 * q, 128 * q + 128)
                    out_real = pattern(0, k)
                    out_imag = pattern(1, k)
                    for i in range(group):
                        rows = slice(i * plan.parents, (i + 1) * plan.parents)
                        op_real = a_real[rows, lanes]
                        op_imag = a_imag[rows, lanes]
                        real = jnp.sum(op_real * out_real - op_imag * out_imag, 0, keepdims=True)
                        imag = jnp.sum(op_real * out_imag + op_imag * out_real, 0, keepdims=True)
                        at = (first_target + i) * 2 * plan.tiles + k
                        out[pl.ds(at, 1), :] = real
                        out[pl.ds(at + plan.tiles, 1), :] = imag

        if targets == group:
            do_group(0)
        else:
            pl.loop(0, targets // group)(lambda g: do_group(g * group))

    return kernel, group, step


def downward_kernel(plan):
    def kernel(received, cosines, sines, interp, rad, product, inner, twin):
        parent_dirs = cosines.shape[1]
        leaf_dirs = rad.shape[0]
        parents_dev = product.shape[0] // 8
        boxes = product.shape[0]
        parts = 2 * parents_dev
        lane = lax.broadcasted_iota(jnp.int32, (parts, plan.width), 1)
        inner[...] = jnp.zeros(inner.shape, F32)
        for i, w in enumerate(plan.order):
            base = plan.dirs * w // 128 * 128
            shift = plan.dirs * w % 128
            span = -(-(shift + plan.dirs) // 128) * 128
            tiles = [
                received[pl.ds(i * parts * plan.tiles + k, parts, stride=plan.tiles), :]
                for k in range(plan.tiles)
            ]
            value = tiles[0] if plan.tiles == 1 else jnp.concatenate(tiles, 1)
            value = jnp.where(lane < plan.dirs, value, 0.0)
            if span > plan.width:
                value = jnp.concatenate([value, jnp.zeros((parts, span - plan.width), F32)], 1)
            if shift:
                value = pltpu.roll(value, shift, 1)
            span = min(value.shape[1], inner.shape[1] - base)
            inner[:, base : base + span] += value[:, 0:span]
        cs = cosines[...]
        sn = sines[...]
        reals, imags = [], []
        for p in range(parents_dev):
            in_real = inner[2 * p : 2 * p + 1, 0:parent_dirs]
            in_imag = inner[2 * p + 1 : 2 * p + 2, 0:parent_dirs]
            reals.append(cs * in_real + sn * in_imag)
            imags.append(cs * in_imag - sn * in_real)
        blank = jnp.zeros((128 - 2 * boxes, parent_dirs), F32)
        down = jnp.concatenate(
            reals + imags + [blank] + imags + [-r for r in reals] + [blank], 0
        ).astype(BF16)
        down_t = jnp.transpose(down)
        quarter = -(-leaf_dirs // 64) * 16
        got = jnp.concatenate(
            [
                jnp.dot(interp[a : min(a + quarter, leaf_dirs), :], down_t, preferred_element_type=F32)
                for a in range(0, leaf_dirs, quarter)
            ],
            0,
        )
        twin[pl.ds(0, leaf_dirs, stride=2), :] = got[:, 0:128]
        twin[pl.ds(1, leaf_dirs, stride=2), :] = got[:, 128:256]
        flat = jnp.transpose(twin[...])[0 : 2 * boxes].astype(BF16)
        matrix = rad[...].reshape(2 * leaf_dirs, rad.shape[2])
        result = jnp.dot(flat, matrix, preferred_element_type=F32)
        product[:, 0, :] = result[0:boxes]
        product[:, 1, :] = result[boxes : 2 * boxes]

    return kernel


def on_device(
    coefficients, radiation, interpolation, angles, translations, sources, operators, counts
):
    boxes = coefficients.shape[0]
    parents_dev = boxes // 8
    leaf_dirs, parent_dirs = interpolation.shape
    bases = coefficients.shape[2]
    n_wide = lax.axis_size("wide")
    n_narrow = lax.axis_size("narrow")
    dirs = translations.shape[2]
    n_ops = translations.shape[0]
    plan = Plan(parents_dev, n_wide, n_narrow, dirs, sources.shape[1], n_ops)
    rad = jnp.transpose(radiation, (2, 0, 1))
    table = jnp.transpose(translations, (1, 2, 0))
    cuts = [0, 1664]
    cuts = [c for c in cuts if c < parent_dirs] + [parent_dirs]
    vmem = pl.BlockSpec(memory_space=pltpu.VMEM)
    anywhere = pl.BlockSpec(memory_space=pl.ANY)

    send, cosines, sines = pl.pallas_call(
        upward_kernel(plan, cuts),
        out_shape=(
            jax.ShapeDtypeStruct((plan.peers * plan.rows, 128), F32),
            jax.ShapeDtypeStruct(angles.shape, F32),
            jax.ShapeDtypeStruct(angles.shape, F32),
        ),
        in_specs=[anywhere] * 7,
        out_specs=(vmem, vmem, vmem),
        scratch_shapes=[
            pltpu.SMEM((parents_dev,), jnp.int32),
            pltpu.VMEM((boxes, 2, bases), BF16),
            pltpu.VMEM((leaf_dirs, 2, bases), BF16),
            pltpu.VMEM((leaf_dirs, parent_dirs), BF16),
            pltpu.VMEM(angles.shape, F32),
            pltpu.VMEM(sources.shape, jnp.int32),
            pltpu.VMEM(operators.shape, jnp.int32),
            pltpu.VMEM((2 * leaf_dirs, 128), F32),
            pltpu.VMEM((2 * leaf_dirs, 128), F32),
            pltpu.VMEM((parents_dev, 128 * plan.entry_tiles), jnp.int32),
            pltpu.VMEM((parents_dev, parent_dirs), F32),
            pltpu.VMEM((parents_dev, parent_dirs), F32),
            pltpu.SemaphoreType.DMA((len(cuts) + 5,)),
        ],
        compiler_params=pltpu.CompilerParams(vmem_limit_bytes=56 * MIB),
        name="upward",
    )(counts, coefficients, rad, interpolation, angles, sources, operators)

    send = send.reshape(plan.peers, 1, plan.rows * 128)
    received = lax.all_to_all(
        send, ("wide", "narrow"), split_axis=0, concat_axis=0, tiled=True, axis_index_groups=plan.groups()
    ).reshape(-1, 128)
    if plan.cores > 1:
        together = [[pair * plan.cores + core for core in range(plan.cores)] for pair in range(plan.pairs)]
        received = lax.all_gather(received, "narrow", axis=0, tiled=True, axis_index_groups=together)

    body, group, step = translate_kernel(plan)
    op_lanes = -(-n_ops // 128) * 128
    incoming = pl.pallas_call(
        body,
        out_shape=jax.ShapeDtypeStruct((n_wide * parents_dev * 2 * plan.tiles, 128), F32),
        in_specs=[vmem, vmem],
        out_specs=vmem,
        scratch_shapes=[
            pltpu.VMEM((2, plan.width, op_lanes), BF16),
            pltpu.VMEM((group * plan.parents, op_lanes), BF16),
            pltpu.VMEM((group * plan.parents, step), F32),
            pltpu.VMEM((group * plan.parents, step), F32),
            pltpu.VMEM((plan.entry_tiles, n_wide * parents_dev, 128), jnp.int32),
            pltpu.VMEM((plan.entry_tiles, n_wide * parents_dev, 128), jnp.int32),
        ],
        compiler_params=pltpu.CompilerParams(vmem_limit_bytes=24 * MIB),
        name="translate",
    )(table, received)

    incoming = incoming.reshape(n_wide, parents_dev * 2 * plan.tiles, 128)
    back = lax.all_to_all(
        incoming, "wide", split_axis=0, concat_axis=0, tiled=True, axis_index_groups=[plan.order]
    )
    back = back.reshape(-1, 128)

    return pl.pallas_call(
        downward_kernel(plan),
        out_shape=jax.ShapeDtypeStruct((boxes, 2, bases), F32),
        in_specs=[vmem] * 5,
        out_specs=vmem,
        scratch_shapes=[
            pltpu.VMEM((2 * parents_dev, parent_dirs + 128), F32),
            pltpu.VMEM((2 * leaf_dirs, 128), F32),
        ],
        compiler_params=pltpu.CompilerParams(vmem_limit_bytes=32 * MIB),
        name="downward",
    )(back, cosines, sines, interpolation, rad)


def solution(mesh):
    in_specs = (
        P(("wide", "narrow"), None, None),
        P(),
        P(),
        P(),
        P(None, None, "wide"),
        P(("wide", "narrow"), None),
        P(("wide", "narrow"), None),
        P(("wide", "narrow")),
    )
    out_specs = P(("wide", "narrow"), None, None)
    return jax.shard_map(
        on_device, mesh=mesh, in_specs=in_specs, out_specs=out_specs, check_vma=False
    )
```

```python
import jax
import jax.numpy as jnp
from jax import lax
from jax.experimental import pallas as pl
from jax.experimental.pallas import tpu as pltpu
from jax.sharding import PartitionSpec as P

F32 = jnp.float32
BF16 = jnp.bfloat16
MIB = 2**20
NT = (((1,), (1,)), ((), ()))


class Plan:
    def __init__(self, own, n_wide, n_narrow, dirs, length, ops):
        self.own = own
        self.n_wide = n_wide
        self.n_narrow = n_narrow
        self.devices = n_wide * n_narrow
        self.parents = own * self.devices
        first = n_wide * 5 // 8
        self.order = list(range(first, -1, -1)) + list(range(first + 1, n_wide))
        self.cores = 2 if n_narrow % 2 == 0 else 1
        self.pairs = n_narrow // self.cores
        self.peers = n_wide * self.pairs
        self.dirs = dirs
        self.length = length
        self.ops = ops
        self.full = dirs // 128
        self.rest = dirs % 128
        self.tiles = -(-dirs // 128)
        self.width = 128 * self.tiles
        self.bits = ops.bit_length()
        entry_bits = self.bits + (self.parents - 1).bit_length()
        self.none = (1 << entry_bits) - 1
        self.rest_row = own * 2 * self.full
        self.shared = 2 * own * self.rest <= 128
        rest_rows = 0 if not self.rest else 1 if self.shared else 2 * own
        self.list_row = self.rest_row + rest_rows
        self.dense = entry_bits <= 15 and length <= 192
        self.entry_tiles = 2 if self.dense else -(-length // 128)
        self.list_rows = 1 if self.dense else self.entry_tiles
        self.rows = self.list_row + own * self.list_rows

    def rest_at(self, p, part):
        if self.shared:
            return self.rest_row, (2 * p + part) * self.rest
        return self.rest_row + 2 * p + part, 0

    def groups(self):
        return [
            [w * self.n_narrow + pair * self.cores + core for w in self.order for pair in range(self.pairs)]
            for core in range(self.cores)
        ]

    def place(self, source):
        narrow_shift = self.own.bit_length() - 1
        device = source >> narrow_shift
        place = jnp.zeros(source.shape, jnp.int32)
        for i, w in enumerate(self.order):
            for pair in range(self.pairs):
                for core in range(self.cores):
                    flat = w * self.n_narrow + pair * self.cores + core
                    block = core * self.peers + i * self.pairs + pair
                    place = jnp.where(device == flat, block, place)
        return (source & (self.own - 1)) * self.devices + place

    def encode(self, entries, lane):
        if not self.dense:
            return entries
        first, third = entries
        low = jnp.where(lane < 64, third & 255, pltpu.roll(third, 64, 1) >> 8)
        return [first * 256 + low]

    def decode(self, words, lane):
        if not self.dense:
            return words
        low = words[0] & 255
        third = low + (pltpu.roll(low, 64, 1) << 8)
        return [words[0] >> 8, jnp.where(lane < 64, third, self.none)]


def sin_cos(angle):
    turns = jnp.floor(angle * 0.6366197723675814 + 0.5)
    quarter = turns.astype(jnp.int32)
    rest = angle - turns * 1.5703125
    rest = rest - turns * 4.837512969970703e-4
    rest = rest - turns * 7.54978995489188e-8
    square = rest * rest
    sine = ((-1.9515295891e-4 * square + 8.3321608736e-3) * square - 1.6666654611e-1) * square * rest + rest
    cosine = ((2.443315711809948e-5 * square - 1.388731625493765e-3) * square + 4.166664568298827e-2) * (
        square * square
    ) - 0.5 * square + 1.0
    swap = (quarter & 1) == 1
    sin_value = jnp.where(swap, cosine, sine)
    cos_value = jnp.where(swap, sine, cosine)
    sin_value = jnp.where((quarter & 2) == 2, -sin_value, sin_value)
    cos_value = jnp.where(((quarter + 1) & 2) == 2, -cos_value, cos_value)
    return sin_value, cos_value


def arrange(boxes, swapped):
    row = lax.broadcasted_iota(jnp.int32, (128, 2 * boxes), 0)
    column = lax.broadcasted_iota(jnp.int32, (128, 2 * boxes), 1)
    real_at = 2 * row
    imag_at = 2 * (row - boxes) + 1
    if swapped:
        first = jnp.where((row < boxes) & (column == real_at + 1), -1.0, 0.0)
        second = jnp.where((row >= boxes) & (row < 2 * boxes) & (column == imag_at - 1), 1.0, 0.0)
    else:
        first = jnp.where((row < boxes) & (column == real_at), 1.0, 0.0)
        second = jnp.where((row >= boxes) & (row < 2 * boxes) & (column == imag_at), 1.0, 0.0)
    return (first + second).astype(BF16)


def upward_kernel(plan, cuts):
    def kernel(
        counts_hbm, coef_hbm, rad_hbm, interp_hbm, angles_hbm, sources_hbm, operators_hbm,
        send,
        counts, coef, rad, interp, angles, sources, operators, cos_out, sin_out,
        even, odd, codes, real_buf, imag_buf, sems,
    ):
        parent_dirs = angles.shape[1]
        leaf_dirs = rad.shape[0]
        boxes = coef.shape[0]
        parents_dev = boxes // 8
        n_chunks = len(cuts) - 1
        half = -(-leaf_dirs // 16) * 16
        first = []
        for source, target in (
            (angles_hbm, angles),
            (coef_hbm, coef),
            (rad_hbm, rad),
            (sources_hbm, sources),
            (operators_hbm, operators),
            (counts_hbm, counts),
        ):
            first.append(pltpu.make_async_copy(source, target, sems.at[n_chunks + len(first)]))
            first[-1].start()
        copies = []
        for c in range(n_chunks):
            cut = (slice(None), pl.ds(cuts[c], cuts[c + 1] - cuts[c]))
            copies.append(pltpu.make_async_copy(interp_hbm.at[cut], interp.at[cut], sems.at[c]))
            copies[-1].start()

        first[0].wait()
        sines, cosines = sin_cos(angles[...])
        sin_out[...] = sines
        cos_out[...] = cosines

        for copy in first[3:]:
            copy.wait()
        code = plan.place(sources[...]) * (1 << plan.bits) + operators[...]
        at = lax.broadcasted_iota(jnp.int32, code.shape, 1)
        parent = lax.broadcasted_iota(jnp.int32, code.shape, 0)
        limit = jnp.zeros(code.shape, jnp.int32)
        for p in range(parents_dev):
            limit = jnp.where(parent == p, counts[p], limit)
        codes[...] = jnp.full(codes.shape, plan.none, jnp.int32)
        codes[:, 0 : plan.length] = jnp.where(at < limit, code, plan.none)

        first[1].wait()
        rows = coef[...].reshape(2 * boxes, coef.shape[2])
        plain = jnp.dot(arrange(boxes, False), rows, preferred_element_type=F32).astype(BF16)
        turned = jnp.dot(arrange(boxes, True), rows, preferred_element_type=F32).astype(BF16)
        weights = jnp.concatenate([plain, turned], 0)

        first[2].wait()
        matrix = rad[...].reshape(2 * leaf_dirs, rad.shape[2])
        weights_t = jnp.transpose(weights)
        for a in range(0, 2 * leaf_dirs, half):
            z = min(a + half, 2 * leaf_dirs)
            both = jnp.dot(matrix[a:z], weights_t, preferred_element_type=F32)
            even[a:z, :] = both[:, 0:128]
            odd[a:z, :] = both[:, 128:256]
        leaf_t = even[pl.ds(0, leaf_dirs, stride=2), :] + odd[pl.ds(1, leaf_dirs, stride=2), :]
        leaf = jnp.transpose(leaf_t)[0 : 2 * boxes].astype(BF16)

        lane = lax.broadcasted_iota(jnp.int32, (parents_dev, 128), 1)
        words = plan.encode([codes[:, 128 * e : 128 * e + 128] for e in range(plan.entry_tiles)], lane)

        def put(w, row, stride, piece):
            for pair in range(plan.pairs):
                at_row = (plan.order.index(w) * plan.pairs + pair) * plan.rows + row
                send[pl.ds(at_row, piece.shape[0], stride=stride), :] = piece

        def pack(w):
            base = plan.dirs * w // 128 * 128
            shift = plan.dirs * w % 128
            span = -(-(shift + plan.dirs) // 128) * 128
            span = min(max(span, plan.width), parent_dirs - base)
            rests = []
            for part, buf in ((0, real_buf), (1, imag_buf)):
                value = buf[:, base : base + span]
                if shift:
                    value = pltpu.roll(value, span - shift, 1)
                for k in range(plan.full):
                    put(w, part * plan.full + k, 2 * plan.full, value[:, 128 * k : 128 * k + 128])
                if plan.rest:
                    piece = value[:, 128 * plan.full : plan.width]
                    rests.append(jnp.where(lane < plan.rest, piece, 0.0))
            if plan.rest and plan.shared:
                total = jnp.zeros((1, 128), F32)
                for p in range(parents_dev):
                    for part in range(2):
                        turn = plan.rest_at(p, part)[1]
                        piece = rests[part] if turn == 0 else pltpu.roll(rests[part], turn, 1)
                        total = total + piece[p : p + 1]
                put(w, plan.rest_row, 1, total)
            elif plan.rest:
                for part in range(2):
                    put(w, plan.rest_row + part, 2, rests[part])
            for e, word in enumerate(words):
                put(w, plan.list_row + e, plan.list_rows, word.astype(F32))

        packed = 0
        n_wide = plan.n_wide
        for c in range(n_chunks):
            copies[c].wait()
            cut = slice(cuts[c], cuts[c + 1])
            up = jnp.dot(leaf, interp[:, cut], preferred_element_type=F32)
            cs = cos_out[:, cut]
            sn = sin_out[:, cut]
            for p in range(parents_dev):
                up_real = up[8 * p : 8 * p + 8]
                up_imag = up[boxes + 8 * p : boxes + 8 * p + 8]
                real_buf[p : p + 1, cut] = jnp.sum(cs * up_real - sn * up_imag, 0, keepdims=True)
                imag_buf[p : p + 1, cut] = jnp.sum(cs * up_imag + sn * up_real, 0, keepdims=True)
            while packed < n_wide and -(-plan.dirs * (packed + 1) // 128) * 128 <= cuts[c + 1]:
                pack(packed)
                packed += 1

    return kernel


class Tally:
    def __init__(self, plan):
        self.plan = plan
        self.targets = plan.n_wide * plan.own
        self.group = max(1, min(self.targets, 1024 // plan.parents))
        self.highs = -(-plan.ops // 128)
        self.rows = self.group * plan.parents
        self.shape = (self.rows, 128 * self.highs)
        lists = pltpu.VMEM((plan.entry_tiles, self.targets, 128), jnp.int32)
        self.scratch = [lists, lists]

    def read(self, received, keys, lows):
        plan = self.plan
        mine = lax.axis_index("narrow")
        own_block = lax.div(mine, plan.cores)
        flip = lax.rem(mine, plan.cores) * plan.peers
        lane = lax.broadcasted_iota(jnp.int32, (self.targets, 128), 1)
        words = []
        for e in range(plan.list_rows):
            rows = [
                received[
                    pl.ds((own_block + i * plan.pairs) * plan.rows + plan.list_row + p * plan.list_rows + e, 1), :
                ]
                for i in range(plan.n_wide)
                for p in range(plan.own)
            ]
            words.append(jnp.concatenate(rows, 0).astype(jnp.int32))
        for e, entry in enumerate(plan.decode(words, lane)):
            op = entry & ((1 << plan.bits) - 1)
            high = op >> 7
            keys[e] = jnp.where(high < self.highs, high * plan.parents + ((entry >> plan.bits) ^ flip), -1)
            lows[e] = op & 127

    def count(self, first_target, keys, lows, tally):
        plan = self.plan
        kind = BF16 if self.highs * plan.parents <= 256 else F32
        key_at = lax.broadcasted_iota(jnp.int32, (self.highs * plan.parents, 128), 0).astype(kind)
        low_at = lax.broadcasted_iota(jnp.int32, (128, 128), 0).astype(BF16)
        for i in range(self.group):
            key_hits, low_hits = [], []
            for e in range(plan.entry_tiles):
                key = keys[e, pl.ds(first_target + i, 1), :].astype(kind)
                low = lows[e, pl.ds(first_target + i, 1), :].astype(BF16)
                key_hits.append(jnp.where(key_at == key, jnp.ones((), kind), jnp.zeros((), kind)).astype(BF16))
                low_hits.append(jnp.where(low_at == low, jnp.ones((), BF16), jnp.zeros((), BF16)))
            count_of = lax.dot_general(
                jnp.concatenate(key_hits, 1), jnp.concatenate(low_hits, 1), NT, preferred_element_type=F32
            ).astype(BF16)
            rows = slice(i * plan.parents, (i + 1) * plan.parents)
            for h in range(self.highs):
                tally[rows, 128 * h : 128 * h + 128] = count_of[h * plan.parents : (h + 1) * plan.parents]

    def sum_operators(self, tally, table, a_real, a_imag):
        for a in range(0, self.rows, 512):
            z = min(a + 512, self.rows)
            a_real[a:z, :] = lax.dot_general(tally[a:z, :], table[0], NT, preferred_element_type=F32)
            a_imag[a:z, :] = lax.dot_general(tally[a:z, :], table[1], NT, preferred_element_type=F32)

    def fill(self, table_in, table):
        table[...] = jnp.zeros(table.shape, BF16)
        table[:, 0 : self.plan.dirs, 0 : self.plan.ops] = table_in[...].astype(BF16)

    def kernel(self, table_in, received, a_real, a_imag, table, tally, keys, lows):
        self.read(received, keys, lows)
        self.count(0, keys, lows, tally)
        self.fill(table_in, table)
        self.sum_operators(tally, table, a_real, a_imag)


def translate_kernel(plan, tallies, ready):
    group = tallies.group

    def kernel(*refs):
        if ready:
            a_real, a_imag, *refs = refs
            blocks = refs[: plan.cores]
            (out,) = refs[plan.cores :]
        else:
            table_in, *refs = refs
            blocks = refs[: plan.cores]
            out, a_real, a_imag, table, tally, keys, lows = refs[plan.cores :]
            tallies.read(blocks[0], keys, lows)
            tallies.fill(table_in, table)

        def pattern(part, k):
            pieces = []
            for p in range(plan.own):
                if k < plan.full:
                    row, turn = (2 * p + part) * plan.full + k, 0
                else:
                    row, turn = plan.rest_at(p, part)
                for block in blocks:
                    piece = block[pl.ds(row, plan.peers, stride=plan.rows), :]
                    pieces.append(pltpu.roll(piece, 128 - turn, 1) if turn else piece)
            return jnp.concatenate(pieces, 0)

        def do_group(first_target):
            if not ready:
                tallies.count(first_target, keys, lows, tally)
                tallies.sum_operators(tally, table, a_real, a_imag)
            for k in range(plan.tiles):
                lanes = slice(128 * k, 128 * k + 128)
                out_real = pattern(0, k)
                out_imag = pattern(1, k)
                for i in range(group):
                    rows = slice(i * plan.parents, (i + 1) * plan.parents)
                    op_real = a_real[rows, lanes]
                    op_imag = a_imag[rows, lanes]
                    real = jnp.sum(op_real * out_real - op_imag * out_imag, 0, keepdims=True)
                    imag = jnp.sum(op_real * out_imag + op_imag * out_real, 0, keepdims=True)
                    at = (first_target + i) * 2 * plan.tiles + k
                    out[pl.ds(at, 1), :] = real
                    out[pl.ds(at + plan.tiles, 1), :] = imag

        if ready:
            do_group(0)
        else:
            pl.loop(0, tallies.targets // group)(lambda g: do_group(g * group))

    return kernel


def downward_kernel(plan):
    def kernel(received, angles, interp, rad, product, inner, twin):
        parent_dirs = angles.shape[1]
        leaf_dirs = rad.shape[0]
        parents_dev = product.shape[0] // 8
        boxes = product.shape[0]
        parts = 2 * parents_dev
        lane = lax.broadcasted_iota(jnp.int32, (parts, plan.width), 1)
        inner[...] = jnp.zeros(inner.shape, F32)
        for i, w in enumerate(plan.order):
            base = plan.dirs * w // 128 * 128
            shift = plan.dirs * w % 128
            span = -(-(shift + plan.dirs) // 128) * 128
            tiles = [
                received[pl.ds(i * parts * plan.tiles + k, parts, stride=plan.tiles), :]
                for k in range(plan.tiles)
            ]
            value = tiles[0] if plan.tiles == 1 else jnp.concatenate(tiles, 1)
            value = jnp.where(lane < plan.dirs, value, 0.0)
            if span > plan.width:
                value = jnp.concatenate([value, jnp.zeros((parts, span - plan.width), F32)], 1)
            if shift:
                value = pltpu.roll(value, shift, 1)
            span = min(value.shape[1], inner.shape[1] - base)
            inner[:, base : base + span] += value[:, 0:span]
        sn, cs = sin_cos(angles[...])
        reals, imags = [], []
        for p in range(parents_dev):
            in_real = inner[2 * p : 2 * p + 1, 0:parent_dirs]
            in_imag = inner[2 * p + 1 : 2 * p + 2, 0:parent_dirs]
            reals.append(cs * in_real + sn * in_imag)
            imags.append(cs * in_imag - sn * in_real)
        blank = jnp.zeros((128 - 2 * boxes, parent_dirs), F32)
        down = jnp.concatenate(
            reals + imags + [blank] + imags + [-r for r in reals] + [blank], 0
        ).astype(BF16)
        down_t = jnp.transpose(down)
        quarter = -(-leaf_dirs // 64) * 16
        got = jnp.concatenate(
            [
                jnp.dot(interp[a : min(a + quarter, leaf_dirs), :], down_t, preferred_element_type=F32)
                for a in range(0, leaf_dirs, quarter)
            ],
            0,
        )
        twin[pl.ds(0, leaf_dirs, stride=2), :] = got[:, 0:128]
        twin[pl.ds(1, leaf_dirs, stride=2), :] = got[:, 128:256]
        flat = jnp.transpose(twin[...])[0 : 2 * boxes].astype(BF16)
        matrix = rad[...].reshape(2 * leaf_dirs, rad.shape[2])
        result = jnp.dot(flat, matrix, preferred_element_type=F32)
        product[:, 0, :] = result[0:boxes]
        product[:, 1, :] = result[boxes : 2 * boxes]

    return kernel


def on_device(
    coefficients, radiation, interpolation, angles, translations, sources, operators, counts
):
    boxes = coefficients.shape[0]
    parents_dev = boxes // 8
    leaf_dirs, parent_dirs = interpolation.shape
    bases = coefficients.shape[2]
    n_wide = lax.axis_size("wide")
    n_narrow = lax.axis_size("narrow")
    dirs = translations.shape[2]
    n_ops = translations.shape[0]
    plan = Plan(parents_dev, n_wide, n_narrow, dirs, sources.shape[1], n_ops)
    rad = jnp.transpose(radiation, (2, 0, 1))
    table = jnp.transpose(translations, (1, 2, 0))
    cuts = [0, 1664]
    cuts = [c for c in cuts if c < parent_dirs] + [parent_dirs]
    vmem = pl.BlockSpec(memory_space=pltpu.VMEM)
    anywhere = pl.BlockSpec(memory_space=pl.ANY)

    send = pl.pallas_call(
        upward_kernel(plan, cuts),
        out_shape=jax.ShapeDtypeStruct((plan.peers * plan.rows, 128), F32),
        in_specs=[anywhere] * 7,
        out_specs=vmem,
        scratch_shapes=[
            pltpu.SMEM((parents_dev,), jnp.int32),
            pltpu.VMEM((boxes, 2, bases), BF16),
            pltpu.VMEM((leaf_dirs, 2, bases), BF16),
            pltpu.VMEM((leaf_dirs, parent_dirs), BF16),
            pltpu.VMEM(angles.shape, F32),
            pltpu.VMEM(sources.shape, jnp.int32),
            pltpu.VMEM(operators.shape, jnp.int32),
            pltpu.VMEM(angles.shape, F32),
            pltpu.VMEM(angles.shape, F32),
            pltpu.VMEM((2 * leaf_dirs, 128), F32),
            pltpu.VMEM((2 * leaf_dirs, 128), F32),
            pltpu.VMEM((parents_dev, 128 * plan.entry_tiles), jnp.int32),
            pltpu.VMEM((parents_dev, parent_dirs), F32),
            pltpu.VMEM((parents_dev, parent_dirs), F32),
            pltpu.SemaphoreType.DMA((len(cuts) + 5,)),
        ],
        compiler_params=pltpu.CompilerParams(vmem_limit_bytes=56 * MIB),
        name="upward",
    )(counts, coefficients, rad, interpolation, angles, sources, operators)

    send = send.reshape(plan.peers, 1, plan.rows * 128)
    received = lax.all_to_all(
        send, ("wide", "narrow"), split_axis=0, concat_axis=0, tiled=True, axis_index_groups=plan.groups()
    ).reshape(-1, 128)
    blocks = [received]
    if plan.cores > 1:
        blocks.append(lax.ppermute(received, "narrow", [(i, i ^ 1) for i in range(n_narrow)]))

    tallies = Tally(plan)
    ready = tallies.targets == tallies.group
    sums = jax.ShapeDtypeStruct((tallies.rows, plan.width), F32)
    scratch = [pltpu.VMEM((2, plan.width, tallies.shape[1]), BF16), pltpu.VMEM(tallies.shape, BF16)] + tallies.scratch
    if ready:
        operands = pl.pallas_call(
            tallies.kernel,
            out_shape=(sums, sums),
            in_specs=[vmem, vmem],
            out_specs=(vmem, vmem),
            scratch_shapes=scratch,
            cost_estimate=pl.CostEstimate(flops=10**9, bytes_accessed=10**6, transcendentals=0),
            compiler_params=pltpu.CompilerParams(vmem_limit_bytes=16 * MIB),
            name="operators",
        )(table, received)
        scratch = []
    else:
        operands = [table]
        scratch = [pltpu.VMEM(sums.shape, F32), pltpu.VMEM(sums.shape, F32)] + scratch
    operands = [*operands, *blocks]
    incoming = pl.pallas_call(
        translate_kernel(plan, tallies, ready),
        out_shape=jax.ShapeDtypeStruct((n_wide * parents_dev * 2 * plan.tiles, 128), F32),
        in_specs=[vmem] * len(operands),
        out_specs=vmem,
        scratch_shapes=scratch,
        compiler_params=pltpu.CompilerParams(vmem_limit_bytes=24 * MIB),
        name="translate",
    )(*operands)

    incoming = incoming.reshape(n_wide, parents_dev * 2 * plan.tiles, 128)
    back = lax.all_to_all(
        incoming, "wide", split_axis=0, concat_axis=0, tiled=True, axis_index_groups=[plan.order]
    )
    back = back.reshape(-1, 128)

    return pl.pallas_call(
        downward_kernel(plan),
        out_shape=jax.ShapeDtypeStruct((boxes, 2, bases), F32),
        in_specs=[vmem] * 4,
        out_specs=vmem,
        scratch_shapes=[
            pltpu.VMEM((2 * parents_dev, parent_dirs + 128), F32),
            pltpu.VMEM((2 * leaf_dirs, 128), F32),
        ],
        compiler_params=pltpu.CompilerParams(vmem_limit_bytes=32 * MIB),
        name="downward",
    )(back, angles, interpolation, rad)


def solution(mesh):
    in_specs = (
        P(("wide", "narrow"), None, None),
        P(),
        P(),
        P(),
        P(None, None, "wide"),
        P(("wide", "narrow"), None),
        P(("wide", "narrow"), None),
        P(("wide", "narrow")),
    )
    out_specs = P(("wide", "narrow"), None, None)
    return jax.shard_map(
        on_device, mesh=mesh, in_specs=in_specs, out_specs=out_specs, check_vma=False
    )
```

```python
import jax
import jax.numpy as jnp
from jax import lax
from jax.experimental import pallas as pl
from jax.experimental.pallas import tpu as pltpu
from jax.sharding import PartitionSpec as P

F32 = jnp.float32
BF16 = jnp.bfloat16
MIB = 2**20
NT = (((1,), (1,)), ((), ()))


class Plan:
    def __init__(self, own, n_wide, n_narrow, dirs, length, ops):
        self.own = own
        self.n_wide = n_wide
        self.n_narrow = n_narrow
        self.devices = n_wide * n_narrow
        self.parents = own * self.devices
        first = n_wide * 5 // 8
        self.order = list(range(first, -1, -1)) + list(range(first + 1, n_wide))
        self.cores = 2 if n_narrow % 2 == 0 else 1
        self.pairs = n_narrow // self.cores
        self.peers = n_wide * self.pairs
        self.dirs = dirs
        self.length = length
        self.ops = ops
        self.full = dirs // 128
        self.rest = dirs % 128
        self.tiles = -(-dirs // 128)
        self.width = 128 * self.tiles
        self.bits = ops.bit_length()
        entry_bits = self.bits + (self.parents - 1).bit_length()
        self.none = (1 << entry_bits) - 1
        self.rest_row = own * 2 * self.full
        self.shared = 2 * own * self.rest <= 128
        rest_rows = 0 if not self.rest else 1 if self.shared else 2 * own
        self.list_row = self.rest_row + rest_rows
        self.dense = entry_bits <= 15 and length <= 192
        self.entry_tiles = 2 if self.dense else -(-length // 128)
        self.list_rows = 1 if self.dense else self.entry_tiles
        self.rows = self.list_row + own * self.list_rows

    def rest_at(self, p, part):
        if self.shared:
            return self.rest_row, (2 * p + part) * self.rest
        return self.rest_row + 2 * p + part, 0

    def swap(self, w, pair):
        return w // (self.n_wide // 2) if self.cores > 1 else 0

    def device(self, w, pair, label):
        return w * self.n_narrow + pair * self.cores + (label ^ self.swap(w, pair))

    def groups(self):
        return [
            [self.device(w, pair, label) for w in self.order for pair in range(self.pairs)]
            for label in range(self.cores)
        ]

    def wide_groups(self):
        return [
            [self.device(w, pair, label) for w in self.order]
            for pair in range(self.pairs)
            for label in range(self.cores)
        ]

    def place(self, source):
        narrow_shift = self.own.bit_length() - 1
        device = source >> narrow_shift
        place = jnp.zeros(source.shape, jnp.int32)
        for i, w in enumerate(self.order):
            for pair in range(self.pairs):
                for label in range(self.cores):
                    block = label * self.peers + i * self.pairs + pair
                    place = jnp.where(device == self.device(w, pair, label), block, place)
        return (source & (self.own - 1)) * self.devices + place

    def encode(self, entries, lane):
        if not self.dense:
            return entries
        first, third = entries
        low = jnp.where(lane < 64, third & 255, pltpu.roll(third, 64, 1) >> 8)
        return [first * 256 + low]

    def decode(self, words, lane):
        if not self.dense:
            return words
        low = words[0] & 255
        third = low + (pltpu.roll(low, 64, 1) << 8)
        return [words[0] >> 8, jnp.where(lane < 64, third, self.none)]


def sin_cos(angle):
    turns = jnp.floor(angle * 0.6366197723675814 + 0.5)
    quarter = turns.astype(jnp.int32)
    rest = angle - turns * 1.5703125
    rest = rest - turns * 4.837512969970703e-4
    rest = rest - turns * 7.54978995489188e-8
    square = rest * rest
    sine = ((-1.9515295891e-4 * square + 8.3321608736e-3) * square - 1.6666654611e-1) * square * rest + rest
    cosine = ((2.443315711809948e-5 * square - 1.388731625493765e-3) * square + 4.166664568298827e-2) * (
        square * square
    ) - 0.5 * square + 1.0
    swap = (quarter & 1) == 1
    sin_value = jnp.where(swap, cosine, sine)
    cos_value = jnp.where(swap, sine, cosine)
    sin_value = jnp.where((quarter & 2) == 2, -sin_value, sin_value)
    cos_value = jnp.where(((quarter + 1) & 2) == 2, -cos_value, cos_value)
    return sin_value, cos_value


def arrange(boxes, swapped):
    row = lax.broadcasted_iota(jnp.int32, (128, 2 * boxes), 0)
    column = lax.broadcasted_iota(jnp.int32, (128, 2 * boxes), 1)
    real_at = 2 * row
    imag_at = 2 * (row - boxes) + 1
    if swapped:
        first = jnp.where((row < boxes) & (column == real_at + 1), -1.0, 0.0)
        second = jnp.where((row >= boxes) & (row < 2 * boxes) & (column == imag_at - 1), 1.0, 0.0)
    else:
        first = jnp.where((row < boxes) & (column == real_at), 1.0, 0.0)
        second = jnp.where((row >= boxes) & (row < 2 * boxes) & (column == imag_at), 1.0, 0.0)
    return (first + second).astype(BF16)


def upward_kernel(plan, cuts):
    def kernel(
        counts_hbm, coef_hbm, rad_hbm, interp_hbm, angles_hbm, sources_hbm, operators_hbm,
        send,
        counts, coef, rad, interp, angles, sources, operators, cos_out, sin_out,
        even, odd, codes, out_buf, sems,
    ):
        parent_dirs = angles.shape[1]
        leaf_dirs = rad.shape[0]
        boxes = coef.shape[0]
        parents_dev = boxes // 8
        n_chunks = len(cuts) - 1
        half = -(-leaf_dirs // 16) * 16
        first = []
        for source, target in (
            (angles_hbm, angles),
            (coef_hbm, coef),
            (rad_hbm, rad),
            (sources_hbm, sources),
            (operators_hbm, operators),
            (counts_hbm, counts),
        ):
            first.append(pltpu.make_async_copy(source, target, sems.at[n_chunks + len(first)]))
            first[-1].start()
        copies = []
        for c in range(n_chunks):
            cut = (slice(None), pl.ds(cuts[c], cuts[c + 1] - cuts[c]))
            copies.append(pltpu.make_async_copy(interp_hbm.at[cut], interp.at[cut], sems.at[c]))
            copies[-1].start()

        first[0].wait()
        sines, cosines = sin_cos(angles[...])
        sin_out[...] = sines
        cos_out[...] = cosines

        for copy in first[3:]:
            copy.wait()
        code = plan.place(sources[...]) * (1 << plan.bits) + operators[...]
        at = lax.broadcasted_iota(jnp.int32, code.shape, 1)
        parent = lax.broadcasted_iota(jnp.int32, code.shape, 0)
        limit = jnp.zeros(code.shape, jnp.int32)
        for p in range(parents_dev):
            limit = jnp.where(parent == p, counts[p], limit)
        codes[...] = jnp.full(codes.shape, plan.none, jnp.int32)
        codes[:, 0 : plan.length] = jnp.where(at < limit, code, plan.none)

        first[1].wait()
        rows = coef[...].reshape(2 * boxes, coef.shape[2])
        plain = jnp.dot(arrange(boxes, False), rows, preferred_element_type=F32).astype(BF16)
        turned = jnp.dot(arrange(boxes, True), rows, preferred_element_type=F32).astype(BF16)
        weights = jnp.concatenate([plain, turned], 0)

        first[2].wait()
        matrix = rad[...].reshape(2 * leaf_dirs, rad.shape[2])
        weights_t = jnp.transpose(weights)
        for a in range(0, 2 * leaf_dirs, half):
            z = min(a + half, 2 * leaf_dirs)
            both = jnp.dot(matrix[a:z], weights_t, preferred_element_type=F32)
            even[a:z, :] = both[:, 0:128]
            odd[a:z, :] = both[:, 128:256]
        leaf_t = even[pl.ds(0, leaf_dirs, stride=2), :] + odd[pl.ds(1, leaf_dirs, stride=2), :]
        leaf = jnp.transpose(leaf_t)[0 : 2 * boxes].astype(BF16)

        lane = lax.broadcasted_iota(jnp.int32, (parents_dev, 128), 1)
        words = plan.encode([codes[:, 128 * e : 128 * e + 128] for e in range(plan.entry_tiles)], lane)

        def put(w, row, stride, piece):
            for pair in range(plan.pairs):
                at_row = (plan.order.index(w) * plan.pairs + pair) * plan.rows + row
                send[pl.ds(at_row, piece.shape[0], stride=stride), :] = piece

        for w in range(plan.n_wide):
            for e, word in enumerate(words):
                put(w, plan.list_row + e, plan.list_rows, word.astype(F32))

        wide_lane = lax.broadcasted_iota(jnp.int32, (2 * parents_dev, 128), 1)

        def pack(w):
            base = plan.dirs * w // 128 * 128
            shift = plan.dirs * w % 128
            span = -(-(shift + plan.dirs) // 128) * 128
            span = min(max(span, plan.width), parent_dirs - base)
            value = out_buf[:, base : base + span]
            if shift:
                value = pltpu.roll(value, span - shift, 1)
            for k in range(plan.full):
                put(w, k, plan.full, value[:, 128 * k : 128 * k + 128])
            if plan.rest:
                piece = jnp.where(wide_lane < plan.rest, value[:, 128 * plan.full : plan.width], 0.0)
                if plan.shared:
                    piece = sum(
                        pltpu.roll(piece[r : r + 1], plan.rest * r, 1) if r else piece[0:1]
                        for r in range(2 * parents_dev)
                    )
                put(w, plan.rest_row, 1, piece)

        n_wide = plan.n_wide
        ups = []
        for c in range(n_chunks):
            copies[c].wait()
            ups.append(jnp.dot(leaf, interp[:, cuts[c] : cuts[c + 1]], preferred_element_type=F32))
        for c in range(n_chunks):
            cut = slice(cuts[c], cuts[c + 1])
            up = ups[c]
            cs = cos_out[:, cut]
            sn = sin_out[:, cut]
            for p in range(parents_dev):
                up_real = up[8 * p : 8 * p + 8]
                up_imag = up[boxes + 8 * p : boxes + 8 * p + 8]
                out_buf[2 * p : 2 * p + 1, cut] = jnp.sum(cs * up_real - sn * up_imag, 0, keepdims=True)
                out_buf[2 * p + 1 : 2 * p + 2, cut] = jnp.sum(cs * up_imag + sn * up_real, 0, keepdims=True)
        for w in range(n_wide):
            pack(w)

    return kernel


class Tally:
    def __init__(self, plan):
        self.plan = plan
        self.targets = plan.n_wide * plan.own
        self.group = max(1, min(self.targets, 1024 // plan.parents))
        self.highs = -(-plan.ops // 128)
        self.rows = self.group * plan.parents
        self.shape = (self.rows, 128 * self.highs)
        lists = pltpu.VMEM((plan.entry_tiles, self.targets, 128), jnp.int32)
        self.scratch = [lists, lists]

    def read(self, received, keys, lows):
        plan = self.plan
        mine = lax.axis_index("narrow")
        own_block = lax.div(mine, plan.cores)
        label = lax.rem(mine, plan.cores) ^ plan.swap(lax.axis_index("wide"), own_block)
        flip = label * plan.peers
        lane = lax.broadcasted_iota(jnp.int32, (self.targets, 128), 1)
        words = []
        for e in range(plan.list_rows):
            rows = [
                received[
                    pl.ds((own_block + i * plan.pairs) * plan.rows + plan.list_row + p * plan.list_rows + e, 1), :
                ]
                for i in range(plan.n_wide)
                for p in range(plan.own)
            ]
            words.append(jnp.concatenate(rows, 0).astype(jnp.int32))
        for e, entry in enumerate(plan.decode(words, lane)):
            op = entry & ((1 << plan.bits) - 1)
            high = op >> 7
            keys[e] = jnp.where(high < self.highs, high * plan.parents + ((entry >> plan.bits) ^ flip), -1)
            lows[e] = op & 127

    def count(self, first_target, keys, lows, tally):
        plan = self.plan
        kind = BF16 if self.highs * plan.parents <= 256 else F32
        key_at = lax.broadcasted_iota(jnp.int32, (self.highs * plan.parents, 128), 0).astype(kind)
        low_at = lax.broadcasted_iota(jnp.int32, (128, 128), 0).astype(BF16)
        for i in range(self.group):
            key_hits, low_hits = [], []
            for e in range(plan.entry_tiles):
                key = keys[e, pl.ds(first_target + i, 1), :].astype(kind)
                low = lows[e, pl.ds(first_target + i, 1), :].astype(BF16)
                key_hits.append(jnp.where(key_at == key, jnp.ones((), kind), jnp.zeros((), kind)).astype(BF16))
                low_hits.append(jnp.where(low_at == low, jnp.ones((), BF16), jnp.zeros((), BF16)))
            count_of = lax.dot_general(
                jnp.concatenate(key_hits, 1), jnp.concatenate(low_hits, 1), NT, preferred_element_type=F32
            ).astype(BF16)
            rows = slice(i * plan.parents, (i + 1) * plan.parents)
            for h in range(self.highs):
                tally[rows, 128 * h : 128 * h + 128] = count_of[h * plan.parents : (h + 1) * plan.parents]

    def sum_operators(self, tally, table, a_real, a_imag):
        for a in range(0, self.rows, 512):
            z = min(a + 512, self.rows)
            a_real[a:z, :] = lax.dot_general(tally[a:z, :], table[0], NT, preferred_element_type=F32)
            a_imag[a:z, :] = lax.dot_general(tally[a:z, :], table[1], NT, preferred_element_type=F32)

    def fill(self, table_in, table):
        table[...] = jnp.zeros(table.shape, BF16)
        table[:, 0 : self.plan.dirs, 0 : self.plan.ops] = table_in[...].astype(BF16)

    def kernel(self, table_in, received, a_real, a_imag, table, tally, keys, lows):
        self.read(received, keys, lows)
        self.count(0, keys, lows, tally)
        self.fill(table_in, table)
        self.sum_operators(tally, table, a_real, a_imag)


def translate_kernel(plan, tallies, ready):
    group = tallies.group

    def kernel(*refs):
        if ready:
            a_real, a_imag, *refs = refs
            blocks = refs[: plan.cores]
            (out,) = refs[plan.cores :]
        else:
            table_in, *refs = refs
            blocks = refs[: plan.cores]
            out, a_real, a_imag, table, tally, keys, lows = refs[plan.cores :]
            tallies.read(blocks[0], keys, lows)
            tallies.fill(table_in, table)

        def pattern(part, k):
            pieces = []
            for p in range(plan.own):
                if k < plan.full:
                    row, turn = (2 * p + part) * plan.full + k, 0
                else:
                    row, turn = plan.rest_at(p, part)
                for block in blocks:
                    piece = block[pl.ds(row, plan.peers, stride=plan.rows), :]
                    pieces.append(pltpu.roll(piece, 128 - turn, 1) if turn else piece)
            return jnp.concatenate(pieces, 0)

        def do_group(first_target):
            if not ready:
                tallies.count(first_target, keys, lows, tally)
                tallies.sum_operators(tally, table, a_real, a_imag)
            for k in range(plan.tiles):
                lanes = slice(128 * k, 128 * k + 128)
                out_real = pattern(0, k)
                out_imag = pattern(1, k)
                for i in range(group):
                    rows = slice(i * plan.parents, (i + 1) * plan.parents)
                    op_real = a_real[rows, lanes]
                    op_imag = a_imag[rows, lanes]
                    real = jnp.sum(op_real * out_real - op_imag * out_imag, 0, keepdims=True)
                    imag = jnp.sum(op_real * out_imag + op_imag * out_real, 0, keepdims=True)
                    at = (first_target + i) * 2 * plan.tiles + k
                    out[pl.ds(at, 1), :] = real
                    out[pl.ds(at + plan.tiles, 1), :] = imag

        if ready:
            do_group(0)
        else:
            pl.loop(0, tallies.targets // group)(lambda g: do_group(g * group))

    return kernel


def downward_kernel(plan):
    def kernel(received, angles, interp, rad, product, inner, twin):
        parent_dirs = angles.shape[1]
        leaf_dirs = rad.shape[0]
        parents_dev = product.shape[0] // 8
        boxes = product.shape[0]
        parts = 2 * parents_dev
        lane = lax.broadcasted_iota(jnp.int32, (parts, plan.width), 1)
        inner[...] = jnp.zeros(inner.shape, F32)
        for i, w in enumerate(plan.order):
            base = plan.dirs * w // 128 * 128
            shift = plan.dirs * w % 128
            span = -(-(shift + plan.dirs) // 128) * 128
            tiles = [
                received[pl.ds(i * parts * plan.tiles + k, parts, stride=plan.tiles), :]
                for k in range(plan.tiles)
            ]
            value = tiles[0] if plan.tiles == 1 else jnp.concatenate(tiles, 1)
            value = jnp.where(lane < plan.dirs, value, 0.0)
            if span > plan.width:
                value = jnp.concatenate([value, jnp.zeros((parts, span - plan.width), F32)], 1)
            if shift:
                value = pltpu.roll(value, shift, 1)
            span = min(value.shape[1], inner.shape[1] - base)
            inner[:, base : base + span] += value[:, 0:span]
        sn, cs = sin_cos(angles[...])
        reals, imags = [], []
        for p in range(parents_dev):
            in_real = inner[2 * p : 2 * p + 1, 0:parent_dirs]
            in_imag = inner[2 * p + 1 : 2 * p + 2, 0:parent_dirs]
            reals.append(cs * in_real + sn * in_imag)
            imags.append(cs * in_imag - sn * in_real)
        blank = jnp.zeros((128 - 2 * boxes, parent_dirs), F32)
        down = jnp.concatenate(
            reals + imags + [blank] + imags + [-r for r in reals] + [blank], 0
        ).astype(BF16)
        down_t = jnp.transpose(down)
        quarter = -(-leaf_dirs // 64) * 16
        got = jnp.concatenate(
            [
                jnp.dot(interp[a : min(a + quarter, leaf_dirs), :], down_t, preferred_element_type=F32)
                for a in range(0, leaf_dirs, quarter)
            ],
            0,
        )
        twin[pl.ds(0, leaf_dirs, stride=2), :] = got[:, 0:128]
        twin[pl.ds(1, leaf_dirs, stride=2), :] = got[:, 128:256]
        flat = jnp.transpose(twin[...])[0 : 2 * boxes].astype(BF16)
        matrix = rad[...].reshape(2 * leaf_dirs, rad.shape[2])
        result = jnp.dot(flat, matrix, preferred_element_type=F32)
        product[:, 0, :] = result[0:boxes]
        product[:, 1, :] = result[boxes : 2 * boxes]

    return kernel


def on_device(
    coefficients, radiation, interpolation, angles, translations, sources, operators, counts
):
    boxes = coefficients.shape[0]
    parents_dev = boxes // 8
    leaf_dirs, parent_dirs = interpolation.shape
    bases = coefficients.shape[2]
    n_wide = lax.axis_size("wide")
    n_narrow = lax.axis_size("narrow")
    dirs = translations.shape[2]
    n_ops = translations.shape[0]
    plan = Plan(parents_dev, n_wide, n_narrow, dirs, sources.shape[1], n_ops)
    rad = jnp.transpose(radiation, (2, 0, 1))
    table = jnp.transpose(translations, (1, 2, 0))
    cuts = [0, 1280, 2432]
    cuts = [c for c in cuts if c < parent_dirs] + [parent_dirs]
    vmem = pl.BlockSpec(memory_space=pltpu.VMEM)
    anywhere = pl.BlockSpec(memory_space=pl.ANY)

    send = pl.pallas_call(
        upward_kernel(plan, cuts),
        out_shape=jax.ShapeDtypeStruct((plan.peers * plan.rows, 128), F32),
        in_specs=[anywhere] * 7,
        out_specs=vmem,
        scratch_shapes=[
            pltpu.SMEM((parents_dev,), jnp.int32),
            pltpu.VMEM((boxes, 2, bases), BF16),
            pltpu.VMEM((leaf_dirs, 2, bases), BF16),
            pltpu.VMEM((leaf_dirs, parent_dirs), BF16),
            pltpu.VMEM(angles.shape, F32),
            pltpu.VMEM(sources.shape, jnp.int32),
            pltpu.VMEM(operators.shape, jnp.int32),
            pltpu.VMEM(angles.shape, F32),
            pltpu.VMEM(angles.shape, F32),
            pltpu.VMEM((2 * leaf_dirs, 128), F32),
            pltpu.VMEM((2 * leaf_dirs, 128), F32),
            pltpu.VMEM((parents_dev, 128 * plan.entry_tiles), jnp.int32),
            pltpu.VMEM((2 * parents_dev, parent_dirs), F32),
            pltpu.SemaphoreType.DMA((len(cuts) + 5,)),
        ],
        compiler_params=pltpu.CompilerParams(vmem_limit_bytes=56 * MIB),
        name="upward",
    )(counts, coefficients, rad, interpolation, angles, sources, operators)

    send = send.reshape(plan.peers, 1, plan.rows * 128)
    received = lax.all_to_all(
        send, ("wide", "narrow"), split_axis=0, concat_axis=0, tiled=True, axis_index_groups=plan.groups()
    ).reshape(-1, 128)
    blocks = [received]
    if plan.cores > 1:
        blocks.append(lax.ppermute(received, "narrow", [(i, i ^ 1) for i in range(n_narrow)]))

    tallies = Tally(plan)
    ready = tallies.targets == tallies.group
    sums = jax.ShapeDtypeStruct((tallies.rows, plan.width), F32)
    scratch = [pltpu.VMEM((2, plan.width, tallies.shape[1]), BF16), pltpu.VMEM(tallies.shape, BF16)] + tallies.scratch
    if ready:
        operands = pl.pallas_call(
            tallies.kernel,
            out_shape=(sums, sums),
            in_specs=[vmem, vmem],
            out_specs=(vmem, vmem),
            scratch_shapes=scratch,
            cost_estimate=pl.CostEstimate(flops=10**9, bytes_accessed=10**6, transcendentals=0),
            compiler_params=pltpu.CompilerParams(vmem_limit_bytes=16 * MIB),
            name="operators",
        )(table, received)
        scratch = []
    else:
        operands = [table]
        scratch = [pltpu.VMEM(sums.shape, F32), pltpu.VMEM(sums.shape, F32)] + scratch
    operands = [*operands, *blocks]
    incoming = pl.pallas_call(
        translate_kernel(plan, tallies, ready),
        out_shape=jax.ShapeDtypeStruct((n_wide * parents_dev * 2 * plan.tiles, 128), F32),
        in_specs=[vmem] * len(operands),
        out_specs=vmem,
        scratch_shapes=scratch,
        compiler_params=pltpu.CompilerParams(vmem_limit_bytes=24 * MIB),
        name="translate",
    )(*operands)

    incoming = incoming.reshape(n_wide, parents_dev * 2 * plan.tiles, 128)
    back = lax.all_to_all(
        incoming, ("wide", "narrow"), split_axis=0, concat_axis=0, tiled=True, axis_index_groups=plan.wide_groups()
    )
    back = back.reshape(-1, 128)

    return pl.pallas_call(
        downward_kernel(plan),
        out_shape=jax.ShapeDtypeStruct((boxes, 2, bases), F32),
        in_specs=[vmem] * 4,
        out_specs=vmem,
        scratch_shapes=[
            pltpu.VMEM((2 * parents_dev, parent_dirs + 128), F32),
            pltpu.VMEM((2 * leaf_dirs, 128), F32),
        ],
        compiler_params=pltpu.CompilerParams(vmem_limit_bytes=32 * MIB),
        name="downward",
    )(back, angles, interpolation, rad)


def solution(mesh):
    in_specs = (
        P(("wide", "narrow"), None, None),
        P(),
        P(),
        P(),
        P(None, None, "wide"),
        P(("wide", "narrow"), None),
        P(("wide", "narrow"), None),
        P(("wide", "narrow")),
    )
    out_specs = P(("wide", "narrow"), None, None)
    return jax.shard_map(
        on_device, mesh=mesh, in_specs=in_specs, out_specs=out_specs, check_vma=False
    )
```

```python
import jax
import jax.numpy as jnp
from jax import lax
from jax.experimental import pallas as pl
from jax.experimental.pallas import tpu as pltpu
from jax.sharding import PartitionSpec as P

F32 = jnp.float32
BF16 = jnp.bfloat16
MIB = 2**20
NT = (((1,), (1,)), ((), ()))


class Plan:
    def __init__(self, own, n_wide, n_narrow, dirs, length, ops):
        self.own = own
        self.n_wide = n_wide
        self.n_narrow = n_narrow
        self.devices = n_wide * n_narrow
        self.parents = own * self.devices
        first = n_wide * 5 // 8
        self.order = list(range(first, -1, -1)) + list(range(first + 1, n_wide))
        self.cores = 2 if n_narrow % 2 == 0 else 1
        self.pairs = n_narrow // self.cores
        self.peers = n_wide * self.pairs
        self.dirs = dirs
        self.length = length
        self.ops = ops
        self.full = dirs // 128
        self.rest = dirs % 128
        self.tiles = -(-dirs // 128)
        self.width = 128 * self.tiles
        self.bits = ops.bit_length()
        entry_bits = self.bits + (self.parents - 1).bit_length()
        self.none = (1 << entry_bits) - 1
        self.rest_row = own * 2 * self.full
        self.shared = 2 * own * self.rest <= 128
        rest_rows = 0 if not self.rest else 1 if self.shared else 2 * own
        self.list_row = self.rest_row + rest_rows
        self.dense = entry_bits <= 15 and length <= 192
        self.entry_tiles = 2 if self.dense else -(-length // 128)
        self.list_rows = 1 if self.dense else self.entry_tiles
        self.rows = self.list_row + own * self.list_rows

    def rest_at(self, p, part):
        if self.shared:
            return self.rest_row, (2 * p + part) * self.rest
        return self.rest_row + 2 * p + part, 0

    def swap(self, w, pair):
        return w // (self.n_wide // 2) if self.cores > 1 else 0

    def device(self, w, pair, label):
        return w * self.n_narrow + pair * self.cores + (label ^ self.swap(w, pair))

    def groups(self):
        return [
            [self.device(w, pair, label) for w in self.order for pair in range(self.pairs)]
            for label in range(self.cores)
        ]

    def wide_groups(self):
        return [
            [self.device(w, pair, label) for w in self.order]
            for pair in range(self.pairs)
            for label in range(self.cores)
        ]

    def place(self, source):
        narrow_shift = self.own.bit_length() - 1
        device = source >> narrow_shift
        place = jnp.zeros(source.shape, jnp.int32)
        for i, w in enumerate(self.order):
            for pair in range(self.pairs):
                for label in range(self.cores):
                    block = label * self.peers + i * self.pairs + pair
                    place = jnp.where(device == self.device(w, pair, label), block, place)
        return (source & (self.own - 1)) * self.devices + place

    def encode(self, entries, lane):
        if not self.dense:
            return entries
        first, third = entries
        low = jnp.where(lane < 64, third & 255, pltpu.roll(third, 64, 1) >> 8)
        return [first * 256 + low]

    def decode(self, words, lane):
        if not self.dense:
            return words
        low = words[0] & 255
        third = low + (pltpu.roll(low, 64, 1) << 8)
        return [words[0] >> 8, jnp.where(lane < 64, third, self.none)]


def sin_cos(angle):
    turns = jnp.floor(angle * 0.6366197723675814 + 0.5)
    quarter = turns.astype(jnp.int32)
    rest = angle - turns * 1.5703125
    rest = rest - turns * 4.837512969970703e-4
    rest = rest - turns * 7.54978995489188e-8
    square = rest * rest
    sine = ((-1.9515295891e-4 * square + 8.3321608736e-3) * square - 1.6666654611e-1) * square * rest + rest
    cosine = ((2.443315711809948e-5 * square - 1.388731625493765e-3) * square + 4.166664568298827e-2) * (
        square * square
    ) - 0.5 * square + 1.0
    swap = (quarter & 1) == 1
    sin_value = jnp.where(swap, cosine, sine)
    cos_value = jnp.where(swap, sine, cosine)
    sin_value = jnp.where((quarter & 2) == 2, -sin_value, sin_value)
    cos_value = jnp.where(((quarter + 1) & 2) == 2, -cos_value, cos_value)
    return sin_value, cos_value


def arrange(boxes, swapped):
    row = lax.broadcasted_iota(jnp.int32, (128, 2 * boxes), 0)
    column = lax.broadcasted_iota(jnp.int32, (128, 2 * boxes), 1)
    real_at = 2 * row
    imag_at = 2 * (row - boxes) + 1
    if swapped:
        first = jnp.where((row < boxes) & (column == real_at + 1), -1.0, 0.0)
        second = jnp.where((row >= boxes) & (row < 2 * boxes) & (column == imag_at - 1), 1.0, 0.0)
    else:
        first = jnp.where((row < boxes) & (column == real_at), 1.0, 0.0)
        second = jnp.where((row >= boxes) & (row < 2 * boxes) & (column == imag_at), 1.0, 0.0)
    return (first + second).astype(BF16)


def upward_kernel(plan, cuts):
    def kernel(
        counts_hbm, coef_hbm, rad_hbm, interp_hbm, angles_hbm, sources_hbm, operators_hbm,
        send_out,
        send, counts, coef, rad, interp, angles, sources, operators, cos_out, sin_out,
        even, odd, codes, out_buf, sems,
    ):
        parent_dirs = angles.shape[1]
        leaf_dirs = rad_hbm.shape[0]
        boxes = coef.shape[0]
        parents_dev = boxes // 8
        n_chunks = len(cuts) - 1
        half = -(-leaf_dirs // 16) * 16
        first = []
        for source, target in (
            (angles_hbm, angles),
            (coef_hbm, coef),
            (rad_hbm, rad.at[pl.ds(0, leaf_dirs)]),
            (sources_hbm, sources),
            (operators_hbm, operators),
            (counts_hbm, counts),
        ):
            first.append(pltpu.make_async_copy(source, target, sems.at[n_chunks + len(first)]))
            first[-1].start()
        copies = []
        for c in range(n_chunks):
            cut = (slice(None), pl.ds(cuts[c], cuts[c + 1] - cuts[c]))
            copies.append(pltpu.make_async_copy(interp_hbm.at[cut], interp.at[cut], sems.at[c]))
            copies[-1].start()

        first[0].wait()
        sines, cosines = sin_cos(angles[...])
        sin_out[...] = sines
        cos_out[...] = cosines

        for copy in first[3:]:
            copy.wait()
        code = plan.place(sources[...]) * (1 << plan.bits) + operators[...]
        at = lax.broadcasted_iota(jnp.int32, code.shape, 1)
        parent = lax.broadcasted_iota(jnp.int32, code.shape, 0)
        limit = jnp.zeros(code.shape, jnp.int32)
        for p in range(parents_dev):
            limit = jnp.where(parent == p, counts[p], limit)
        codes[...] = jnp.full(codes.shape, plan.none, jnp.int32)
        codes[:, 0 : plan.length] = jnp.where(at < limit, code, plan.none)

        first[1].wait()
        rows = coef[...].reshape(2 * boxes, coef.shape[2])
        plain = jnp.dot(arrange(boxes, False), rows, preferred_element_type=F32).astype(BF16)
        turned = jnp.dot(arrange(boxes, True), rows, preferred_element_type=F32).astype(BF16)
        weights = jnp.concatenate([plain, turned], 0)

        first[2].wait()
        matrix = rad[0:leaf_dirs].reshape(2 * leaf_dirs, rad.shape[2])
        weights_t = jnp.transpose(weights)
        for a in range(0, 2 * leaf_dirs, half):
            z = min(a + half, 2 * leaf_dirs)
            both = jnp.dot(matrix[a:z], weights_t, preferred_element_type=F32)
            even[a:z, :] = both[:, 0:128]
            odd[a:z, :] = both[:, 128:256]
        leaf_t = even[pl.ds(0, leaf_dirs, stride=2), :] + odd[pl.ds(1, leaf_dirs, stride=2), :]
        leaf = jnp.transpose(leaf_t)[0 : 2 * boxes].astype(BF16)

        lane = lax.broadcasted_iota(jnp.int32, (parents_dev, 128), 1)
        words = plan.encode([codes[:, 128 * e : 128 * e + 128] for e in range(plan.entry_tiles)], lane)

        def put(w, row, stride, piece):
            for pair in range(plan.pairs):
                at_row = (plan.order.index(w) * plan.pairs + pair) * plan.rows + row
                send[pl.ds(at_row, piece.shape[0], stride=stride), :] = piece

        for w in range(plan.n_wide):
            for e, word in enumerate(words):
                put(w, plan.list_row + e, plan.list_rows, word.astype(F32))

        wide_lane = lax.broadcasted_iota(jnp.int32, (2 * parents_dev, 128), 1)

        def pack(w):
            base = plan.dirs * w // 128 * 128
            shift = plan.dirs * w % 128
            span = -(-(shift + plan.dirs) // 128) * 128
            span = min(max(span, plan.width), parent_dirs - base)
            value = out_buf[:, base : base + span]
            if shift:
                value = pltpu.roll(value, span - shift, 1)
            for k in range(plan.full):
                put(w, k, plan.full, value[:, 128 * k : 128 * k + 128])
            if plan.rest:
                piece = jnp.where(wide_lane < plan.rest, value[:, 128 * plan.full : plan.width], 0.0)
                if plan.shared:
                    piece = sum(
                        pltpu.roll(piece[r : r + 1], plan.rest * r, 1) if r else piece[0:1]
                        for r in range(2 * parents_dev)
                    )
                put(w, plan.rest_row, 1, piece)

        n_wide = plan.n_wide
        ups = []
        for c in range(n_chunks):
            copies[c].wait()
            ups.append(jnp.dot(leaf, interp[:, cuts[c] : cuts[c + 1]], preferred_element_type=F32))
        for c in range(n_chunks):
            cut = slice(cuts[c], cuts[c + 1])
            up = ups[c]
            cs = cos_out[:, cut]
            sn = sin_out[:, cut]
            for p in range(parents_dev):
                up_real = up[8 * p : 8 * p + 8]
                up_imag = up[boxes + 8 * p : boxes + 8 * p + 8]
                out_buf[2 * p : 2 * p + 1, cut] = jnp.sum(cs * up_real - sn * up_imag, 0, keepdims=True)
                out_buf[2 * p + 1 : 2 * p + 2, cut] = jnp.sum(cs * up_imag + sn * up_real, 0, keepdims=True)
        for w in range(n_wide):
            pack(w)
        send_out[...] = send[0 : send_out.shape[0], :]

    return kernel


class Tally:
    def __init__(self, plan):
        self.plan = plan
        self.targets = plan.n_wide * plan.own
        self.group = max(1, min(self.targets, 1024 // plan.parents))
        self.highs = -(-plan.ops // 128)
        self.rows = self.group * plan.parents
        self.shape = (self.rows, 128 * self.highs)
        lists = pltpu.VMEM((plan.entry_tiles, self.targets, 128), jnp.int32)
        self.scratch = [lists, lists]

    def read(self, received, keys, lows):
        plan = self.plan
        mine = lax.axis_index("narrow")
        own_block = lax.div(mine, plan.cores)
        label = lax.rem(mine, plan.cores) ^ plan.swap(lax.axis_index("wide"), own_block)
        flip = label * plan.peers
        lane = lax.broadcasted_iota(jnp.int32, (self.targets, 128), 1)
        words = []
        for e in range(plan.list_rows):
            rows = [
                received[
                    pl.ds((own_block + i * plan.pairs) * plan.rows + plan.list_row + p * plan.list_rows + e, 1), :
                ]
                for i in range(plan.n_wide)
                for p in range(plan.own)
            ]
            words.append(jnp.concatenate(rows, 0).astype(jnp.int32))
        for e, entry in enumerate(plan.decode(words, lane)):
            op = entry & ((1 << plan.bits) - 1)
            high = op >> 7
            keys[e] = jnp.where(high < self.highs, high * plan.parents + ((entry >> plan.bits) ^ flip), -1)
            lows[e] = op & 127

    def count(self, first_target, keys, lows, tally):
        plan = self.plan
        kind = BF16 if self.highs * plan.parents <= 256 else F32
        key_at = lax.broadcasted_iota(jnp.int32, (self.highs * plan.parents, 128), 0).astype(kind)
        low_at = lax.broadcasted_iota(jnp.int32, (128, 128), 0).astype(BF16)
        for i in range(self.group):
            key_hits, low_hits = [], []
            for e in range(plan.entry_tiles):
                key = keys[e, pl.ds(first_target + i, 1), :].astype(kind)
                low = lows[e, pl.ds(first_target + i, 1), :].astype(BF16)
                key_hits.append(jnp.where(key_at == key, jnp.ones((), kind), jnp.zeros((), kind)).astype(BF16))
                low_hits.append(jnp.where(low_at == low, jnp.ones((), BF16), jnp.zeros((), BF16)))
            count_of = lax.dot_general(
                jnp.concatenate(key_hits, 1), jnp.concatenate(low_hits, 1), NT, preferred_element_type=F32
            ).astype(BF16)
            rows = slice(i * plan.parents, (i + 1) * plan.parents)
            for h in range(self.highs):
                tally[rows, 128 * h : 128 * h + 128] = count_of[h * plan.parents : (h + 1) * plan.parents]

    def sum_operators(self, tally, table, a_real, a_imag):
        for a in range(0, self.rows, 512):
            z = min(a + 512, self.rows)
            a_real[a:z, :] = lax.dot_general(tally[a:z, :], table[0], NT, preferred_element_type=F32)
            a_imag[a:z, :] = lax.dot_general(tally[a:z, :], table[1], NT, preferred_element_type=F32)

    def fill(self, table_in, table):
        table[...] = jnp.zeros(table.shape, BF16)
        table[:, 0 : self.plan.dirs, 0 : self.plan.ops] = table_in[...].astype(BF16)

    def kernel(self, table_in, received, a_real, a_imag, table, tally, keys, lows):
        self.read(received, keys, lows)
        self.count(0, keys, lows, tally)
        self.fill(table_in, table)
        self.sum_operators(tally, table, a_real, a_imag)


def translate_kernel(plan, tallies, ready):
    group = tallies.group

    def kernel(*refs):
        if ready:
            a_real, a_imag, *refs = refs
            blocks = refs[: plan.cores]
            (out,) = refs[plan.cores :]
        else:
            table_in, *refs = refs
            blocks = refs[: plan.cores]
            out, a_real, a_imag, table, tally, keys, lows = refs[plan.cores :]
            tallies.read(blocks[0], keys, lows)
            tallies.fill(table_in, table)

        def pattern(part, k):
            pieces = []
            for p in range(plan.own):
                if k < plan.full:
                    row, turn = (2 * p + part) * plan.full + k, 0
                else:
                    row, turn = plan.rest_at(p, part)
                for block in blocks:
                    piece = block[pl.ds(row, plan.peers, stride=plan.rows), :]
                    pieces.append(pltpu.roll(piece, 128 - turn, 1) if turn else piece)
            return jnp.concatenate(pieces, 0)

        def do_group(first_target):
            if not ready:
                tallies.count(first_target, keys, lows, tally)
                tallies.sum_operators(tally, table, a_real, a_imag)
            for k in range(plan.tiles):
                lanes = slice(128 * k, 128 * k + 128)
                out_real = pattern(0, k)
                out_imag = pattern(1, k)
                for i in range(group):
                    rows = slice(i * plan.parents, (i + 1) * plan.parents)
                    op_real = a_real[rows, lanes]
                    op_imag = a_imag[rows, lanes]
                    real = jnp.sum(op_real * out_real - op_imag * out_imag, 0, keepdims=True)
                    imag = jnp.sum(op_real * out_imag + op_imag * out_real, 0, keepdims=True)
                    at = (first_target + i) * 2 * plan.tiles + k
                    out[pl.ds(at, 1), :] = real
                    out[pl.ds(at + plan.tiles, 1), :] = imag

        if ready:
            do_group(0)
        else:
            pl.loop(0, tallies.targets // group)(lambda g: do_group(g * group))

    return kernel


def downward_kernel(plan):
    def kernel(arrived, angles, interp, rad, product, received, inner, twin):
        parent_dirs = angles.shape[1]
        leaf_dirs = rad.shape[0]
        parents_dev = product.shape[0] // 8
        boxes = product.shape[0]
        parts = 2 * parents_dev
        lane = lax.broadcasted_iota(jnp.int32, (parts, plan.width), 1)
        received[0 : arrived.shape[0], :] = arrived[...]
        inner[...] = jnp.zeros(inner.shape, F32)
        for i, w in enumerate(plan.order):
            base = plan.dirs * w // 128 * 128
            shift = plan.dirs * w % 128
            span = -(-(shift + plan.dirs) // 128) * 128
            tiles = [
                received[pl.ds(i * parts * plan.tiles + k, parts, stride=plan.tiles), :]
                for k in range(plan.tiles)
            ]
            value = tiles[0] if plan.tiles == 1 else jnp.concatenate(tiles, 1)
            value = jnp.where(lane < plan.dirs, value, 0.0)
            if span > plan.width:
                value = jnp.concatenate([value, jnp.zeros((parts, span - plan.width), F32)], 1)
            if shift:
                value = pltpu.roll(value, shift, 1)
            span = min(value.shape[1], inner.shape[1] - base)
            inner[:, base : base + span] += value[:, 0:span]
        sn, cs = sin_cos(angles[...])
        reals, imags = [], []
        for p in range(parents_dev):
            in_real = inner[2 * p : 2 * p + 1, 0:parent_dirs]
            in_imag = inner[2 * p + 1 : 2 * p + 2, 0:parent_dirs]
            reals.append(cs * in_real + sn * in_imag)
            imags.append(cs * in_imag - sn * in_real)
        blank = jnp.zeros((128 - 2 * boxes, parent_dirs), F32)
        down = jnp.concatenate(
            reals + imags + [blank] + imags + [-r for r in reals] + [blank], 0
        ).astype(BF16)
        down_t = jnp.transpose(down)
        quarter = -(-leaf_dirs // 64) * 16
        got = jnp.concatenate(
            [
                jnp.dot(interp[a : min(a + quarter, leaf_dirs), :], down_t, preferred_element_type=F32)
                for a in range(0, leaf_dirs, quarter)
            ],
            0,
        )
        twin[pl.ds(0, leaf_dirs, stride=2), :] = got[:, 0:128]
        twin[pl.ds(1, leaf_dirs, stride=2), :] = got[:, 128:256]
        flat = jnp.transpose(twin[0 : 2 * leaf_dirs, :])[0 : 2 * boxes].astype(BF16)
        matrix = rad[...].reshape(2 * leaf_dirs, rad.shape[2])
        result = jnp.dot(flat, matrix, preferred_element_type=F32)
        product[:, 0, :] = result[0:boxes]
        product[:, 1, :] = result[boxes : 2 * boxes]

    return kernel


def on_device(
    coefficients, radiation, interpolation, angles, translations, sources, operators, counts
):
    boxes = coefficients.shape[0]
    parents_dev = boxes // 8
    leaf_dirs, parent_dirs = interpolation.shape
    bases = coefficients.shape[2]
    n_wide = lax.axis_size("wide")
    n_narrow = lax.axis_size("narrow")
    dirs = translations.shape[2]
    n_ops = translations.shape[0]
    plan = Plan(parents_dev, n_wide, n_narrow, dirs, sources.shape[1], n_ops)
    rad = jnp.transpose(radiation, (2, 0, 1))
    table = jnp.transpose(translations, (1, 2, 0))
    room = -(-leaf_dirs // 16) * 16 + 16
    cuts = [0, 1280, 2432]
    cuts = [c for c in cuts if c < parent_dirs] + [parent_dirs]
    vmem = pl.BlockSpec(memory_space=pltpu.VMEM)
    anywhere = pl.BlockSpec(memory_space=pl.ANY)

    send = pl.pallas_call(
        upward_kernel(plan, cuts),
        out_shape=jax.ShapeDtypeStruct((plan.peers * plan.rows, 128), F32),
        in_specs=[anywhere] * 7,
        out_specs=vmem,
        scratch_shapes=[
            pltpu.VMEM((plan.peers * plan.rows + 64, 128), F32),
            pltpu.SMEM((parents_dev,), jnp.int32),
            pltpu.VMEM((boxes, 2, bases), BF16),
            pltpu.VMEM((room, 2, bases), BF16),
            pltpu.VMEM((leaf_dirs, parent_dirs), BF16),
            pltpu.VMEM(angles.shape, F32),
            pltpu.VMEM(sources.shape, jnp.int32),
            pltpu.VMEM(operators.shape, jnp.int32),
            pltpu.VMEM(angles.shape, F32),
            pltpu.VMEM(angles.shape, F32),
            pltpu.VMEM((2 * room, 128), F32),
            pltpu.VMEM((2 * room, 128), F32),
            pltpu.VMEM((parents_dev, 128 * plan.entry_tiles), jnp.int32),
            pltpu.VMEM((2 * parents_dev, parent_dirs), F32),
            pltpu.SemaphoreType.DMA((len(cuts) + 5,)),
        ],
        compiler_params=pltpu.CompilerParams(vmem_limit_bytes=56 * MIB),
        name="upward",
    )(counts, coefficients, rad, interpolation, angles, sources, operators)

    send = send.reshape(plan.peers, 1, plan.rows * 128)
    received = lax.all_to_all(
        send, ("wide", "narrow"), split_axis=0, concat_axis=0, tiled=True, axis_index_groups=plan.groups()
    ).reshape(-1, 128)
    blocks = [received]
    if plan.cores > 1:
        blocks.append(lax.ppermute(received, "narrow", [(i, i ^ 1) for i in range(n_narrow)]))

    tallies = Tally(plan)
    ready = tallies.targets == tallies.group
    sums = jax.ShapeDtypeStruct((tallies.rows, plan.width), F32)
    scratch = [pltpu.VMEM((2, plan.width, tallies.shape[1]), BF16), pltpu.VMEM(tallies.shape, BF16)] + tallies.scratch
    if ready:
        operands = pl.pallas_call(
            tallies.kernel,
            out_shape=(sums, sums),
            in_specs=[vmem, vmem],
            out_specs=(vmem, vmem),
            scratch_shapes=scratch,
            cost_estimate=pl.CostEstimate(flops=10**9, bytes_accessed=10**6, transcendentals=0),
            compiler_params=pltpu.CompilerParams(vmem_limit_bytes=16 * MIB),
            name="operators",
        )(table, received)
        scratch = []
    else:
        operands = [table]
        scratch = [pltpu.VMEM(sums.shape, F32), pltpu.VMEM(sums.shape, F32)] + scratch
    operands = [*operands, *blocks]
    incoming = pl.pallas_call(
        translate_kernel(plan, tallies, ready),
        out_shape=jax.ShapeDtypeStruct((n_wide * parents_dev * 2 * plan.tiles, 128), F32),
        in_specs=[vmem] * len(operands),
        out_specs=vmem,
        scratch_shapes=scratch,
        compiler_params=pltpu.CompilerParams(vmem_limit_bytes=24 * MIB),
        name="translate",
    )(*operands)

    incoming = incoming.reshape(n_wide, parents_dev * 2 * plan.tiles, 128)
    back = lax.all_to_all(
        incoming, ("wide", "narrow"), split_axis=0, concat_axis=0, tiled=True, axis_index_groups=plan.wide_groups()
    )
    back = back.reshape(-1, 128)

    return pl.pallas_call(
        downward_kernel(plan),
        out_shape=jax.ShapeDtypeStruct((boxes, 2, bases), F32),
        in_specs=[vmem] * 4,
        out_specs=vmem,
        scratch_shapes=[
            pltpu.VMEM((n_wide * parents_dev * 2 * plan.tiles + 64, 128), F32),
            pltpu.VMEM((2 * parents_dev, parent_dirs + 128), F32),
            pltpu.VMEM((2 * room, 128), F32),
        ],
        compiler_params=pltpu.CompilerParams(vmem_limit_bytes=32 * MIB),
        name="downward",
    )(back, angles, interpolation, rad)


def solution(mesh):
    in_specs = (
        P(("wide", "narrow"), None, None),
        P(),
        P(),
        P(),
        P(None, None, "wide"),
        P(("wide", "narrow"), None),
        P(("wide", "narrow"), None),
        P(("wide", "narrow")),
    )
    out_specs = P(("wide", "narrow"), None, None)
    return jax.shard_map(
        on_device, mesh=mesh, in_specs=in_specs, out_specs=out_specs, check_vma=False
    )
```

```python
import jax
import jax.numpy as jnp
from jax import lax
from jax.experimental import pallas as pl
from jax.experimental.pallas import tpu as pltpu
from jax.sharding import PartitionSpec as P

F32 = jnp.float32
BF16 = jnp.bfloat16
MIB = 2**20
NT = (((1,), (1,)), ((), ()))


class Plan:
    def __init__(self, own, n_wide, n_narrow, dirs, length, ops):
        self.own = own
        self.n_wide = n_wide
        self.n_narrow = n_narrow
        self.devices = n_wide * n_narrow
        self.parents = own * self.devices
        first = n_wide * 5 // 8
        self.order = list(range(first, -1, -1)) + list(range(first + 1, n_wide))
        self.cores = 2 if n_narrow % 2 == 0 else 1
        self.pairs = n_narrow // self.cores
        self.peers = n_wide * self.pairs
        self.dirs = dirs
        self.length = length
        self.ops = ops
        self.full = dirs // 128
        self.rest = dirs % 128
        self.tiles = -(-dirs // 128)
        self.width = 128 * self.tiles
        self.bits = ops.bit_length()
        entry_bits = self.bits + (self.parents - 1).bit_length()
        self.none = (1 << entry_bits) - 1
        self.rest_row = own * 2 * self.full
        self.shared = 2 * own * self.rest <= 128
        rest_rows = 0 if not self.rest else 1 if self.shared else 2 * own
        self.list_row = self.rest_row + rest_rows
        self.dense = entry_bits <= 15 and length <= 192
        self.entry_tiles = 2 if self.dense else -(-length // 128)
        self.list_rows = 1 if self.dense else self.entry_tiles
        self.rows = self.list_row + own * self.list_rows

    def rest_at(self, p, part):
        if self.shared:
            return self.rest_row, (2 * p + part) * self.rest
        return self.rest_row + 2 * p + part, 0

    def swap(self, w, pair):
        return w // (self.n_wide // 2) if self.cores > 1 else 0

    def device(self, w, pair, label):
        return w * self.n_narrow + pair * self.cores + (label ^ self.swap(w, pair))

    def groups(self):
        return [
            [self.device(w, pair, label) for w in self.order for pair in range(self.pairs)]
            for label in range(self.cores)
        ]

    def wide_groups(self):
        return [
            [self.device(w, pair, label) for w in self.order]
            for pair in range(self.pairs)
            for label in range(self.cores)
        ]

    def place(self, source):
        narrow_shift = self.own.bit_length() - 1
        device = source >> narrow_shift
        place = jnp.zeros(source.shape, jnp.int32)
        for i, w in enumerate(self.order):
            for pair in range(self.pairs):
                for label in range(self.cores):
                    block = label * self.peers + i * self.pairs + pair
                    place = jnp.where(device == self.device(w, pair, label), block, place)
        return (source & (self.own - 1)) * self.devices + place

    def encode(self, entries, lane):
        if not self.dense:
            return entries
        first, third = entries
        low = jnp.where(lane < 64, third & 255, pltpu.roll(third, 64, 1) >> 8)
        return [first * 256 + low]

    def decode(self, words, lane):
        if not self.dense:
            return words
        low = words[0] & 255
        third = low + (pltpu.roll(low, 64, 1) << 8)
        return [words[0] >> 8, jnp.where(lane < 64, third, self.none)]


def sin_cos(angle):
    turns = jnp.floor(angle * 0.6366197723675814 + 0.5)
    quarter = turns.astype(jnp.int32)
    rest = angle - turns * 1.5703125
    rest = rest - turns * 4.837512969970703e-4
    rest = rest - turns * 7.54978995489188e-8
    square = rest * rest
    sine = ((-1.9515295891e-4 * square + 8.3321608736e-3) * square - 1.6666654611e-1) * square * rest + rest
    cosine = ((2.443315711809948e-5 * square - 1.388731625493765e-3) * square + 4.166664568298827e-2) * (
        square * square
    ) - 0.5 * square + 1.0
    swap = (quarter & 1) == 1
    sin_value = jnp.where(swap, cosine, sine)
    cos_value = jnp.where(swap, sine, cosine)
    sin_value = jnp.where((quarter & 2) == 2, -sin_value, sin_value)
    cos_value = jnp.where(((quarter + 1) & 2) == 2, -cos_value, cos_value)
    return sin_value, cos_value


def arrange(boxes, swapped):
    row = lax.broadcasted_iota(jnp.int32, (128, 2 * boxes), 0)
    column = lax.broadcasted_iota(jnp.int32, (128, 2 * boxes), 1)
    real_at = 2 * row
    imag_at = 2 * (row - boxes) + 1
    if swapped:
        first = jnp.where((row < boxes) & (column == real_at + 1), -1.0, 0.0)
        second = jnp.where((row >= boxes) & (row < 2 * boxes) & (column == imag_at - 1), 1.0, 0.0)
    else:
        first = jnp.where((row < boxes) & (column == real_at), 1.0, 0.0)
        second = jnp.where((row >= boxes) & (row < 2 * boxes) & (column == imag_at), 1.0, 0.0)
    return (first + second).astype(BF16)


def upward_kernel(plan, cuts):
    def kernel(
        counts_hbm, coef_hbm, rad_hbm, interp_hbm, angles_hbm, sources_hbm, operators_hbm,
        send_out,
        send, counts, coef, rad, interp, angles, sources, operators, cos_out, sin_out,
        even, odd, codes, out_buf, sems,
    ):
        parent_dirs = angles.shape[1]
        leaf_dirs = rad_hbm.shape[0]
        boxes = coef.shape[0]
        parents_dev = boxes // 8
        n_chunks = len(cuts) - 1
        half = -(-leaf_dirs // 16) * 16
        first = []
        for source, target in (
            (angles_hbm, angles),
            (coef_hbm, coef),
            (rad_hbm, rad.at[pl.ds(0, leaf_dirs)]),
            (sources_hbm, sources),
            (operators_hbm, operators),
            (counts_hbm, counts),
        ):
            first.append(pltpu.make_async_copy(source, target, sems.at[n_chunks + len(first)]))
            first[-1].start()
        copies = []
        for c in range(n_chunks):
            cut = (slice(None), pl.ds(cuts[c], cuts[c + 1] - cuts[c]))
            copies.append(pltpu.make_async_copy(interp_hbm.at[cut], interp.at[cut], sems.at[c]))
            copies[-1].start()

        first[0].wait()
        sines, cosines = sin_cos(angles[...])
        sin_out[...] = sines
        cos_out[...] = cosines

        for copy in first[3:]:
            copy.wait()
        code = plan.place(sources[...]) * (1 << plan.bits) + operators[...]
        at = lax.broadcasted_iota(jnp.int32, code.shape, 1)
        parent = lax.broadcasted_iota(jnp.int32, code.shape, 0)
        limit = jnp.zeros(code.shape, jnp.int32)
        for p in range(parents_dev):
            limit = jnp.where(parent == p, counts[p], limit)
        codes[...] = jnp.full(codes.shape, plan.none, jnp.int32)
        codes[:, 0 : plan.length] = jnp.where(at < limit, code, plan.none)

        first[1].wait()
        rows = coef[...].reshape(2 * boxes, coef.shape[2])
        plain = jnp.dot(arrange(boxes, False), rows, preferred_element_type=F32).astype(BF16)
        turned = jnp.dot(arrange(boxes, True), rows, preferred_element_type=F32).astype(BF16)
        weights = jnp.concatenate([plain, turned], 0)

        first[2].wait()
        matrix = rad[0:leaf_dirs].reshape(2 * leaf_dirs, rad.shape[2])
        weights_t = jnp.transpose(weights)
        for a in range(0, 2 * leaf_dirs, half):
            z = min(a + half, 2 * leaf_dirs)
            both = jnp.dot(matrix[a:z], weights_t, preferred_element_type=F32)
            even[a:z, :] = both[:, 0:128]
            odd[a:z, :] = both[:, 128:256]
        leaf_t = even[pl.ds(0, leaf_dirs, stride=2), :] + odd[pl.ds(1, leaf_dirs, stride=2), :]
        leaf = jnp.transpose(leaf_t)[0 : 2 * boxes].astype(BF16)

        lane = lax.broadcasted_iota(jnp.int32, (parents_dev, 128), 1)
        words = plan.encode([codes[:, 128 * e : 128 * e + 128] for e in range(plan.entry_tiles)], lane)

        def put(w, row, stride, piece):
            for pair in range(plan.pairs):
                at_row = (plan.order.index(w) * plan.pairs + pair) * plan.rows + row
                send[pl.ds(at_row, piece.shape[0], stride=stride), :] = piece

        for w in range(plan.n_wide):
            for e, word in enumerate(words):
                put(w, plan.list_row + e, plan.list_rows, word.astype(F32))

        wide_lane = lax.broadcasted_iota(jnp.int32, (2 * parents_dev, 128), 1)

        def pack(w):
            base = plan.dirs * w // 128 * 128
            shift = plan.dirs * w % 128
            span = -(-(shift + plan.dirs) // 128) * 128
            span = min(max(span, plan.width), parent_dirs - base)
            value = out_buf[:, base : base + span]
            if shift:
                value = pltpu.roll(value, span - shift, 1)
            for k in range(plan.full):
                put(w, k, plan.full, value[:, 128 * k : 128 * k + 128])
            if plan.rest:
                piece = jnp.where(wide_lane < plan.rest, value[:, 128 * plan.full : plan.width], 0.0)
                if plan.shared:
                    piece = sum(
                        pltpu.roll(piece[r : r + 1], plan.rest * r, 1) if r else piece[0:1]
                        for r in range(2 * parents_dev)
                    )
                put(w, plan.rest_row, 1, piece)

        n_wide = plan.n_wide
        ups = []
        for c in range(n_chunks):
            copies[c].wait()
            ups.append(jnp.dot(leaf, interp[:, cuts[c] : cuts[c + 1]], preferred_element_type=F32))
        for c in range(n_chunks):
            cut = slice(cuts[c], cuts[c + 1])
            up = ups[c]
            cs = cos_out[:, cut]
            sn = sin_out[:, cut]
            for p in range(parents_dev):
                up_real = up[8 * p : 8 * p + 8]
                up_imag = up[boxes + 8 * p : boxes + 8 * p + 8]
                out_buf[2 * p : 2 * p + 1, cut] = jnp.sum(cs * up_real - sn * up_imag, 0, keepdims=True)
                out_buf[2 * p + 1 : 2 * p + 2, cut] = jnp.sum(cs * up_imag + sn * up_real, 0, keepdims=True)
        for w in range(n_wide):
            pack(w)
        send_out[...] = send[0 : send_out.shape[0], :]

    return kernel


class Tally:
    def __init__(self, plan):
        self.plan = plan
        self.targets = plan.n_wide * plan.own
        self.group = max(1, min(self.targets, 1024 // plan.parents))
        self.highs = -(-plan.ops // 128)
        self.rows = self.group * plan.parents
        self.shape = (self.rows, 128 * self.highs)
        lists = pltpu.VMEM((plan.entry_tiles, self.targets, 128), jnp.int32)
        self.scratch = [lists, lists]

    def read(self, received, keys, lows):
        plan = self.plan
        mine = lax.axis_index("narrow")
        own_block = lax.div(mine, plan.cores)
        label = lax.rem(mine, plan.cores) ^ plan.swap(lax.axis_index("wide"), own_block)
        flip = label * plan.peers
        lane = lax.broadcasted_iota(jnp.int32, (self.targets, 128), 1)
        words = []
        for e in range(plan.list_rows):
            rows = [
                received[
                    pl.ds((own_block + i * plan.pairs) * plan.rows + plan.list_row + p * plan.list_rows + e, 1), :
                ]
                for i in range(plan.n_wide)
                for p in range(plan.own)
            ]
            words.append(jnp.concatenate(rows, 0).astype(jnp.int32))
        for e, entry in enumerate(plan.decode(words, lane)):
            op = entry & ((1 << plan.bits) - 1)
            high = op >> 7
            keys[e] = jnp.where(high < self.highs, high * plan.parents + ((entry >> plan.bits) ^ flip), -1)
            lows[e] = op & 127

    def count(self, first_target, keys, lows, tally):
        plan = self.plan
        kind = BF16 if self.highs * plan.parents <= 256 else F32
        key_at = lax.broadcasted_iota(jnp.int32, (self.highs * plan.parents, 128), 0).astype(kind)
        low_at = lax.broadcasted_iota(jnp.int32, (128, 128), 0).astype(BF16)
        for i in range(self.group):
            key_hits, low_hits = [], []
            for e in range(plan.entry_tiles):
                key = keys[e, pl.ds(first_target + i, 1), :].astype(kind)
                low = lows[e, pl.ds(first_target + i, 1), :].astype(BF16)
                key_hits.append(jnp.where(key_at == key, jnp.ones((), kind), jnp.zeros((), kind)).astype(BF16))
                low_hits.append(jnp.where(low_at == low, jnp.ones((), BF16), jnp.zeros((), BF16)))
            count_of = lax.dot_general(
                jnp.concatenate(key_hits, 1), jnp.concatenate(low_hits, 1), NT, preferred_element_type=F32
            ).astype(BF16)
            rows = slice(i * plan.parents, (i + 1) * plan.parents)
            for h in range(self.highs):
                tally[rows, 128 * h : 128 * h + 128] = count_of[h * plan.parents : (h + 1) * plan.parents]

    def sum_operators(self, tally, table, a_real, a_imag):
        for a in range(0, self.rows, 512):
            z = min(a + 512, self.rows)
            a_real[a:z, :] = lax.dot_general(tally[a:z, :], table[0], NT, preferred_element_type=F32)
            a_imag[a:z, :] = lax.dot_general(tally[a:z, :], table[1], NT, preferred_element_type=F32)

    def fill(self, table_in, table):
        table[...] = jnp.zeros(table.shape, BF16)
        table[:, 0 : self.plan.dirs, 0 : self.plan.ops] = table_in[...].astype(BF16)

    def apply(self, blocks, first_block, a_real, a_imag, targets, k):
        plan = self.plan
        many = len(blocks) * plan.peers
        out = [[], []]
        for part in range(2):
            for p in range(plan.own):
                row, turn = plan.rest_at(p, part) if k >= plan.full else ((2 * p + part) * plan.full + k, 0)
                for block in blocks:
                    piece = block[pl.ds(row, plan.peers, stride=plan.rows), :]
                    out[part].append(pltpu.roll(piece, 128 - turn, 1) if turn else piece)
        out_real, out_imag = [jnp.concatenate(pieces, 0) for pieces in out]
        lanes = slice(128 * k, 128 * k + 128)
        results = []
        for i in targets:
            starts = [i * plan.parents + p * plan.devices + first_block * plan.peers for p in range(plan.own)]
            op_real = jnp.concatenate([a_real[a : a + many, lanes] for a in starts], 0)
            op_imag = jnp.concatenate([a_imag[a : a + many, lanes] for a in starts], 0)
            real = jnp.sum(op_real * out_real - op_imag * out_imag, 0, keepdims=True)
            imag = jnp.sum(op_real * out_imag + op_imag * out_real, 0, keepdims=True)
            results.append((i, real, imag))
        return results

    def kernel(self, table_in, received, a_real, a_imag, partial, table, tally, keys, lows):
        plan = self.plan
        self.read(received, keys, lows)
        self.count(0, keys, lows, tally)
        self.fill(table_in, table)
        self.sum_operators(tally, table, a_real, a_imag)
        for k in range(plan.tiles):
            for i, real, imag in self.apply([received], 0, a_real, a_imag, range(self.group), k):
                at = i * 2 * plan.tiles + k
                partial[at : at + 1, :] = real
                partial[at + plan.tiles : at + plan.tiles + 1, :] = imag


def translate_kernel(plan, tallies, ready):
    group = tallies.group

    def kernel(*refs):
        if ready:
            a_real, a_imag, partial, *refs = refs
            blocks = refs[: plan.cores]
            (out,) = refs[plan.cores :]
        else:
            table_in, *refs = refs
            blocks = refs[: plan.cores]
            out, a_real, a_imag, table, tally, keys, lows = refs[plan.cores :]
            tallies.read(blocks[0], keys, lows)
            tallies.fill(table_in, table)

        def do_group(first_target):
            if not ready:
                tallies.count(first_target, keys, lows, tally)
                tallies.sum_operators(tally, table, a_real, a_imag)
            for k in range(plan.tiles):
                start = 1 if ready else 0
                for i, real, imag in tallies.apply(blocks[start:], start, a_real, a_imag, range(group), k):
                    at = (first_target + i) * 2 * plan.tiles + k
                    if ready:
                        real = real + partial[at : at + 1, :]
                        imag = imag + partial[at + plan.tiles : at + plan.tiles + 1, :]
                    out[pl.ds(at, 1), :] = real
                    out[pl.ds(at + plan.tiles, 1), :] = imag

        if ready:
            do_group(0)
        else:
            pl.loop(0, tallies.targets // group)(lambda g: do_group(g * group))

    return kernel


def downward_kernel(plan):
    def kernel(arrived, angles, interp, rad, product, received, inner, twin):
        parent_dirs = angles.shape[1]
        leaf_dirs = rad.shape[0]
        parents_dev = product.shape[0] // 8
        boxes = product.shape[0]
        parts = 2 * parents_dev
        lane = lax.broadcasted_iota(jnp.int32, (parts, plan.width), 1)
        received[0 : arrived.shape[0], :] = arrived[...]
        inner[...] = jnp.zeros(inner.shape, F32)
        for i, w in enumerate(plan.order):
            base = plan.dirs * w // 128 * 128
            shift = plan.dirs * w % 128
            span = -(-(shift + plan.dirs) // 128) * 128
            tiles = [
                received[pl.ds(i * parts * plan.tiles + k, parts, stride=plan.tiles), :]
                for k in range(plan.tiles)
            ]
            value = tiles[0] if plan.tiles == 1 else jnp.concatenate(tiles, 1)
            value = jnp.where(lane < plan.dirs, value, 0.0)
            if span > plan.width:
                value = jnp.concatenate([value, jnp.zeros((parts, span - plan.width), F32)], 1)
            if shift:
                value = pltpu.roll(value, shift, 1)
            span = min(value.shape[1], inner.shape[1] - base)
            inner[:, base : base + span] += value[:, 0:span]
        sn, cs = sin_cos(angles[...])
        reals, imags = [], []
        for p in range(parents_dev):
            in_real = inner[2 * p : 2 * p + 1, 0:parent_dirs]
            in_imag = inner[2 * p + 1 : 2 * p + 2, 0:parent_dirs]
            reals.append(cs * in_real + sn * in_imag)
            imags.append(cs * in_imag - sn * in_real)
        blank = jnp.zeros((128 - 2 * boxes, parent_dirs), F32)
        down = jnp.concatenate(
            reals + imags + [blank] + imags + [-r for r in reals] + [blank], 0
        ).astype(BF16)
        down_t = jnp.transpose(down)
        quarter = -(-leaf_dirs // 64) * 16
        got = jnp.concatenate(
            [
                jnp.dot(interp[a : min(a + quarter, leaf_dirs), :], down_t, preferred_element_type=F32)
                for a in range(0, leaf_dirs, quarter)
            ],
            0,
        )
        twin[pl.ds(0, leaf_dirs, stride=2), :] = got[:, 0:128]
        twin[pl.ds(1, leaf_dirs, stride=2), :] = got[:, 128:256]
        flat = jnp.transpose(twin[0 : 2 * leaf_dirs, :])[0 : 2 * boxes].astype(BF16)
        matrix = rad[...].reshape(2 * leaf_dirs, rad.shape[2])
        result = jnp.dot(flat, matrix, preferred_element_type=F32)
        product[:, 0, :] = result[0:boxes]
        product[:, 1, :] = result[boxes : 2 * boxes]

    return kernel


def on_device(
    coefficients, radiation, interpolation, angles, translations, sources, operators, counts
):
    boxes = coefficients.shape[0]
    parents_dev = boxes // 8
    leaf_dirs, parent_dirs = interpolation.shape
    bases = coefficients.shape[2]
    n_wide = lax.axis_size("wide")
    n_narrow = lax.axis_size("narrow")
    dirs = translations.shape[2]
    n_ops = translations.shape[0]
    plan = Plan(parents_dev, n_wide, n_narrow, dirs, sources.shape[1], n_ops)
    rad = jnp.transpose(radiation, (2, 0, 1))
    table = jnp.transpose(translations, (1, 2, 0))
    room = -(-leaf_dirs // 16) * 16 + 16
    cuts = [0, 1280, 2432]
    cuts = [c for c in cuts if c < parent_dirs] + [parent_dirs]
    vmem = pl.BlockSpec(memory_space=pltpu.VMEM)
    anywhere = pl.BlockSpec(memory_space=pl.ANY)

    send = pl.pallas_call(
        upward_kernel(plan, cuts),
        out_shape=jax.ShapeDtypeStruct((plan.peers * plan.rows, 128), F32),
        in_specs=[anywhere] * 7,
        out_specs=vmem,
        scratch_shapes=[
            pltpu.VMEM((plan.peers * plan.rows + 64, 128), F32),
            pltpu.SMEM((parents_dev,), jnp.int32),
            pltpu.VMEM((boxes, 2, bases), BF16),
            pltpu.VMEM((room, 2, bases), BF16),
            pltpu.VMEM((leaf_dirs, parent_dirs), BF16),
            pltpu.VMEM(angles.shape, F32),
            pltpu.VMEM(sources.shape, jnp.int32),
            pltpu.VMEM(operators.shape, jnp.int32),
            pltpu.VMEM(angles.shape, F32),
            pltpu.VMEM(angles.shape, F32),
            pltpu.VMEM((2 * room, 128), F32),
            pltpu.VMEM((2 * room, 128), F32),
            pltpu.VMEM((parents_dev, 128 * plan.entry_tiles), jnp.int32),
            pltpu.VMEM((2 * parents_dev, parent_dirs), F32),
            pltpu.SemaphoreType.DMA((len(cuts) + 5,)),
        ],
        compiler_params=pltpu.CompilerParams(vmem_limit_bytes=56 * MIB),
        name="upward",
    )(counts, coefficients, rad, interpolation, angles, sources, operators)

    send = send.reshape(plan.peers, 1, plan.rows * 128)
    received = lax.all_to_all(
        send, ("wide", "narrow"), split_axis=0, concat_axis=0, tiled=True, axis_index_groups=plan.groups()
    ).reshape(-1, 128)
    blocks = [received]
    if plan.cores > 1:
        blocks.append(lax.ppermute(received, "narrow", [(i, i ^ 1) for i in range(n_narrow)]))

    tallies = Tally(plan)
    ready = tallies.targets == tallies.group and plan.cores > 1
    sums = jax.ShapeDtypeStruct((tallies.rows, plan.width), F32)
    scratch = [pltpu.VMEM((2, plan.width, tallies.shape[1]), BF16), pltpu.VMEM(tallies.shape, BF16)] + tallies.scratch
    if ready:
        operands = pl.pallas_call(
            tallies.kernel,
            out_shape=(sums, sums, jax.ShapeDtypeStruct((tallies.targets * 2 * plan.tiles, 128), F32)),
            in_specs=[vmem, vmem],
            out_specs=(vmem,) * 3,
            scratch_shapes=scratch,
            cost_estimate=pl.CostEstimate(flops=10**9, bytes_accessed=10**6, transcendentals=0),
            compiler_params=pltpu.CompilerParams(vmem_limit_bytes=16 * MIB),
            name="operators",
        )(table, received)
        scratch = []
    else:
        operands = [table]
        scratch = [pltpu.VMEM(sums.shape, F32), pltpu.VMEM(sums.shape, F32)] + scratch
    operands = [*operands, *blocks]
    incoming = pl.pallas_call(
        translate_kernel(plan, tallies, ready),
        out_shape=jax.ShapeDtypeStruct((n_wide * parents_dev * 2 * plan.tiles, 128), F32),
        in_specs=[vmem] * len(operands),
        out_specs=vmem,
        scratch_shapes=scratch,
        compiler_params=pltpu.CompilerParams(vmem_limit_bytes=24 * MIB),
        name="translate",
    )(*operands)

    incoming = incoming.reshape(n_wide, parents_dev * 2 * plan.tiles, 128)
    back = lax.all_to_all(
        incoming, ("wide", "narrow"), split_axis=0, concat_axis=0, tiled=True, axis_index_groups=plan.wide_groups()
    )
    back = back.reshape(-1, 128)

    return pl.pallas_call(
        downward_kernel(plan),
        out_shape=jax.ShapeDtypeStruct((boxes, 2, bases), F32),
        in_specs=[vmem] * 4,
        out_specs=vmem,
        scratch_shapes=[
            pltpu.VMEM((n_wide * parents_dev * 2 * plan.tiles + 64, 128), F32),
            pltpu.VMEM((2 * parents_dev, parent_dirs + 128), F32),
            pltpu.VMEM((2 * room, 128), F32),
        ],
        compiler_params=pltpu.CompilerParams(vmem_limit_bytes=32 * MIB),
        name="downward",
    )(back, angles, interpolation, rad)


def solution(mesh):
    in_specs = (
        P(("wide", "narrow"), None, None),
        P(),
        P(),
        P(),
        P(None, None, "wide"),
        P(("wide", "narrow"), None),
        P(("wide", "narrow"), None),
        P(("wide", "narrow")),
    )
    out_specs = P(("wide", "narrow"), None, None)
    return jax.shard_map(
        on_device, mesh=mesh, in_specs=in_specs, out_specs=out_specs, check_vma=False
    )
```

```python
import jax
import jax.numpy as jnp
from jax import lax
from jax.experimental import pallas as pl
from jax.experimental.pallas import tpu as pltpu
from jax.sharding import PartitionSpec as P

F32 = jnp.float32
BF16 = jnp.bfloat16
MIB = 2**20
NT = (((1,), (1,)), ((), ()))


class Plan:
    def __init__(self, own, n_wide, n_narrow, dirs, length, ops):
        self.own = own
        self.n_wide = n_wide
        self.n_narrow = n_narrow
        self.devices = n_wide * n_narrow
        self.parents = own * self.devices
        first = n_wide * 5 // 8
        self.order_back = list(range(first, -1, -1)) + list(range(first + 1, n_wide))
        self.order = [first, first - 1, *range(first + 1, n_wide), *range(first - 2, -1, -1)]
        self.cores = 2 if n_narrow % 2 == 0 else 1
        self.pairs = n_narrow // self.cores
        self.peers = n_wide * self.pairs
        self.dirs = dirs
        self.length = length
        self.ops = ops
        self.full = dirs // 128
        self.rest = dirs % 128
        self.tiles = -(-dirs // 128)
        self.width = 128 * self.tiles
        self.bits = ops.bit_length()
        entry_bits = self.bits + (self.parents - 1).bit_length()
        self.none = (1 << entry_bits) - 1
        self.rest_row = own * 2 * self.full
        self.shared = 2 * own * self.rest <= 128
        rest_rows = 0 if not self.rest else 1 if self.shared else 2 * own
        self.list_row = self.rest_row + rest_rows
        self.dense = entry_bits <= 15 and length <= 192
        self.entry_tiles = 2 if self.dense else -(-length // 128)
        self.list_rows = 1 if self.dense else self.entry_tiles
        self.rows = self.list_row + own * self.list_rows

    def rest_at(self, p, part):
        if self.shared:
            return self.rest_row, (2 * p + part) * self.rest
        return self.rest_row + 2 * p + part, 0

    def swap(self, w, pair):
        return w // (self.n_wide // 2) if self.cores > 1 else 0

    def device(self, w, pair, label):
        return w * self.n_narrow + pair * self.cores + (label ^ self.swap(w, pair))

    def groups(self):
        return [
            [self.device(w, pair, label) for w in self.order for pair in range(self.pairs)]
            for label in range(self.cores)
        ]

    def wide_groups(self):
        return [
            [self.device(w, pair, label) for w in self.order_back]
            for pair in range(self.pairs)
            for label in range(self.cores)
        ]

    def place(self, source):
        narrow_shift = self.own.bit_length() - 1
        device = source >> narrow_shift
        place = jnp.zeros(source.shape, jnp.int32)
        for i, w in enumerate(self.order):
            for pair in range(self.pairs):
                for label in range(self.cores):
                    block = label * self.peers + i * self.pairs + pair
                    place = jnp.where(device == self.device(w, pair, label), block, place)
        return (source & (self.own - 1)) * self.devices + place

    def encode(self, entries, lane):
        if not self.dense:
            return entries
        first, third = entries
        low = jnp.where(lane < 64, third & 255, pltpu.roll(third, 64, 1) >> 8)
        return [first * 256 + low]

    def decode(self, words, lane):
        if not self.dense:
            return words
        low = words[0] & 255
        third = low + (pltpu.roll(low, 64, 1) << 8)
        return [words[0] >> 8, jnp.where(lane < 64, third, self.none)]


def sin_cos(angle):
    turns = jnp.floor(angle * 0.6366197723675814 + 0.5)
    quarter = turns.astype(jnp.int32)
    rest = angle - turns * 1.5703125
    rest = rest - turns * 4.837512969970703e-4
    rest = rest - turns * 7.54978995489188e-8
    square = rest * rest
    sine = ((-1.9515295891e-4 * square + 8.3321608736e-3) * square - 1.6666654611e-1) * square * rest + rest
    cosine = ((2.443315711809948e-5 * square - 1.388731625493765e-3) * square + 4.166664568298827e-2) * (
        square * square
    ) - 0.5 * square + 1.0
    swap = (quarter & 1) == 1
    sin_value = jnp.where(swap, cosine, sine)
    cos_value = jnp.where(swap, sine, cosine)
    sin_value = jnp.where((quarter & 2) == 2, -sin_value, sin_value)
    cos_value = jnp.where(((quarter + 1) & 2) == 2, -cos_value, cos_value)
    return sin_value, cos_value


def arrange(boxes, swapped):
    row = lax.broadcasted_iota(jnp.int32, (128, 2 * boxes), 0)
    column = lax.broadcasted_iota(jnp.int32, (128, 2 * boxes), 1)
    real_at = 2 * row
    imag_at = 2 * (row - boxes) + 1
    if swapped:
        first = jnp.where((row < boxes) & (column == real_at + 1), -1.0, 0.0)
        second = jnp.where((row >= boxes) & (row < 2 * boxes) & (column == imag_at - 1), 1.0, 0.0)
    else:
        first = jnp.where((row < boxes) & (column == real_at), 1.0, 0.0)
        second = jnp.where((row >= boxes) & (row < 2 * boxes) & (column == imag_at), 1.0, 0.0)
    return (first + second).astype(BF16)


def upward_kernel(plan, cuts):
    def kernel(
        counts_hbm, coef_hbm, rad_hbm, interp_hbm, angles_hbm, sources_hbm, operators_hbm,
        send_out,
        send, counts, coef, rad, interp, angles, sources, operators, cos_out, sin_out,
        even, odd, codes, out_buf, sems,
    ):
        parent_dirs = angles.shape[1]
        leaf_dirs = rad_hbm.shape[0]
        boxes = coef.shape[0]
        parents_dev = boxes // 8
        n_chunks = len(cuts) - 1
        half = -(-leaf_dirs // 16) * 16
        first = []
        for source, target in (
            (angles_hbm, angles),
            (coef_hbm, coef),
            (rad_hbm, rad.at[pl.ds(0, leaf_dirs)]),
            (sources_hbm, sources),
            (operators_hbm, operators),
            (counts_hbm, counts),
        ):
            first.append(pltpu.make_async_copy(source, target, sems.at[n_chunks + len(first)]))
            first[-1].start()
        copies = []
        for c in range(n_chunks):
            cut = (slice(None), pl.ds(cuts[c], cuts[c + 1] - cuts[c]))
            copies.append(pltpu.make_async_copy(interp_hbm.at[cut], interp.at[cut], sems.at[c]))
            copies[-1].start()

        first[0].wait()
        sines, cosines = sin_cos(angles[...])
        sin_out[...] = sines
        cos_out[...] = cosines

        for copy in first[3:]:
            copy.wait()
        code = plan.place(sources[...]) * (1 << plan.bits) + operators[...]
        at = lax.broadcasted_iota(jnp.int32, code.shape, 1)
        parent = lax.broadcasted_iota(jnp.int32, code.shape, 0)
        limit = jnp.zeros(code.shape, jnp.int32)
        for p in range(parents_dev):
            limit = jnp.where(parent == p, counts[p], limit)
        codes[...] = jnp.full(codes.shape, plan.none, jnp.int32)
        codes[:, 0 : plan.length] = jnp.where(at < limit, code, plan.none)

        first[1].wait()
        rows = coef[...].reshape(2 * boxes, coef.shape[2])
        plain = jnp.dot(arrange(boxes, False), rows, preferred_element_type=F32).astype(BF16)
        turned = jnp.dot(arrange(boxes, True), rows, preferred_element_type=F32).astype(BF16)
        weights = jnp.concatenate([plain, turned], 0)

        first[2].wait()
        matrix = rad[0:leaf_dirs].reshape(2 * leaf_dirs, rad.shape[2])
        weights_t = jnp.transpose(weights)
        for a in range(0, 2 * leaf_dirs, half):
            z = min(a + half, 2 * leaf_dirs)
            both = jnp.dot(matrix[a:z], weights_t, preferred_element_type=F32)
            even[a:z, :] = both[:, 0:128]
            odd[a:z, :] = both[:, 128:256]
        leaf_t = even[pl.ds(0, leaf_dirs, stride=2), :] + odd[pl.ds(1, leaf_dirs, stride=2), :]
        leaf = jnp.transpose(leaf_t)[0 : 2 * boxes].astype(BF16)

        lane = lax.broadcasted_iota(jnp.int32, (parents_dev, 128), 1)
        words = plan.encode([codes[:, 128 * e : 128 * e + 128] for e in range(plan.entry_tiles)], lane)

        def put(w, row, stride, piece):
            for pair in range(plan.pairs):
                at_row = (plan.order.index(w) * plan.pairs + pair) * plan.rows + row
                send[pl.ds(at_row, piece.shape[0], stride=stride), :] = piece

        for w in range(plan.n_wide):
            for e, word in enumerate(words):
                put(w, plan.list_row + e, plan.list_rows, word.astype(F32))

        wide_lane = lax.broadcasted_iota(jnp.int32, (2 * parents_dev, 128), 1)

        def pack(w):
            base = plan.dirs * w // 128 * 128
            shift = plan.dirs * w % 128
            span = -(-(shift + plan.dirs) // 128) * 128
            span = min(max(span, plan.width), parent_dirs - base)
            value = out_buf[:, base : base + span]
            if shift:
                value = pltpu.roll(value, span - shift, 1)
            for k in range(plan.full):
                put(w, k, plan.full, value[:, 128 * k : 128 * k + 128])
            if plan.rest:
                piece = jnp.where(wide_lane < plan.rest, value[:, 128 * plan.full : plan.width], 0.0)
                if plan.shared:
                    piece = sum(
                        pltpu.roll(piece[r : r + 1], plan.rest * r, 1) if r else piece[0:1]
                        for r in range(2 * parents_dev)
                    )
                put(w, plan.rest_row, 1, piece)

        n_wide = plan.n_wide
        ups = []
        for c in range(n_chunks):
            copies[c].wait()
            ups.append(jnp.dot(leaf, interp[:, cuts[c] : cuts[c + 1]], preferred_element_type=F32))
        for c in range(n_chunks):
            cut = slice(cuts[c], cuts[c + 1])
            up = ups[c]
            cs = cos_out[:, cut]
            sn = sin_out[:, cut]
            for p in range(parents_dev):
                up_real = up[8 * p : 8 * p + 8]
                up_imag = up[boxes + 8 * p : boxes + 8 * p + 8]
                out_buf[2 * p : 2 * p + 1, cut] = jnp.sum(cs * up_real - sn * up_imag, 0, keepdims=True)
                out_buf[2 * p + 1 : 2 * p + 2, cut] = jnp.sum(cs * up_imag + sn * up_real, 0, keepdims=True)
        for w in range(n_wide):
            pack(w)
        send_out[...] = send[0 : send_out.shape[0], :]

    return kernel


class Tally:
    def __init__(self, plan):
        self.plan = plan
        self.targets = plan.n_wide * plan.own
        self.group = max(1, min(self.targets, 1024 // plan.parents))
        self.highs = -(-plan.ops // 128)
        self.rows = self.group * plan.parents
        self.shape = (self.rows, 128 * self.highs)
        lists = pltpu.VMEM((plan.entry_tiles, self.targets, 128), jnp.int32)
        self.scratch = [lists, lists]

    def read(self, received, keys, lows):
        plan = self.plan
        mine = lax.axis_index("narrow")
        own_block = lax.div(mine, plan.cores)
        label = lax.rem(mine, plan.cores) ^ plan.swap(lax.axis_index("wide"), own_block)
        flip = label * plan.peers
        lane = lax.broadcasted_iota(jnp.int32, (self.targets, 128), 1)
        words = []
        for e in range(plan.list_rows):
            rows = [
                received[
                    pl.ds((own_block + plan.order.index(w) * plan.pairs) * plan.rows + plan.list_row + p * plan.list_rows + e, 1), :
                ]
                for w in plan.order_back
                for p in range(plan.own)
            ]
            words.append(jnp.concatenate(rows, 0).astype(jnp.int32))
        for e, entry in enumerate(plan.decode(words, lane)):
            op = entry & ((1 << plan.bits) - 1)
            high = op >> 7
            keys[e] = jnp.where(high < self.highs, high * plan.parents + ((entry >> plan.bits) ^ flip), -1)
            lows[e] = op & 127

    def count(self, first_target, keys, lows, tally):
        plan = self.plan
        kind = BF16 if self.highs * plan.parents <= 256 else F32
        key_at = lax.broadcasted_iota(jnp.int32, (self.highs * plan.parents, 128), 0).astype(kind)
        low_at = lax.broadcasted_iota(jnp.int32, (128, 128), 0).astype(BF16)
        for i in range(self.group):
            key_hits, low_hits = [], []
            for e in range(plan.entry_tiles):
                key = keys[e, pl.ds(first_target + i, 1), :].astype(kind)
                low = lows[e, pl.ds(first_target + i, 1), :].astype(BF16)
                key_hits.append(jnp.where(key_at == key, jnp.ones((), kind), jnp.zeros((), kind)).astype(BF16))
                low_hits.append(jnp.where(low_at == low, jnp.ones((), BF16), jnp.zeros((), BF16)))
            count_of = lax.dot_general(
                jnp.concatenate(key_hits, 1), jnp.concatenate(low_hits, 1), NT, preferred_element_type=F32
            ).astype(BF16)
            rows = slice(i * plan.parents, (i + 1) * plan.parents)
            for h in range(self.highs):
                tally[rows, 128 * h : 128 * h + 128] = count_of[h * plan.parents : (h + 1) * plan.parents]

    def sum_operators(self, tally, table, a_real, a_imag):
        for a in range(0, self.rows, 512):
            z = min(a + 512, self.rows)
            a_real[a:z, :] = lax.dot_general(tally[a:z, :], table[0], NT, preferred_element_type=F32)
            a_imag[a:z, :] = lax.dot_general(tally[a:z, :], table[1], NT, preferred_element_type=F32)

    def fill(self, table_in, table):
        table[...] = jnp.zeros(table.shape, BF16)
        table[:, 0 : self.plan.dirs, 0 : self.plan.ops] = table_in[...].astype(BF16)

    def apply(self, blocks, first_block, a_real, a_imag, targets, k):
        plan = self.plan
        many = len(blocks) * plan.peers
        out = [[], []]
        for part in range(2):
            for p in range(plan.own):
                row, turn = plan.rest_at(p, part) if k >= plan.full else ((2 * p + part) * plan.full + k, 0)
                for block in blocks:
                    piece = block[pl.ds(row, plan.peers, stride=plan.rows), :]
                    out[part].append(pltpu.roll(piece, 128 - turn, 1) if turn else piece)
        out_real, out_imag = [jnp.concatenate(pieces, 0) for pieces in out]
        lanes = slice(128 * k, 128 * k + 128)
        results = []
        for i in targets:
            starts = [i * plan.parents + p * plan.devices + first_block * plan.peers for p in range(plan.own)]
            op_real = jnp.concatenate([a_real[a : a + many, lanes] for a in starts], 0)
            op_imag = jnp.concatenate([a_imag[a : a + many, lanes] for a in starts], 0)
            real = jnp.sum(op_real * out_real - op_imag * out_imag, 0, keepdims=True)
            imag = jnp.sum(op_real * out_imag + op_imag * out_real, 0, keepdims=True)
            results.append((i, real, imag))
        return results

    def kernel(self, table_in, received, a_real, a_imag, partial, table, tally, keys, lows):
        plan = self.plan
        self.read(received, keys, lows)
        self.count(0, keys, lows, tally)
        self.fill(table_in, table)
        self.sum_operators(tally, table, a_real, a_imag)
        for k in range(plan.tiles):
            for i, real, imag in self.apply([received], 0, a_real, a_imag, range(self.group), k):
                at = i * 2 * plan.tiles + k
                partial[at : at + 1, :] = real
                partial[at + plan.tiles : at + plan.tiles + 1, :] = imag


def translate_kernel(plan, tallies, ready):
    group = tallies.group

    def kernel(*refs):
        if ready:
            a_real, a_imag, partial, *refs = refs
            blocks = refs[: plan.cores]
            (out,) = refs[plan.cores :]
        else:
            table_in, *refs = refs
            blocks = refs[: plan.cores]
            out, a_real, a_imag, table, tally, keys, lows = refs[plan.cores :]
            tallies.read(blocks[0], keys, lows)
            tallies.fill(table_in, table)

        def do_group(first_target):
            if not ready:
                tallies.count(first_target, keys, lows, tally)
                tallies.sum_operators(tally, table, a_real, a_imag)
            for k in range(plan.tiles):
                start = 1 if ready else 0
                for i, real, imag in tallies.apply(blocks[start:], start, a_real, a_imag, range(group), k):
                    at = (first_target + i) * 2 * plan.tiles + k
                    if ready:
                        real = real + partial[at : at + 1, :]
                        imag = imag + partial[at + plan.tiles : at + plan.tiles + 1, :]
                    out[pl.ds(at, 1), :] = real
                    out[pl.ds(at + plan.tiles, 1), :] = imag

        if ready:
            do_group(0)
        else:
            pl.loop(0, tallies.targets // group)(lambda g: do_group(g * group))

    return kernel


def downward_kernel(plan):
    def kernel(arrived, angles, interp, rad, product, received, inner, twin):
        parent_dirs = angles.shape[1]
        leaf_dirs = rad.shape[0]
        parents_dev = product.shape[0] // 8
        boxes = product.shape[0]
        parts = 2 * parents_dev
        lane = lax.broadcasted_iota(jnp.int32, (parts, plan.width), 1)
        received[0 : arrived.shape[0], :] = arrived[...]
        inner[...] = jnp.zeros(inner.shape, F32)
        for i, w in enumerate(plan.order_back):
            base = plan.dirs * w // 128 * 128
            shift = plan.dirs * w % 128
            span = -(-(shift + plan.dirs) // 128) * 128
            tiles = [
                received[pl.ds(i * parts * plan.tiles + k, parts, stride=plan.tiles), :]
                for k in range(plan.tiles)
            ]
            value = tiles[0] if plan.tiles == 1 else jnp.concatenate(tiles, 1)
            value = jnp.where(lane < plan.dirs, value, 0.0)
            if span > plan.width:
                value = jnp.concatenate([value, jnp.zeros((parts, span - plan.width), F32)], 1)
            if shift:
                value = pltpu.roll(value, shift, 1)
            span = min(value.shape[1], inner.shape[1] - base)
            inner[:, base : base + span] += value[:, 0:span]
        sn, cs = sin_cos(angles[...])
        reals, imags = [], []
        for p in range(parents_dev):
            in_real = inner[2 * p : 2 * p + 1, 0:parent_dirs]
            in_imag = inner[2 * p + 1 : 2 * p + 2, 0:parent_dirs]
            reals.append(cs * in_real + sn * in_imag)
            imags.append(cs * in_imag - sn * in_real)
        blank = jnp.zeros((128 - 2 * boxes, parent_dirs), F32)
        down = jnp.concatenate(
            reals + imags + [blank] + imags + [-r for r in reals] + [blank], 0
        ).astype(BF16)
        down_t = jnp.transpose(down)
        quarter = -(-leaf_dirs // 64) * 16
        got = jnp.concatenate(
            [
                jnp.dot(interp[a : min(a + quarter, leaf_dirs), :], down_t, preferred_element_type=F32)
                for a in range(0, leaf_dirs, quarter)
            ],
            0,
        )
        twin[pl.ds(0, leaf_dirs, stride=2), :] = got[:, 0:128]
        twin[pl.ds(1, leaf_dirs, stride=2), :] = got[:, 128:256]
        flat = jnp.transpose(twin[0 : 2 * leaf_dirs, :])[0 : 2 * boxes].astype(BF16)
        matrix = rad[...].reshape(2 * leaf_dirs, rad.shape[2])
        result = jnp.dot(flat, matrix, preferred_element_type=F32)
        product[:, 0, :] = result[0:boxes]
        product[:, 1, :] = result[boxes : 2 * boxes]

    return kernel


def on_device(
    coefficients, radiation, interpolation, angles, translations, sources, operators, counts
):
    boxes = coefficients.shape[0]
    parents_dev = boxes // 8
    leaf_dirs, parent_dirs = interpolation.shape
    bases = coefficients.shape[2]
    n_wide = lax.axis_size("wide")
    n_narrow = lax.axis_size("narrow")
    dirs = translations.shape[2]
    n_ops = translations.shape[0]
    plan = Plan(parents_dev, n_wide, n_narrow, dirs, sources.shape[1], n_ops)
    rad = jnp.transpose(radiation, (2, 0, 1))
    table = jnp.transpose(translations, (1, 2, 0))
    room = -(-leaf_dirs // 16) * 16 + 16
    cuts = [0, 1280, 2432]
    cuts = [c for c in cuts if c < parent_dirs] + [parent_dirs]
    vmem = pl.BlockSpec(memory_space=pltpu.VMEM)
    anywhere = pl.BlockSpec(memory_space=pl.ANY)

    send = pl.pallas_call(
        upward_kernel(plan, cuts),
        out_shape=jax.ShapeDtypeStruct((plan.peers * plan.rows, 128), F32),
        in_specs=[anywhere] * 7,
        out_specs=vmem,
        scratch_shapes=[
            pltpu.VMEM((plan.peers * plan.rows + 64, 128), F32),
            pltpu.SMEM((parents_dev,), jnp.int32),
            pltpu.VMEM((boxes, 2, bases), BF16),
            pltpu.VMEM((room, 2, bases), BF16),
            pltpu.VMEM((leaf_dirs, parent_dirs), BF16),
            pltpu.VMEM(angles.shape, F32),
            pltpu.VMEM(sources.shape, jnp.int32),
            pltpu.VMEM(operators.shape, jnp.int32),
            pltpu.VMEM(angles.shape, F32),
            pltpu.VMEM(angles.shape, F32),
            pltpu.VMEM((2 * room, 128), F32),
            pltpu.VMEM((2 * room, 128), F32),
            pltpu.VMEM((parents_dev, 128 * plan.entry_tiles), jnp.int32),
            pltpu.VMEM((2 * parents_dev, parent_dirs), F32),
            pltpu.SemaphoreType.DMA((len(cuts) + 5,)),
        ],
        compiler_params=pltpu.CompilerParams(vmem_limit_bytes=56 * MIB),
        name="upward",
    )(counts, coefficients, rad, interpolation, angles, sources, operators)

    send = send.reshape(plan.peers, 1, plan.rows * 128)
    received = lax.all_to_all(
        send, ("wide", "narrow"), split_axis=0, concat_axis=0, tiled=True, axis_index_groups=plan.groups()
    ).reshape(-1, 128)
    blocks = [received]
    if plan.cores > 1:
        blocks.append(lax.ppermute(received, "narrow", [(i, i ^ 1) for i in range(n_narrow)]))

    tallies = Tally(plan)
    ready = tallies.targets == tallies.group and plan.cores > 1
    sums = jax.ShapeDtypeStruct((tallies.rows, plan.width), F32)
    scratch = [pltpu.VMEM((2, plan.width, tallies.shape[1]), BF16), pltpu.VMEM(tallies.shape, BF16)] + tallies.scratch
    if ready:
        operands = pl.pallas_call(
            tallies.kernel,
            out_shape=(sums, sums, jax.ShapeDtypeStruct((tallies.targets * 2 * plan.tiles, 128), F32)),
            in_specs=[vmem, vmem],
            out_specs=(vmem,) * 3,
            scratch_shapes=scratch,
            cost_estimate=pl.CostEstimate(flops=10**9, bytes_accessed=10**6, transcendentals=0),
            compiler_params=pltpu.CompilerParams(vmem_limit_bytes=16 * MIB),
            name="operators",
        )(table, received)
        scratch = []
    else:
        operands = [table]
        scratch = [pltpu.VMEM(sums.shape, F32), pltpu.VMEM(sums.shape, F32)] + scratch
    operands = [*operands, *blocks]
    incoming = pl.pallas_call(
        translate_kernel(plan, tallies, ready),
        out_shape=jax.ShapeDtypeStruct((n_wide * parents_dev * 2 * plan.tiles, 128), F32),
        in_specs=[vmem] * len(operands),
        out_specs=vmem,
        scratch_shapes=scratch,
        compiler_params=pltpu.CompilerParams(vmem_limit_bytes=24 * MIB),
        name="translate",
    )(*operands)

    incoming = incoming.reshape(n_wide, parents_dev * 2 * plan.tiles, 128)
    back = lax.all_to_all(
        incoming, ("wide", "narrow"), split_axis=0, concat_axis=0, tiled=True, axis_index_groups=plan.wide_groups()
    )
    back = back.reshape(-1, 128)

    return pl.pallas_call(
        downward_kernel(plan),
        out_shape=jax.ShapeDtypeStruct((boxes, 2, bases), F32),
        in_specs=[vmem] * 4,
        out_specs=vmem,
        scratch_shapes=[
            pltpu.VMEM((n_wide * parents_dev * 2 * plan.tiles + 64, 128), F32),
            pltpu.VMEM((2 * parents_dev, parent_dirs + 128), F32),
            pltpu.VMEM((2 * room, 128), F32),
        ],
        compiler_params=pltpu.CompilerParams(vmem_limit_bytes=32 * MIB),
        name="downward",
    )(back, angles, interpolation, rad)


def solution(mesh):
    in_specs = (
        P(("wide", "narrow"), None, None),
        P(),
        P(),
        P(),
        P(None, None, "wide"),
        P(("wide", "narrow"), None),
        P(("wide", "narrow"), None),
        P(("wide", "narrow")),
    )
    out_specs = P(("wide", "narrow"), None, None)
    return jax.shard_map(
        on_device, mesh=mesh, in_specs=in_specs, out_specs=out_specs, check_vma=False
    )
```
